32 devices in a mesh: dp: 8 (over z, y), tensor: 4 (over x, core).
Axes of the slice: x: 2, y: 2, z: 4, core: 2. Of those that a mesh axis runs over, the one named last changes fastest.
Arguments:
- tokens: bfloat16 [8192, 1536], P(('dp', 'tensor')), may hold values from -6 to 6
- cotangent: bfloat16 [8192, 1536], P(('dp', 'tensor')), may hold values from -20 to 20
- lengths: int32 [8], replicated, may hold values from 1 to 1024, 6144 in all
- order: int32 [8], replicated, may hold values from 0 to 7, as said below
- in_weight: float32 [1536, 6448], P('dp', 'tensor'), may hold values from -0.15625 to 0.15625
- in_first: float32 [1536, 6448], P('dp', 'tensor'), may hold values from -0.00390625 to 0.00390625
- in_second: float32 [1536, 6448], P('dp', 'tensor'), may hold values from 3.4143415e-08 to 5.4629464e-07
- out_weight: float32 [3072, 1536], P('tensor', 'dp'), may hold values from -0.109375 to 0.109375
- out_first: float32 [3072, 1536], P('tensor', 'dp'), may hold values from -0.00390625 to 0.00390625
- out_second: float32 [3072, 1536], P('tensor', 'dp'), may hold values from 3.4143415e-08 to 5.4629464e-07
- conv_weight: float32 [3328, 5], P('tensor'), may hold values from -3 to 3
- conv_first: float32 [3328, 5], P('tensor'), may hold values from -0.00390625 to 0.00390625
- conv_second: float32 [3328, 5], P('tensor'), may hold values from 3.4143415e-08 to 5.4629464e-07
- gain_vector: float32 [4608], replicated, may hold values from 0.8 to 6.25
- gain_first: float32 [4608], replicated, may hold values from -0.00390625 to 0.00390625
- gain_second: float32 [4608], replicated, may hold values from 3.4143415e-08 to 5.4629464e-07
- head_params: float32 [48, 3], P('tensor'), may hold values from -7 to 3
- head_first: float32 [48, 3], P('tensor'), may hold values from -0.00390625 to 0.00390625
- head_second: float32 [48, 3], P('tensor'), may hold values from 3.4143415e-08 to 5.4629464e-07
Outputs:
- layer_output: bfloat16 [8192, 1536], P(('dp', 'tensor'))
- input_grad: bfloat16 [8192, 1536], P(('dp', 'tensor'))
- grad_norm: float32 [], replicated
- new_in_weight: float32 [1536, 6448], P('dp', 'tensor')
- new_in_first: float32 [1536, 6448], P('dp', 'tensor')
- new_in_second: float32 [1536, 6448], P('dp', 'tensor')
- new_out_weight: float32 [3072, 1536], P('tensor', 'dp')
- new_out_first: float32 [3072, 1536], P('tensor', 'dp')
- new_out_second: float32 [3072, 1536], P('tensor', 'dp')
- new_conv_weight: float32 [3328, 5], P('tensor')
- new_conv_first: float32 [3328, 5], P('tensor')
- new_conv_second: float32 [3328, 5], P('tensor')
- new_gain_vector: float32 [4608], replicated
- new_gain_first: float32 [4608], replicated
- new_gain_second: float32 [4608], replicated
- new_head_params: float32 [48, 3], P('tensor')
- new_head_first: float32 [48, 3], P('tensor')
- new_head_second: float32 [48, 3], P('tensor')
- in_copy: bfloat16 [1536, 6448], P('dp', 'tensor')
- out_copy: bfloat16 [3072, 1536], P('tensor', 'dp')
The draws below stay inside these ranges and needn't reach their ends.
Inputs may be any that keep to these rules, and one draw needn't show every extreme that they name: `lengths`: each sequence has at least one valid position; the longest has exactly 1024. A permutation of the sequences in which order[j] % 1 equals j % 1 (1 sequences per index of dp: 1 here, 2 on the larger slice).
All inputs are finite; a program needn't handle non-finite values.
Results may differ from the reference program's by a relative error of at most 0.019.
Values may be sent and summed in bfloat16 or wider, within the bound.
No kernel may reach another device: no remote copies, remote signals or barrier semaphores. Data moves between devices by JAX's collectives and lax.ppermute only.
A program may use at most 192 MiB of HBM per device.

```python
import math
import jax
import jax.numpy as jnp
import numpy as np
from jax import lax

D = 1536
HEADS = 48
STATE = 128
KW = 4
SPAN = 256
LEN = 1024
SEQ_DEV = 1
STEP = 5
DI = 3072
IN_COLS = 6448
CONV_CH = 3328
SEQS = 8
TOKENS = 8192
INNER_DEV = 768
BC_DEV = 64
IN_DEV = 1612
CONV_DEV = 832
NPARAMS = 14644112
N_TENSOR = 4


def draw_cotangent(key, part):
    key = jax.random.fold_in(key, 11)
    columns = jnp.arange(D).astype(jnp.float32) / (D - 1)
    base = jnp.clip(jax.random.normal(key, (TOKENS, D), jnp.float32), -4.0, 4.0)
    rising = 1.0 + 2.0 * columns
    return (base * rising[None, :]).astype(jnp.bfloat16)


def draw_gain_vector(key, part):
    key = jax.random.fold_in(key, 12)
    index = jnp.arange(D + DI)
    norm_place = index.astype(jnp.float32) / (D - 1)
    gate_place = (index - D).astype(jnp.float32) / (DI - 1)
    place = jnp.where(index < D, norm_place, gate_place)
    spread = 2.0
    factor = jax.random.uniform(key, (D + DI,), jnp.float32, 0.8, 1.25)
    return (1.0 + spread * place) * factor


def draw_head_params(key, part):
    key = jax.random.fold_in(key, 13)
    key_list = jax.random.split(key, 3)
    step_bias = jax.random.uniform(key_list[0], (HEADS,), jnp.float32, -6.0, -2.0)
    decay_log = jax.random.uniform(key_list[1], (HEADS,), jnp.float32, 0.0, 2.77)
    skip_gain = jax.random.uniform(key_list[2], (HEADS,), jnp.float32, 0.5, 1.5)
    return jnp.stack([step_bias, decay_log, skip_gain], axis=1)


def draw_order(key, part):
    key = jax.random.fold_in(key, 14)
    groups = SEQS // SEQ_DEV
    key_list = jax.random.split(key, SEQ_DEV)
    perms = jnp.stack([jax.random.permutation(key_list[residue], groups) for residue in range(SEQ_DEV)])
    order = perms.T.astype(jnp.int32) * SEQ_DEV + jnp.arange(SEQ_DEV).astype(jnp.int32)[None, :]
    return order.reshape(SEQS).astype(jnp.int32)


def shard_levels(key, extent, shards, least, largest):
    def one(position, parts):
        draws = jax.random.uniform(jax.random.fold_in(jax.random.fold_in(key, 6), position), (parts,), jnp.float32, least / len(shards), largest / len(shards))
        return jnp.repeat(jnp.exp(draws), extent[position] // parts).reshape((-1,) + (1,) * (len(extent) - position - 1))

    loudness = one(*shards[0])
    for cut in shards[1:]:
        loudness = loudness * one(*cut)
    return loudness


def profile(amount, total, most, lean):
    portions = [(1 << 20) // math.isqrt(rank ** lean) + 1 for rank in range(2, amount + 1)]
    surplus, holding = total - most - (amount - 1), [1] * (amount - 1)
    while surplus > 0:
        movable = [i for i in range(amount - 1) if holding[i] < most]
        whole, left = sum([portions[i] for i in movable]), surplus
        for i in movable:
            addition = min(most - holding[i], max(1, left * portions[i] // whole), surplus)
            holding[i] = holding[i] + addition
            surplus = surplus - addition
    return np.array([most] + holding)


def uneven_parts(rng, amount, total, bound, slope):
    if amount == 2:
        one = jax.random.randint(rng, (), max(1, total - bound), min(bound, total - 1) + 1)
        return jnp.stack([one, total - one])
    tallies = jnp.asarray(profile(amount, total, bound, slope), jnp.int32)
    twos = (amount - 1) // 2
    giver, taker = tallies[1:1 + 2 * twos:2], tallies[2:2 + 2 * twos:2]
    room = jnp.minimum(giver - 1, bound - taker)
    moved = jax.random.randint(jax.random.fold_in(rng, 1), (twos,), 0, 1 << 20) % (room + 1)
    tallies = tallies.at[1:1 + 2 * twos:2].set(giver - moved).at[2:2 + 2 * twos:2].set(taker + moved)
    return tallies[jax.random.permutation(jax.random.fold_in(rng, 2), amount)]


def scatter_about(stream_key, extent, scale, limit, cuts=(), dtype=jnp.bfloat16):
    entries = jax.random.normal(stream_key, extent, jnp.float32) * scale
    if len(cuts) > 0:
        entries = shard_levels(stream_key, extent, cuts, -0.22, 0.18) * entries
    return jnp.clip(entries, min=-limit, max=limit).astype(dtype)


def setup_inputs(seed: int = 0) -> dict:
    keys = jax.random.split(jax.random.key(seed), 20)
    tokens = scatter_about(keys[0], (TOKENS, D), 1.0, 6.0, ((0, 32),))
    cotangent = draw_cotangent(jax.random.fold_in(keys[19], 71), 0)
    lengths = uneven_parts(keys[2], SEQS, SEQS * LEN * 3 // 4, LEN, 1).astype(jnp.int32)
    order = draw_order(jax.random.fold_in(keys[19], 71), 0)
    in_weight = scatter_about(keys[4], (D, IN_COLS), D ** -0.5, 0.15625, ((0, 8), (1, 4)), jnp.float32)
    in_first = scatter_about(keys[5], (D, IN_COLS), (NPARAMS ** -0.5), 0.00390625, ((0, 8), (1, 4)), jnp.float32)
    in_second = jnp.clip(jnp.exp(math.log(5.462946432999161e-07) - 2.7725887 * jax.random.uniform(keys[6], (D, IN_COLS), jnp.float32) ** shard_levels(keys[6], (D, IN_COLS), ((0, 8), (1, 4)), -0.2, 0.2)), 3.4143415206244754e-08, 5.462946432999161e-07)
    out_weight = scatter_about(keys[7], (DI, D), DI ** -0.5, 0.109375, ((0, 4), (1, 8)), jnp.float32)
    out_first = scatter_about(keys[8], (DI, D), (NPARAMS ** -0.5), 0.00390625, ((0, 4), (1, 8)), jnp.float32)
    out_second = jnp.clip(jnp.exp(math.log(5.462946432999161e-07) - 2.7725887 * jax.random.uniform(keys[9], (DI, D), jnp.float32) ** shard_levels(keys[9], (DI, D), ((0, 4), (1, 8)), -0.2, 0.2)), 3.4143415206244754e-08, 5.462946432999161e-07)
    conv_weight = scatter_about(keys[10], (CONV_CH, KW + 1), 0.5, 3.0, ((0, 4),), jnp.float32)
    conv_first = scatter_about(keys[11], (CONV_CH, KW + 1), (NPARAMS ** -0.5), 0.00390625, ((0, 4),), jnp.float32)
    conv_second = jnp.clip(jnp.exp(math.log(5.462946432999161e-07) - 2.7725887 * jax.random.uniform(keys[12], (CONV_CH, KW + 1), jnp.float32) ** shard_levels(keys[12], (CONV_CH, KW + 1), ((0, 4),), -0.2, 0.2)), 3.4143415206244754e-08, 5.462946432999161e-07)
    gain_vector = draw_gain_vector(jax.random.fold_in(keys[19], 71), 0)
    gain_first = scatter_about(keys[14], (D + DI,), (NPARAMS ** -0.5), 0.00390625, (), jnp.float32)
    gain_second = jnp.clip(jnp.exp(jax.random.uniform(keys[15], (D + DI,), jnp.float32, math.log(3.4143415206244754e-08), math.log(5.462946432999161e-07))), 3.4143415206244754e-08, 5.462946432999161e-07)
    head_params = draw_head_params(jax.random.fold_in(keys[19], 71), 0)
    head_first = scatter_about(keys[17], (HEADS, 3), (NPARAMS ** -0.5), 0.00390625, ((0, 4),), jnp.float32)
    head_second = jnp.clip(jnp.exp(math.log(5.462946432999161e-07) - 2.7725887 * jax.random.uniform(keys[18], (HEADS, 3), jnp.float32) ** shard_levels(keys[18], (HEADS, 3), ((0, 4),), -0.2, 0.2)), 3.4143415206244754e-08, 5.462946432999161e-07)
    return {"tokens": tokens, "cotangent": cotangent, "lengths": lengths, "order": order, "in_weight": in_weight, "in_first": in_first, "in_second": in_second, "out_weight": out_weight, "out_first": out_first, "out_second": out_second, "conv_weight": conv_weight, "conv_first": conv_first, "conv_second": conv_second, "gain_vector": gain_vector, "gain_first": gain_first, "gain_second": gain_second, "head_params": head_params, "head_first": head_first, "head_second": head_second}


EPS_NORM = 1e-05
BETA_ONE = 0.5
BETA_TWO = 0.5
ADAM_EPS = 1e-08
DECAY = 0.1
RATE_MATRIX = 0.02
RATE_VECTOR = 0.8
CLIP_NORM = 1.0
HIGHEST_PRECISION = lax.Precision.HIGHEST

@jax.custom_vjp
def low(v):
    return lax.optimization_barrier(v.astype(jnp.bfloat16)).astype(jnp.float32)

@jax.custom_vjp
def low_back(v):
    return v

def low_keep(v):
    return (low(v), None)

def low_pass(kept, grad):
    return (grad,)

def back_keep(v):
    return (v, None)

def back_low(kept, grad):
    return (low(grad),)
low.defvjp(low_keep, low_pass)
low_back.defvjp(back_keep, back_low)

def product(left, right):
    return jnp.dot(left, right, preferred_element_type=jnp.float32, precision=HIGHEST_PRECISION)

def causal_conv(values, taps):
    width = taps.shape[1] - 1
    length = values.shape[1]
    padded = jnp.pad(values, ((0, 0), (width - 1, 0), (0, 0)))
    result = jnp.zeros_like(values) + taps[:, width]
    for offset in range(width):
        result = result + taps[:, offset] * padded[:, offset:offset + length, :]
    return result

def state_scan(values, step, rate, state_in, state_out, span):
    seq_count, length, head_count, width = values.shape
    state_size = state_in.shape[-1]
    blocks = length // span
    value_blocks = values.reshape(seq_count, blocks, span, head_count, width)
    step_blocks = step.reshape(seq_count, blocks, span, head_count)
    in_blocks = state_in.reshape(seq_count, blocks, span, state_size)
    out_blocks = state_out.reshape(seq_count, blocks, span, state_size)
    logs = jnp.cumsum(step_blocks * rate, axis=2)
    weighted = step_blocks[..., None] * value_blocks
    lower = (jnp.arange(span)[:, None] >= jnp.arange(span)[None, :])[None, None, :, :, None]
    differ = logs[:, :, :, None, :] - logs[:, :, None, :, :]
    within = jnp.where(lower, jnp.exp(jnp.where(lower, differ, 0.0)), 0.0)
    scores = jnp.einsum('skin,skjn->skij', out_blocks, in_blocks, precision=HIGHEST_PRECISION)
    inner = jnp.einsum('skijh,skjhp->skihp', within * scores[..., None], weighted, precision=HIGHEST_PRECISION)
    to_end = jnp.exp(logs[:, :, -1:, :] - logs)
    block_states = jnp.einsum('skjn,skjhp->skhnp', in_blocks, to_end[..., None] * weighted, precision=HIGHEST_PRECISION)
    carry_decay = jnp.exp(logs[:, :, -1, :])

    def advance(carried, element):
        decay_now, fresh = element
        return (carried * decay_now[..., None, None] + fresh, carried)
    start = jnp.zeros((seq_count, head_count, state_size, width), jnp.float32)
    _, entering = lax.scan(advance, start, (jnp.moveaxis(carry_decay, 1, 0), jnp.moveaxis(block_states, 1, 0)))
    entering = jnp.moveaxis(entering, 0, 1)
    outer = jnp.einsum('skin,skhnp->skihp', out_blocks, entering, precision=HIGHEST_PRECISION) * jnp.exp(logs)[..., None]
    return (inner + outer).reshape(seq_count, length, head_count, width)

def mixing(gate_pre, inner_pre, step_pre, state_in, state_out, taps, head_side):
    seq_count, length, channels = inner_pre.shape
    head_count = head_side.shape[0]
    inner = jax.nn.silu(causal_conv(inner_pre, taps))
    step = jax.nn.softplus(step_pre + head_side[:, 0])
    rate = -jnp.exp(head_side[:, 1])
    values = inner.reshape(seq_count, length, head_count, channels // head_count)
    mixed = state_scan(values, step, rate, state_in, state_out, SPAN)
    mixed = mixed + head_side[:, 2][:, None] * values
    return mixed.reshape(seq_count, length, channels) * jax.nn.silu(gate_pre)

def adam_step(weight, first, second, grad, rate, decay):
    first = BETA_ONE * first + (1.0 - BETA_ONE) * grad
    second = BETA_TWO * second + (1.0 - BETA_TWO) * grad * grad
    update = first / (1.0 - BETA_ONE ** STEP) / (jnp.sqrt(second / (1.0 - BETA_TWO ** STEP)) + ADAM_EPS)
    return (weight - rate * (update + decay * weight), first, second)

def layer_forward(rows, in_weight, out_weight, conv_weight, gain_vector, head_params, live):
    blocks = low(in_weight).reshape(D, N_TENSOR, IN_DEV)
    w_gate = blocks[:, :, :INNER_DEV].reshape(D, DI)
    w_inner = blocks[:, :, INNER_DEV:2 * INNER_DEV].reshape(D, DI)
    w_state = blocks[:, :, 2 * INNER_DEV:2 * INNER_DEV + BC_DEV].reshape(D, 2 * STATE)
    w_step = blocks[:, :, 2 * INNER_DEV + BC_DEV:].reshape(D, HEADS)
    tap_blocks = conv_weight.reshape(N_TENSOR, CONV_DEV, KW + 1)
    taps_inner = tap_blocks[:, :INNER_DEV].reshape(DI, KW + 1)
    taps_state = tap_blocks[:, INNER_DEV:].reshape(2 * STATE, KW + 1)
    norm_gain = gain_vector[:D]
    gate_gain = gain_vector[D:]
    out_low = low(out_weight)

    def per_sequence(paired):
        values, valid_rows = paired
        inv_rms = lax.rsqrt(lax.optimization_barrier(jnp.mean(values * values, axis=-1, keepdims=True)) + EPS_NORM)
        normed = low(values * inv_rms * norm_gain)
        gate_pre = low_back(product(normed, w_gate))
        inner_pre = low_back(product(normed, w_inner))
        state_pre = low_back(product(normed, w_state))
        step_pre = low_back(product(normed, w_step))
        states = low(jax.nn.silu(causal_conv(state_pre[None], taps_state)))
        mixed = mixing(gate_pre[None], inner_pre[None], step_pre[None], states[:, :, :STATE], states[:, :, STATE:], taps_inner, head_params)[0]
        gate_inv = lax.rsqrt(lax.optimization_barrier(jnp.mean(mixed * mixed, axis=-1, keepdims=True)) + EPS_NORM)
        normed_out = low(mixed * gate_inv * gate_gain)
        branch = product(normed_out, out_low)
        return valid_rows[:, None] * (values + branch)
    return lax.map(jax.checkpoint(per_sequence), (rows, live))

def reference(tokens, cotangent, lengths, order, in_weight, in_first, in_second, out_weight, out_first, out_second, conv_weight, conv_first, conv_second, gain_vector, gain_first, gain_second, head_params, head_first, head_second):
    rows = tokens.astype(jnp.float32).reshape(SEQS, LEN, D)
    order = order.astype(jnp.int32)
    inverse = jnp.zeros((SEQS,), jnp.int32).at[order].set(jnp.arange(SEQS).astype(jnp.int32))
    live = (jnp.arange(LEN)[None, :] < lengths[order][:, None]).astype(jnp.float32)

    def forward(values, weight_in, weight_out, weight_conv, gain_values, head_values):
        return layer_forward(values[order], weight_in, weight_out, weight_conv, gain_values, head_values, live)
    result, pullback = jax.vjp(forward, rows, in_weight, out_weight, conv_weight, gain_vector, head_params)
    gradients = pullback(cotangent.astype(jnp.float32).reshape(SEQS, LEN, D))
    squares = sum((jnp.sum(part_grad * part_grad) for part_grad in gradients[1:]))
    grad_norm = jnp.sqrt(squares)
    factor = CLIP_NORM / jnp.maximum(grad_norm, CLIP_NORM)
    new_in = adam_step(in_weight, in_first, in_second, factor * gradients[1], RATE_MATRIX, DECAY)
    new_out = adam_step(out_weight, out_first, out_second, factor * gradients[2], RATE_MATRIX, DECAY)
    new_conv = adam_step(conv_weight, conv_first, conv_second, factor * gradients[3], RATE_VECTOR, 0.0)
    new_gain = adam_step(gain_vector, gain_first, gain_second, factor * gradients[4], RATE_VECTOR, 0.0)
    new_head = adam_step(head_params, head_first, head_second, factor * gradients[5], RATE_VECTOR, 0.0)
    returned = result[inverse]
    return (returned.reshape(TOKENS, D).astype(jnp.bfloat16), gradients[0].reshape(TOKENS, D).astype(jnp.bfloat16), grad_norm, new_in[0], new_in[1], new_in[2], new_out[0], new_out[1], new_out[2], new_conv[0], new_conv[1], new_conv[2], new_gain[0], new_gain[1], new_gain[2], new_head[0], new_head[1], new_head[2], new_in[0].astype(jnp.bfloat16), new_out[0].astype(jnp.bfloat16))
```

```python
import functools

import jax
import jax.numpy as jnp
from jax import lax
from jax.experimental import pallas as pl
from jax.experimental.pallas import tpu as pltpu
from jax.sharding import PartitionSpec as P

HEAD_DIM = 64
STATE = 128
LEN = 1024
STEP = 5
CHUNK = 128
PAIR = 2 * HEAD_DIM

EPS_NORM = 1e-05
BETA_ONE = 0.5
BETA_TWO = 0.5
ADAM_EPS = 1e-08
DECAY = 0.1
RATE_MATRIX = 0.02
RATE_VECTOR = 0.8
CLIP_NORM = 1.0
HIGHEST_PRECISION = lax.Precision.HIGHEST
MASKED = -1e30
BF16 = jnp.bfloat16
F32 = jnp.float32


def sigmoid(values):
    return 1.0 / (1.0 + jnp.exp(-values))


def softplus(values):
    return jnp.maximum(values, 0.0) + jnp.log1p(jnp.exp(-jnp.abs(values)))


def dot_nn(left, right):
    return lax.dot_general(left, right, (((1,), (0,)), ((), ())), preferred_element_type=F32)


def dot_nt(left, right):
    return lax.dot_general(left, right, (((1,), (1,)), ((), ())), preferred_element_type=F32)


def dot_tn(left, right):
    return lax.dot_general(left, right, (((0,), (0,)), ((), ())), preferred_element_type=F32)


def dot_exact(left, right):
    return lax.dot_general(
        left,
        right,
        (((1,), (0,)), ((), ())),
        preferred_element_type=F32,
        precision=HIGHEST_PRECISION,
    )


def square_places():
    row = lax.broadcasted_iota(jnp.int32, (CHUNK, CHUNK), 0)
    column = lax.broadcasted_iota(jnp.int32, (CHUNK, CHUNK), 1)
    return row, column


def chunk_logs(step_ref, head_ref):
    biased = step_ref[...] + head_ref[:, 0:1]
    step = softplus(biased)
    row, column = square_places()
    upto = jnp.where(row <= column, 1.0, 0.0)
    logs = dot_exact(step * head_ref[:, 1:2], upto)
    padding = jnp.zeros((CHUNK - step.shape[0], CHUNK), F32)
    step_rows = jnp.transpose(jnp.concatenate([step, padding], axis=0))
    logs_rows = jnp.transpose(jnp.concatenate([logs, padding], axis=0))
    return biased, step, logs, step_rows, logs_rows


def spread(columns, head):
    return jnp.broadcast_to(columns[:, head : head + 1], (CHUNK, CHUNK))


def scan_forward_kernel(
    head_count, x_ref, bc_ref, step_ref, chan_ref, head_ref, y_ref, xc_ref, entry_ref, rows, state, fresh
):
    @pl.when(pl.program_id(1) == 0)
    def _():
        state[...] = jnp.zeros_like(state)
        rows[0:8, :] = jnp.zeros((8, rows.shape[1]), F32)

    rows[8 : 8 + CHUNK, :] = x_ref[...]
    entry_ref[0, 0] = state[...].astype(BF16)
    _, _, logs, step_rows, logs_rows = chunk_logs(step_ref, head_ref)
    state_in = bc_ref[:, :STATE]
    state_out = bc_ref[:, STATE:]
    scores = dot_nt(state_out, state_in)
    row, column = square_places()
    first_half = column < HEAD_DIM
    later = row >= column
    for pair in range(head_count // 2):
        lanes = slice(pair * PAIR, (pair + 1) * PAIR)
        conv = chan_ref[4:5, lanes]
        for tap in range(4):
            conv = conv + chan_ref[tap : tap + 1, lanes] * rows[5 + tap : 5 + tap + CHUNK, lanes]
        xc_ref[:, lanes] = conv
        values = conv * sigmoid(conv)
        even, odd = 2 * pair, 2 * pair + 1
        step_pair = jnp.where(first_half, spread(step_rows, even), spread(step_rows, odd))
        logs_even, logs_odd = spread(logs_rows, even), spread(logs_rows, odd)
        logs_pair = jnp.where(first_half, logs_even, logs_odd)
        within_even = jnp.exp(jnp.where(later, logs_even - logs[even : even + 1, :], MASKED))
        within_odd = jnp.exp(jnp.where(later, logs_odd - logs[odd : odd + 1, :], MASKED))
        mixing = jnp.concatenate(
            [(scores * within_even).astype(BF16), (scores * within_odd).astype(BF16)], axis=1
        )
        weighted = step_pair * values
        zero = jnp.zeros_like(weighted)
        stacked = jnp.concatenate(
            [
                jnp.where(first_half, weighted, zero).astype(BF16),
                jnp.where(first_half, zero, weighted).astype(BF16),
            ],
            axis=0,
        )
        inner = dot_nn(mixing, stacked)
        outer = dot_nn(state_out, entry_ref[0, 0, :, lanes]) * jnp.exp(logs_pair)
        y_ref[:, lanes] = inner + outer + chan_ref[5:6, lanes] * values
        last = logs_pair[CHUNK - 1 : CHUNK, :]
        fresh[:, lanes] = (jnp.exp(last - logs_pair) * weighted).astype(BF16)
        state[:, lanes] = jnp.exp(last) * state[:, lanes]
    state[...] += dot_tn(state_in, fresh[...])
    rows[0:8, :] = rows[CHUNK : CHUNK + 8, :]


def scan_backward_kernel(
    head_count,
    dy_ref,
    x_ref,
    xc_ref,
    bc_ref,
    step_ref,
    entry_ref,
    chan_ref,
    head_ref,
    dx_ref,
    dbc_ref,
    dstep_ref,
    dchan_ref,
    dhead_ref,
    rows,
    back,
    leaving,
    arriving,
    sums_one,
    sums_two,
    sums_three,
):
    @pl.when(pl.program_id(1) == 0)
    def _():
        back[...] = jnp.zeros_like(back)
        rows[CHUNK : CHUNK + 8, :] = jnp.zeros((8, rows.shape[1]), F32)

    @pl.when((pl.program_id(0) == 0) & (pl.program_id(1) == 0))
    def _():
        dchan_ref[...] = jnp.zeros_like(dchan_ref)
        dhead_ref[...] = jnp.zeros_like(dhead_ref)

    padded = step_ref.shape[0]
    biased, step, logs, step_rows, logs_rows = chunk_logs(step_ref, head_ref)
    state_in = bc_ref[:, :STATE]
    state_out = bc_ref[:, STATE:]
    scores = dot_nt(state_in, state_out)
    back_low = back[...].astype(BF16)
    entry = entry_ref[0, 0]
    row, column = square_places()
    first_half = column < HEAD_DIM
    later = column >= row
    head_row = lax.broadcasted_iota(jnp.int32, (padded, CHUNK), 0)
    total = jnp.zeros((CHUNK, CHUNK), F32)
    over_rows = jnp.zeros((padded, CHUNK), F32)
    over_columns = jnp.zeros((padded, CHUNK), F32)
    for pair in range(head_count // 2):
        lanes = slice(pair * PAIR, (pair + 1) * PAIR)
        even, odd = 2 * pair, 2 * pair + 1
        conv = xc_ref[:, lanes]
        gate = sigmoid(conv)
        values = conv * gate
        dy = dy_ref[:, lanes]
        step_pair = jnp.where(first_half, spread(step_rows, even), spread(step_rows, odd))
        logs_even, logs_odd = spread(logs_rows, even), spread(logs_rows, odd)
        logs_pair = jnp.where(first_half, logs_even, logs_odd)
        weighted = step_pair * values
        zero = jnp.zeros_like(weighted)
        dy_low = dy.astype(BF16)
        dy_stacked = jnp.concatenate(
            [
                jnp.where(first_half, dy, zero).astype(BF16),
                jnp.where(first_half, zero, dy).astype(BF16),
            ],
            axis=0,
        )
        transfers = []
        for head, log_column, part in (
            (even, logs_even, jnp.where(first_half, weighted, zero).astype(BF16)),
            (odd, logs_odd, jnp.where(first_half, zero, weighted).astype(BF16)),
        ):
            within = jnp.exp(jnp.where(later, logs[head : head + 1, :] - log_column, MASKED))
            product = within * dot_nt(part, dy_low)
            total = total + product
            crossing = (scores * product).astype(BF16)
            chosen = jnp.where(head_row == head, 1.0, 0.0).astype(BF16)
            over_rows = over_rows + dot_nn(chosen, crossing)
            over_columns = over_columns + dot_nt(chosen, crossing)
            transfers.append((scores * within).astype(BF16))
        grown = jnp.exp(logs_pair)
        last = logs_pair[CHUNK - 1 : CHUNK, :]
        to_end = jnp.exp(last - logs_pair)
        from_end = to_end * dot_nn(state_in, back_low[:, lanes])
        dweighted = dot_nn(jnp.concatenate(transfers, axis=1), dy_stacked) + from_end
        grown_dy = grown * dy
        leaving[:, lanes] = grown_dy.astype(BF16)
        arriving[:, lanes] = (to_end * weighted).astype(BF16)
        sums_one[:, lanes] = (grown_dy * dot_nn(state_out, entry[:, lanes])).astype(BF16)
        sums_two[:, lanes] = (weighted * from_end).astype(BF16)
        sums_three[:, lanes] = (values * dweighted).astype(BF16)
        dvalues = step_pair * dweighted + chan_ref[5:6, lanes] * dy
        dconv = dvalues * (gate * (1.0 + conv * (1.0 - gate)))
        rows[0:CHUNK, lanes] = dconv
        dchan_ref[5:6, lanes] += jnp.sum(dy * values, axis=0, keepdims=True)
        dchan_ref[4:5, lanes] += jnp.sum(dconv, axis=0, keepdims=True)
        raw = x_ref[:, lanes]
        dx = jnp.zeros((CHUNK, PAIR), F32)
        for tap in range(4):
            shifted = rows[3 - tap : 3 - tap + CHUNK, lanes]
            dx = dx + chan_ref[tap : tap + 1, lanes] * shifted
            dchan_ref[tap : tap + 1, lanes] += jnp.sum(raw * shifted, axis=0, keepdims=True)
        dx_ref[:, lanes] = dx.astype(BF16)
    rows[CHUNK : CHUNK + 8, :] = rows[0:8, :]
    total_low = total.astype(BF16)
    dbc_ref[:, :STATE] = (
        dot_nn(total_low, state_out) + dot_nt(arriving[...], back_low)
    ).astype(BF16)
    dbc_ref[:, STATE:] = (dot_tn(total_low, state_in) + dot_nt(leaving[...], entry)).astype(BF16)
    channels = back.shape[1]
    owner = lax.broadcasted_iota(jnp.int32, (padded, channels), 1) // HEAD_DIM
    member = owner == lax.broadcasted_iota(jnp.int32, (padded, channels), 0)
    member = jnp.where(member, 1.0, 0.0).astype(BF16)
    from_entry = dot_nt(member, sums_one[...])
    to_exit = dot_nt(member, sums_two[...])
    step_direct = dot_nt(member, sums_three[...])
    decay_last = jnp.concatenate(
        [
            jnp.exp(
                jnp.where(
                    first_half[0:1, :],
                    spread(logs_rows, 2 * pair)[CHUNK - 1 :, :],
                    spread(logs_rows, 2 * pair + 1)[CHUNK - 1 :, :],
                )
            )
            for pair in range(head_count // 2)
        ],
        axis=1,
    )
    decayed = decay_last * back[...]
    carried = jnp.sum(decayed * entry.astype(F32), axis=0, keepdims=True)
    carried = jnp.broadcast_to(carried, (CHUNK, channels)).astype(BF16)
    carried = dot_nt(member, carried)
    back[...] = decayed + dot_tn(state_out, leaving[...])
    onward = jnp.where(row >= column, 1.0, 0.0)
    before = jnp.where(row < column, 1.0, 0.0)
    dlogs = dot_exact(over_rows - over_columns + from_entry, onward) + dot_exact(to_exit, before)
    dlogs = dlogs + carried
    rate = head_ref[:, 1:2]
    dstep = (rate * dlogs + step_direct) * sigmoid(biased)
    dstep_ref[...] = dstep
    dhead_ref[:, 0:1] += jnp.sum(dstep, axis=1, keepdims=True)
    dhead_ref[:, 1:2] += rate * jnp.sum(step * dlogs, axis=1, keepdims=True)


def chunk_specs(seq_count, channels, padded, reverse):
    chunks = LEN // CHUNK

    def place(seq, chunk):
        return chunks - 1 - chunk if reverse else chunk

    def by_rows(width):
        return pl.BlockSpec(
            (CHUNK, width), lambda seq, chunk: (seq * chunks + place(seq, chunk), 0)
        )

    step_spec = pl.BlockSpec((padded, CHUNK), lambda seq, chunk: (seq, place(seq, chunk)))
    entry_spec = pl.BlockSpec(
        (1, 1, STATE, channels), lambda seq, chunk: (seq, place(seq, chunk), 0, 0)
    )

    def fixed(*shape):
        return pl.BlockSpec(shape, lambda seq, chunk: (0, 0))

    return (seq_count, chunks), by_rows, step_spec, entry_spec, fixed


def scan_forward(x_pre, states, step_pre, chan, heads, head_count):
    token_rows, channels = x_pre.shape
    padded = heads.shape[0]
    seq_count = token_rows // LEN
    grid, by_rows, step_spec, entry_spec, fixed = chunk_specs(seq_count, channels, padded, False)
    return pl.pallas_call(
        functools.partial(scan_forward_kernel, head_count),
        grid=grid,
        in_specs=[
            by_rows(channels),
            by_rows(2 * STATE),
            step_spec,
            fixed(8, channels),
            fixed(padded, 128),
        ],
        out_specs=[by_rows(channels), by_rows(channels), entry_spec],
        out_shape=[
            jax.ShapeDtypeStruct((token_rows, channels), F32),
            jax.ShapeDtypeStruct((token_rows, channels), F32),
            jax.ShapeDtypeStruct((seq_count, LEN // CHUNK, STATE, channels), BF16),
        ],
        scratch_shapes=[
            pltpu.VMEM((CHUNK + 8, channels), F32),
            pltpu.VMEM((STATE, channels), F32),
            pltpu.VMEM((CHUNK, channels), BF16),
        ],
        compiler_params=pltpu.CompilerParams(vmem_limit_bytes=32 * 1024 * 1024),
        name="scan_forward",
    )(x_pre, states, step_pre, chan, heads)


def scan_backward(dy, x_pre, conv, states, step_pre, entry, chan, heads, head_count):
    token_rows, channels = x_pre.shape
    padded = heads.shape[0]
    seq_count = token_rows // LEN
    grid, by_rows, step_spec, entry_spec, fixed = chunk_specs(seq_count, channels, padded, True)
    low_rows = pltpu.VMEM((CHUNK, channels), BF16)
    return pl.pallas_call(
        functools.partial(scan_backward_kernel, head_count),
        grid=grid,
        in_specs=[
            by_rows(channels),
            by_rows(channels),
            by_rows(channels),
            by_rows(2 * STATE),
            step_spec,
            entry_spec,
            fixed(8, channels),
            fixed(padded, 128),
        ],
        out_specs=[
            by_rows(channels),
            by_rows(2 * STATE),
            step_spec,
            fixed(8, channels),
            fixed(padded, 128),
        ],
        out_shape=[
            jax.ShapeDtypeStruct((token_rows, channels), BF16),
            jax.ShapeDtypeStruct((token_rows, 2 * STATE), BF16),
            jax.ShapeDtypeStruct((seq_count * padded, LEN), F32),
            jax.ShapeDtypeStruct((8, channels), F32),
            jax.ShapeDtypeStruct((padded, 128), F32),
        ],
        scratch_shapes=[
            pltpu.VMEM((CHUNK + 8, channels), F32),
            pltpu.VMEM((STATE, channels), F32),
            low_rows,
            low_rows,
            low_rows,
            low_rows,
            low_rows,
        ],
        compiler_params=pltpu.CompilerParams(vmem_limit_bytes=32 * 1024 * 1024),
        name="scan_backward",
    )(dy, x_pre, conv, states, step_pre, entry, chan, heads)


def causal_conv(values, taps):
    width = taps.shape[1] - 1
    length = values.shape[1]
    padded = jnp.pad(values, ((0, 0), (width - 1, 0), (0, 0)))
    result = jnp.zeros_like(values) + taps[:, width]
    for offset in range(width):
        result = result + taps[:, offset] * padded[:, offset : offset + length, :]
    return result


def adam_step(weight, first, second, grad, rate, decay):
    first = BETA_ONE * first + (1.0 - BETA_ONE) * grad
    second = BETA_TWO * second + (1.0 - BETA_TWO) * grad * grad
    update = first / (1.0 - BETA_ONE**STEP) / (jnp.sqrt(second / (1.0 - BETA_TWO**STEP)) + ADAM_EPS)
    return (weight - rate * (update + decay * weight), first, second)


def gather_dp(values):
    return lax.all_gather(values, "dp", axis=0, tiled=True)


def scatter_dp(values):
    return lax.psum_scatter(values, "dp", scatter_dimension=0, tiled=True).astype(F32)


def gather_tensor(values, axis):
    return lax.all_gather(values, "tensor", axis=axis, tiled=True)


def scatter_tensor(values, axis):
    return lax.psum_scatter(values, "tensor", scatter_dimension=axis, tiled=True).astype(F32)


def sum_over(values, axes):
    for axis in axes:
        count = lax.axis_size(axis)
        step = 1
        while step < count:
            pairs = [(place, place ^ step) for place in range(count)]
            values = values + lax.ppermute(values, axis, pairs)
            step *= 2
    return values


def deal(values, sources):
    count = lax.axis_size("dp")
    own_rows, width = values.shape
    pieces = values.reshape(count, own_rows // count, width)
    spread_out = lax.all_to_all(pieces, "dp", split_axis=0, concat_axis=0, tiled=True)
    chosen = jnp.take(spread_out, sources, axis=0)
    arrived = lax.all_to_all(chosen, "dp", split_axis=0, concat_axis=0, tiled=True)
    return arrived.reshape(own_rows, width)


def shards(
    tokens,
    cotangent,
    lengths,
    order,
    in_weight,
    in_first,
    in_second,
    out_weight,
    out_first,
    out_second,
    conv_weight,
    conv_first,
    conv_second,
    gain_vector,
    gain_first,
    gain_second,
    head_params,
    head_first,
    head_second,
):
    count_dp = lax.axis_size("dp")
    count_tensor = lax.axis_size("tensor")
    group = lax.axis_index("dp")
    place = lax.axis_index("tensor")
    own_rows, width = tokens.shape
    token_rows = own_rows * count_tensor
    seq_count = token_rows // LEN
    seq_total = order.shape[0]
    head_count = head_params.shape[0]
    padded_heads = -(-head_count // 8) * 8
    inner_cols = head_count * HEAD_DIM
    conv_rows = conv_weight.shape[0]
    state_cols = conv_rows - inner_cols
    inner_total = inner_cols * count_tensor
    norm_gain = gain_vector[:width]
    gate_gain = lax.dynamic_slice_in_dim(gain_vector, width + place * inner_cols, inner_cols, 0)

    positions = jnp.arange(seq_total)
    inverse = jnp.sum(
        jnp.where(order[:, None] == positions[None, :], positions[:, None], 0), axis=0
    )
    own_seq = (place * own_rows) // LEN
    sources = inverse[jnp.arange(count_dp) * seq_count + own_seq] // seq_count
    cot_own = deal(cotangent, sources)
    seq_lengths = lax.dynamic_slice_in_dim(lengths, group * seq_count, seq_count, 0)
    live_all = (
        (jnp.arange(LEN)[None, :] < seq_lengths[:, None]).astype(F32).reshape(token_rows, 1)
    )
    live_own = lax.dynamic_slice_in_dim(live_all, place * own_rows, own_rows, 0)

    in_low = in_weight.astype(BF16)
    in_mixed = gather_dp(in_low[:, inner_cols:])
    in_gate = gather_dp(in_low[:, :inner_cols])
    out_low = gather_dp(out_weight.astype(BF16).T)

    own = tokens.astype(F32)
    inv_own = lax.rsqrt(jnp.mean(own * own, axis=1, keepdims=True) + EPS_NORM)
    normed_own = (own * inv_own * norm_gain).astype(BF16)
    normed = gather_tensor(normed_own, 0)

    back_out_own = (cot_own.astype(F32) * live_own).astype(BF16)
    back_out = gather_tensor(back_out_own, 0)

    inner_pre = dot_nn(normed, in_mixed[:, :inner_cols])
    side_pre = dot_nn(normed, in_mixed[:, inner_cols:])
    state_pre = side_pre[:, :state_cols]
    step_pre = side_pre[:, state_cols:].reshape(seq_count, LEN, head_count)
    step_pre = jnp.pad(
        jnp.swapaxes(step_pre, 1, 2), ((0, 0), (0, padded_heads - head_count), (0, 0))
    ).reshape(seq_count * padded_heads, LEN)
    chan = jnp.concatenate(
        [
            conv_weight[:inner_cols].T,
            jnp.repeat(head_params[:, 2], HEAD_DIM)[None, :],
            jnp.zeros((2, inner_cols), F32),
        ],
        axis=0,
    )
    rate = -jnp.exp(head_params[:, 1])
    heads = jnp.pad(
        jnp.stack([head_params[:, 0], rate], axis=1),
        ((0, padded_heads - head_count), (0, 126)),
    )

    def state_local(values, taps):
        return jax.nn.silu(causal_conv(values.reshape(seq_count, LEN, -1), taps)).reshape(
            token_rows, -1
        )

    state_own, state_pull = jax.vjp(state_local, state_pre, conv_weight[inner_cols:])
    states = gather_tensor(state_own.astype(BF16), 1)

    scanned, conv, entry = scan_forward(inner_pre, states, step_pre, chan, heads, head_count)

    gate_pre = dot_nn(normed, in_gate)
    gate_sigmoid = jax.nn.sigmoid(gate_pre)
    gate = gate_pre * gate_sigmoid
    mixed = scanned * gate
    back_normed = dot_nn(back_out, out_low)
    row_sums = jnp.stack(
        [jnp.sum(mixed * mixed, axis=1), jnp.sum(back_normed * gate_gain * mixed, axis=1)]
    )
    row_sums = lax.psum(row_sums, "tensor")
    gate_inv = lax.rsqrt(row_sums[0] / inner_total + EPS_NORM)[:, None]
    scaled = mixed * gate_inv
    normed_out = (scaled * gate_gain).astype(BF16)
    partial_out = dot_nt(normed_out, out_low)
    branch = scatter_tensor(partial_out.astype(BF16), 0)
    layer_output = (live_own * (own + branch)).astype(BF16)

    grad_out = scatter_dp(dot_tn(back_out, normed_out).astype(BF16)).T
    grad_gate_gain = jnp.sum(back_normed * scaled, axis=0)
    back_mixed = gate_inv * (back_normed * gate_gain) - mixed * (
        gate_inv**3 * (row_sums[1][:, None] / inner_total)
    )
    back_gate = (
        back_mixed * scanned * (gate_sigmoid * (1.0 + gate_pre * (1.0 - gate_sigmoid)))
    ).astype(BF16)
    grad_in_gate = scatter_dp(dot_tn(normed, back_gate).astype(BF16))

    back_inner, back_states, back_step, dchan, dhead = scan_backward(
        back_mixed * gate, inner_pre, conv, states, step_pre, entry, chan, heads, head_count
    )
    state_back = scatter_tensor(back_states, 1)
    back_state_pre, grad_taps_state = state_pull(state_back)
    back_step = jnp.swapaxes(back_step.reshape(seq_count, padded_heads, LEN), 1, 2)
    back_step = back_step[:, :, :head_count].reshape(token_rows, head_count)
    back_side = jnp.concatenate([back_state_pre, back_step], axis=1).astype(BF16)
    back_rest = jnp.concatenate([back_inner, back_side], axis=1)
    grad_in_mixed = scatter_dp(dot_tn(normed, back_rest).astype(BF16))
    back_input = dot_nt(back_gate, in_gate) + dot_nt(back_rest, in_mixed)
    back_part = scatter_tensor(back_input.astype(BF16), 0)
    row_term = jnp.sum(back_part * norm_gain * own, axis=1, keepdims=True)
    back_own = inv_own * norm_gain * back_part - own * inv_own**3 * (row_term / width)
    input_grad = (live_own * cot_own.astype(F32) + back_own).astype(BF16)
    grad_norm_gain = jnp.sum(back_part * own * inv_own, axis=0)

    grad_heads = jnp.stack(
        [
            dhead[:head_count, 0],
            dhead[:head_count, 1],
            jnp.sum(dchan[5].reshape(head_count, HEAD_DIM), axis=1),
        ],
        axis=1,
    )
    side = jnp.concatenate(
        [
            dchan[:5].reshape(-1),
            grad_taps_state.reshape(-1),
            grad_heads.reshape(-1),
            grad_gate_gain,
        ]
    )
    side_sum = sum_over(side, ("dp",))
    grad_conv = jnp.concatenate(
        [
            side_sum[: 5 * inner_cols].reshape(5, inner_cols).T,
            side_sum[5 * inner_cols : 5 * conv_rows].reshape(state_cols, 5),
        ],
        axis=0,
    )
    heads_end = 5 * conv_rows + 3 * head_count
    grad_head = side_sum[5 * conv_rows : heads_end].reshape(head_count, 3)
    grad_gate_all = gather_tensor(side_sum[heads_end:], 0)
    grad_norm_all = sum_over(grad_norm_gain, ("tensor", "dp"))
    grad_gains = jnp.concatenate([grad_norm_all, grad_gate_all])
    squares = (
        jnp.sum(grad_in_mixed * grad_in_mixed)
        + jnp.sum(grad_in_gate * grad_in_gate)
        + jnp.sum(grad_out * grad_out)
        + jnp.sum(side_sum * side_sum) / count_dp
    )
    squares = sum_over(squares.reshape(1, 1), ("tensor", "dp"))[0, 0]
    grad_norm = jnp.sqrt(squares + jnp.sum(grad_norm_all * grad_norm_all))
    factor = CLIP_NORM / jnp.maximum(grad_norm, CLIP_NORM)
    grad_in = jnp.concatenate([grad_in_gate, grad_in_mixed], axis=1)
    new_in = adam_step(in_weight, in_first, in_second, factor * grad_in, RATE_MATRIX, DECAY)
    new_out = adam_step(out_weight, out_first, out_second, factor * grad_out, RATE_MATRIX, DECAY)
    new_conv = adam_step(conv_weight, conv_first, conv_second, factor * grad_conv, RATE_VECTOR, 0.0)
    new_gain = adam_step(
        gain_vector, gain_first, gain_second, factor * grad_gains, RATE_VECTOR, 0.0
    )
    new_head = adam_step(head_params, head_first, head_second, factor * grad_head, RATE_VECTOR, 0.0)
    return (
        layer_output,
        input_grad,
        grad_norm,
        *new_in,
        *new_out,
        *new_conv,
        *new_gain,
        *new_head,
        new_in[0].astype(BF16),
        new_out[0].astype(BF16),
    )


def solution(mesh):
    rows = P(("dp", "tensor"), None)
    in_matrix = P("dp", "tensor")
    out_matrix = P("tensor", "dp")
    by_tensor = P("tensor", None)
    same = P()
    in_specs = (
        (rows, rows, same, same)
        + (in_matrix,) * 3
        + (out_matrix,) * 3
        + (by_tensor,) * 3
        + (same,) * 3
        + (by_tensor,) * 3
    )
    out_specs = (
        (rows, rows, same)
        + (in_matrix,) * 3
        + (out_matrix,) * 3
        + (by_tensor,) * 3
        + (same,) * 3
        + (by_tensor,) * 3
        + (in_matrix, out_matrix)
    )
    return jax.shard_map(shards, mesh=mesh, in_specs=in_specs, out_specs=out_specs, check_vma=False)
```

```python
import functools

import jax
import jax.numpy as jnp
from jax import lax
from jax.experimental import pallas as pl
from jax.experimental.pallas import tpu as pltpu
from jax.sharding import PartitionSpec as P

HEAD_DIM = 64
STATE = 128
LEN = 1024
STEP = 5
CHUNK = 128
PAIR = 2 * HEAD_DIM

EPS_NORM = 1e-05
BETA_ONE = 0.5
BETA_TWO = 0.5
ADAM_EPS = 1e-08
DECAY = 0.1
RATE_MATRIX = 0.02
RATE_VECTOR = 0.8
CLIP_NORM = 1.0
HIGHEST_PRECISION = lax.Precision.HIGHEST
MASKED = -1e30
BF16 = jnp.bfloat16
F32 = jnp.float32


def sigmoid(values):
    return 1.0 / (1.0 + jnp.exp(-values))


def softplus(values):
    return jnp.maximum(values, 0.0) + jnp.log1p(jnp.exp(-jnp.abs(values)))


def dot_nn(left, right):
    return lax.dot_general(left, right, (((1,), (0,)), ((), ())), preferred_element_type=F32)


def dot_nt(left, right):
    return lax.dot_general(left, right, (((1,), (1,)), ((), ())), preferred_element_type=F32)


def dot_tn(left, right):
    return lax.dot_general(left, right, (((0,), (0,)), ((), ())), preferred_element_type=F32)


def dot_general_tt(left, right):
    return lax.dot_general(left, right, (((0,), (1,)), ((), ())), preferred_element_type=F32)


def by_sequence(values, seq_count):
    if seq_count == 1:
        return values
    rows = values.shape[0]
    return jnp.swapaxes(values.reshape(rows, seq_count, LEN), 0, 1).reshape(-1, LEN)


def from_sequence(values, seq_count):
    if seq_count == 1:
        return values
    rows = values.shape[0] // seq_count
    return jnp.swapaxes(values.reshape(seq_count, rows, LEN), 0, 1).reshape(rows, -1)


def dot_exact(left, right):
    return lax.dot_general(
        left,
        right,
        (((1,), (0,)), ((), ())),
        preferred_element_type=F32,
        precision=HIGHEST_PRECISION,
    )


def square_places():
    row = lax.broadcasted_iota(jnp.int32, (CHUNK, CHUNK), 0)
    column = lax.broadcasted_iota(jnp.int32, (CHUNK, CHUNK), 1)
    return row, column


def chunk_logs(step_ref, head_ref):
    biased = step_ref[...] + head_ref[:, 0:1]
    step = softplus(biased)
    row, column = square_places()
    upto = jnp.where(row <= column, 1.0, 0.0)
    logs = dot_exact(step * head_ref[:, 1:2], upto)
    padding = jnp.zeros((CHUNK - step.shape[0], CHUNK), F32)
    step_rows = jnp.transpose(jnp.concatenate([step, padding], axis=0))
    logs_rows = jnp.transpose(jnp.concatenate([logs, padding], axis=0))
    return biased, step, logs, step_rows, logs_rows


def spread(columns, head):
    return jnp.broadcast_to(columns[:, head : head + 1], (CHUNK, CHUNK))


def scan_forward_kernel(
    head_count, x_ref, bc_ref, step_ref, chan_ref, head_ref, y_ref, xc_ref, entry_ref, rows, state, fresh
):
    @pl.when(pl.program_id(1) == 0)
    def _():
        state[...] = jnp.zeros_like(state)
        rows[0:8, :] = jnp.zeros((8, rows.shape[1]), F32)

    rows[8 : 8 + CHUNK, :] = x_ref[...]
    entry_ref[0, 0] = state[...].astype(BF16)
    _, _, logs, step_rows, logs_rows = chunk_logs(step_ref, head_ref)
    in_columns = bc_ref[:STATE, :]
    state_out = jnp.transpose(bc_ref[STATE:, :])
    scores = dot_nn(state_out, in_columns)
    row, column = square_places()
    first_half = column < HEAD_DIM
    later = row >= column
    for pair in range(head_count // 2):
        lanes = slice(pair * PAIR, (pair + 1) * PAIR)
        conv = chan_ref[4:5, lanes]
        for tap in range(4):
            conv = conv + chan_ref[tap : tap + 1, lanes] * rows[5 + tap : 5 + tap + CHUNK, lanes]
        xc_ref[:, lanes] = conv
        values = conv * sigmoid(conv)
        even, odd = 2 * pair, 2 * pair + 1
        step_pair = jnp.where(first_half, spread(step_rows, even), spread(step_rows, odd))
        logs_even, logs_odd = spread(logs_rows, even), spread(logs_rows, odd)
        logs_pair = jnp.where(first_half, logs_even, logs_odd)
        within_even = jnp.exp(jnp.where(later, logs_even - logs[even : even + 1, :], MASKED))
        within_odd = jnp.exp(jnp.where(later, logs_odd - logs[odd : odd + 1, :], MASKED))
        mixing = jnp.concatenate(
            [(scores * within_even).astype(BF16), (scores * within_odd).astype(BF16)], axis=1
        )
        weighted = step_pair * values
        zero = jnp.zeros_like(weighted)
        stacked = jnp.concatenate(
            [
                jnp.where(first_half, weighted, zero).astype(BF16),
                jnp.where(first_half, zero, weighted).astype(BF16),
            ],
            axis=0,
        )
        inner = dot_nn(mixing, stacked)
        outer = dot_nn(state_out, entry_ref[0, 0, :, lanes]) * jnp.exp(logs_pair)
        y_ref[:, lanes] = inner + outer + chan_ref[5:6, lanes] * values
        last = logs_pair[CHUNK - 1 : CHUNK, :]
        fresh[:, lanes] = (jnp.exp(last - logs_pair) * weighted).astype(BF16)
        state[:, lanes] = jnp.exp(last) * state[:, lanes]
    state[...] += dot_nn(in_columns, fresh[...])
    rows[0:8, :] = rows[CHUNK : CHUNK + 8, :]


def scan_backward_kernel(
    first_head,
    head_count,
    dy_ref,
    x_ref,
    xc_ref,
    bc_ref,
    step_ref,
    entry_ref,
    chan_ref,
    head_ref,
    *outputs_and_scratch,
):
    (
    dx_ref,
    dbc_ref,
    dstep_ref,
    dchan_ref,
    dhead_ref,
    rows,
    back,
    leaving,
    arriving,
    sums_one,
    sums_two,
    sums_three,
    ) = outputs_and_scratch[-12:]

    @pl.when(pl.program_id(1) == 0)
    def _():
        back[...] = jnp.zeros_like(back)
        rows[CHUNK : CHUNK + 8, :] = jnp.zeros((8, rows.shape[1]), F32)

    @pl.when((pl.program_id(0) == 0) & (pl.program_id(1) == 0))
    def _():
        dchan_ref[...] = jnp.zeros_like(dchan_ref)
        dhead_ref[...] = jnp.zeros_like(dhead_ref)

    padded = step_ref.shape[0]
    biased, step, logs, step_rows, logs_rows = chunk_logs(step_ref, head_ref)
    in_columns = bc_ref[:STATE, :]
    out_columns = bc_ref[STATE:, :]
    state_in = jnp.transpose(in_columns)
    state_out = jnp.transpose(out_columns)
    scores = dot_nn(state_in, out_columns)
    back_low = back[...].astype(BF16)
    entry = entry_ref[0, 0]
    row, column = square_places()
    first_half = column < HEAD_DIM
    later = column >= row
    head_row = lax.broadcasted_iota(jnp.int32, (padded, CHUNK), 0)
    total = jnp.zeros((CHUNK, CHUNK), F32)
    over_rows = jnp.zeros((padded, CHUNK), F32)
    over_columns = jnp.zeros((padded, CHUNK), F32)
    for pair in range(head_count // 2):
        lanes = slice(pair * PAIR, (pair + 1) * PAIR)
        even = first_head + 2 * pair
        odd = even + 1
        conv = xc_ref[:, lanes]
        gate = sigmoid(conv)
        values = conv * gate
        dy = dy_ref[:, lanes]
        step_pair = jnp.where(first_half, spread(step_rows, even), spread(step_rows, odd))
        logs_even, logs_odd = spread(logs_rows, even), spread(logs_rows, odd)
        logs_pair = jnp.where(first_half, logs_even, logs_odd)
        weighted = step_pair * values
        zero = jnp.zeros_like(weighted)
        dy_low = dy.astype(BF16)
        dy_stacked = jnp.concatenate(
            [
                jnp.where(first_half, dy, zero).astype(BF16),
                jnp.where(first_half, zero, dy).astype(BF16),
            ],
            axis=0,
        )
        transfers = []
        for head, log_column, part in (
            (even, logs_even, jnp.where(first_half, weighted, zero).astype(BF16)),
            (odd, logs_odd, jnp.where(first_half, zero, weighted).astype(BF16)),
        ):
            within = jnp.exp(jnp.where(later, logs[head : head + 1, :] - log_column, MASKED))
            product = within * dot_nt(part, dy_low)
            total = total + product
            crossing = (scores * product).astype(BF16)
            chosen = jnp.where(head_row == head, 1.0, 0.0).astype(BF16)
            over_rows = over_rows + dot_nn(chosen, crossing)
            over_columns = over_columns + dot_nt(chosen, crossing)
            transfers.append((scores * within).astype(BF16))
        grown = jnp.exp(logs_pair)
        last = logs_pair[CHUNK - 1 : CHUNK, :]
        to_end = jnp.exp(last - logs_pair)
        from_end = to_end * dot_nn(state_in, back_low[:, lanes])
        dweighted = dot_nn(jnp.concatenate(transfers, axis=1), dy_stacked) + from_end
        grown_dy = grown * dy
        leaving[:, lanes] = grown_dy.astype(BF16)
        arriving[:, lanes] = (to_end * weighted).astype(BF16)
        sums_one[:, lanes] = (grown_dy * dot_nn(state_out, entry[:, lanes])).astype(BF16)
        sums_two[:, lanes] = (weighted * from_end).astype(BF16)
        sums_three[:, lanes] = (values * dweighted).astype(BF16)
        dvalues = step_pair * dweighted + chan_ref[5:6, lanes] * dy
        dconv = dvalues * (gate * (1.0 + conv * (1.0 - gate)))
        rows[0:CHUNK, lanes] = dconv
        dchan_ref[5:6, lanes] += jnp.sum(dy * values, axis=0, keepdims=True)
        dchan_ref[4:5, lanes] += jnp.sum(dconv, axis=0, keepdims=True)
        raw = x_ref[:, lanes]
        dx = jnp.zeros((CHUNK, PAIR), F32)
        for tap in range(4):
            shifted = rows[3 - tap : 3 - tap + CHUNK, lanes]
            dx = dx + chan_ref[tap : tap + 1, lanes] * shifted
            dchan_ref[tap : tap + 1, lanes] += jnp.sum(raw * shifted, axis=0, keepdims=True)
        dx_ref[:, lanes] = dx.astype(BF16)
    rows[CHUNK : CHUNK + 8, :] = rows[0:8, :]
    total_low = total.astype(BF16)
    dbc_ref[:STATE, :] = (
        dot_nt(out_columns, total_low) + dot_nt(back_low, arriving[...])
    ).astype(BF16)
    dbc_ref[STATE:, :] = (dot_nn(in_columns, total_low) + dot_nt(entry, leaving[...])).astype(BF16)
    channels = back.shape[1]
    owner = first_head + lax.broadcasted_iota(jnp.int32, (padded, channels), 1) // HEAD_DIM
    member = owner == lax.broadcasted_iota(jnp.int32, (padded, channels), 0)
    member = jnp.where(member, 1.0, 0.0).astype(BF16)
    from_entry = dot_nt(member, sums_one[...])
    to_exit = dot_nt(member, sums_two[...])
    step_direct = dot_nt(member, sums_three[...])
    decay_last = jnp.concatenate(
        [
            jnp.exp(
                jnp.where(
                    first_half[0:1, :],
                    spread(logs_rows, first_head + 2 * pair)[CHUNK - 1 :, :],
                    spread(logs_rows, first_head + 2 * pair + 1)[CHUNK - 1 :, :],
                )
            )
            for pair in range(head_count // 2)
        ],
        axis=1,
    )
    decayed = decay_last * back[...]
    carried = jnp.sum(decayed * entry.astype(F32), axis=0, keepdims=True)
    carried = jnp.broadcast_to(carried, (CHUNK, channels)).astype(BF16)
    carried = dot_nt(member, carried)
    back[...] = decayed + dot_nn(out_columns, leaving[...])
    onward = jnp.where(row >= column, 1.0, 0.0)
    before = jnp.where(row < column, 1.0, 0.0)
    dlogs = dot_exact(over_rows - over_columns + from_entry, onward) + dot_exact(to_exit, before)
    dlogs = dlogs + carried
    rate = head_ref[:, 1:2]
    dstep = (rate * dlogs + step_direct) * sigmoid(biased)
    dstep_ref[...] = dstep
    dhead_ref[:, 0:1] += jnp.sum(dstep, axis=1, keepdims=True)
    dhead_ref[:, 1:2] += rate * jnp.sum(step * dlogs, axis=1, keepdims=True)


def chunk_specs(seq_count, channels, padded, reverse):
    chunks = LEN // CHUNK

    def place(seq, chunk):
        return chunks - 1 - chunk if reverse else chunk

    def by_rows(width):
        return pl.BlockSpec(
            (CHUNK, width), lambda seq, chunk: (seq * chunks + place(seq, chunk), 0)
        )

    step_spec = pl.BlockSpec((padded, CHUNK), lambda seq, chunk: (seq, place(seq, chunk)))
    entry_spec = pl.BlockSpec(
        (1, 1, STATE, channels), lambda seq, chunk: (seq, place(seq, chunk), 0, 0)
    )

    def fixed(*shape):
        return pl.BlockSpec(shape, lambda seq, chunk: (0, 0))

    state_spec = pl.BlockSpec((2 * STATE, CHUNK), lambda seq, chunk: (seq, place(seq, chunk)))
    return (seq_count, chunks), by_rows, step_spec, state_spec, entry_spec, fixed


def scan_forward(x_pre, states, step_pre, chan, heads, head_count):
    token_rows, channels = x_pre.shape
    padded = heads.shape[0]
    seq_count = token_rows // LEN
    grid, by_rows, step_spec, state_spec, entry_spec, fixed = chunk_specs(seq_count, channels, padded, False)
    return pl.pallas_call(
        functools.partial(scan_forward_kernel, head_count),
        grid=grid,
        in_specs=[
            by_rows(channels),
            state_spec,
            step_spec,
            fixed(8, channels),
            fixed(padded, 128),
        ],
        out_specs=[by_rows(channels), by_rows(channels), entry_spec],
        out_shape=[
            jax.ShapeDtypeStruct((token_rows, channels), F32),
            jax.ShapeDtypeStruct((token_rows, channels), F32),
            jax.ShapeDtypeStruct((seq_count, LEN // CHUNK, STATE, channels), BF16),
        ],
        scratch_shapes=[
            pltpu.VMEM((CHUNK + 8, channels), F32),
            pltpu.VMEM((STATE, channels), F32),
            pltpu.VMEM((CHUNK, channels), BF16),
        ],
        compiler_params=pltpu.CompilerParams(vmem_limit_bytes=32 * 1024 * 1024),
        cost_estimate=pl.CostEstimate(
            flops=token_rows * channels * 14000, bytes_accessed=0, transcendentals=0
        ),
        name="scan_forward",
    )(x_pre, states, step_pre, chan, heads)


def scan_backward(dy, x_pre, conv, states, step_pre, entry, chan, heads, head_count, part, parts, held):
    token_rows, channels = x_pre.shape
    padded = heads.shape[0]
    seq_count = token_rows // LEN
    part_heads = head_count // parts
    width = channels // parts
    chunks = LEN // CHUNK

    def by_rows(seq, chunk):
        return seq * chunks + chunks - 1 - chunk, part

    wide = pl.BlockSpec((CHUNK, width), by_rows)
    step_spec = pl.BlockSpec((padded, CHUNK), lambda seq, chunk: (seq, chunks - 1 - chunk))
    state_spec = pl.BlockSpec((2 * STATE, CHUNK), lambda seq, chunk: (seq, chunks - 1 - chunk))
    entry_spec = pl.BlockSpec(
        (1, 1, STATE, width), lambda seq, chunk: (seq, chunks - 1 - chunk, 0, part)
    )
    chan_spec = pl.BlockSpec((8, width), lambda seq, chunk: (0, part))
    head_spec = pl.BlockSpec((padded, 128), lambda seq, chunk: (0, 0))
    low_rows = pltpu.VMEM((CHUNK, width), BF16)
    in_specs = [wide, wide, wide, state_spec, step_spec, entry_spec, chan_spec, head_spec]
    in_place = {}
    if held:
        in_place = {len(in_specs): 0, len(in_specs) + 1: 3}
        in_specs = in_specs + [pl.BlockSpec(memory_space=pl.ANY)] * 2
    return pl.pallas_call(
        functools.partial(scan_backward_kernel, part * part_heads, part_heads),
        grid=(seq_count, chunks),
        in_specs=in_specs,
        out_specs=[wide, state_spec, step_spec, chan_spec, head_spec],
        out_shape=[
            jax.ShapeDtypeStruct((token_rows, channels), BF16),
            jax.ShapeDtypeStruct((seq_count * 2 * STATE, LEN), BF16),
            jax.ShapeDtypeStruct((seq_count * padded, LEN), F32),
            jax.ShapeDtypeStruct((8, channels), F32),
            jax.ShapeDtypeStruct((padded, 128), F32),
        ],
        scratch_shapes=[
            pltpu.VMEM((CHUNK + 8, width), F32),
            pltpu.VMEM((STATE, width), F32),
            low_rows,
            low_rows,
            low_rows,
            low_rows,
            low_rows,
        ],
        input_output_aliases=in_place,
        compiler_params=pltpu.CompilerParams(vmem_limit_bytes=32 * 1024 * 1024),
        cost_estimate=pl.CostEstimate(
            flops=token_rows * width * 50000, bytes_accessed=0, transcendentals=0
        ),
        name="scan_backward",
    )(dy, x_pre, conv, states, step_pre, entry, chan, heads, *held)


def lane_shift(values, amount):
    if amount == 0:
        return values
    lane = lax.broadcasted_iota(jnp.int32, values.shape, 1)
    if amount > 0:
        return jnp.where(lane >= amount, pltpu.roll(values, amount, 1), 0.0)
    return jnp.where(lane < LEN + amount, pltpu.roll(values, LEN + amount, 1), 0.0)


def state_conv(pre, taps_ref):
    conv = jnp.broadcast_to(taps_ref[:, 4:5], pre.shape)
    for tap in range(4):
        conv = conv + taps_ref[:, tap : tap + 1] * lane_shift(pre, 3 - tap)
    return conv


def state_forward_kernel(pre_ref, taps_ref, states_ref):
    conv = state_conv(pre_ref[...], taps_ref)
    states_ref[...] = (conv * sigmoid(conv)).astype(BF16)


def state_backward_kernel(back_ref, pre_ref, taps_ref, dpre_ref, dtaps_ref):
    @pl.when(pl.program_id(0) == 0)
    def _():
        dtaps_ref[...] = jnp.zeros_like(dtaps_ref)

    pre = pre_ref[...]
    conv = state_conv(pre, taps_ref)
    gate = sigmoid(conv)
    dconv = back_ref[...] * (gate * (1.0 + conv * (1.0 - gate)))
    dpre = jnp.zeros_like(pre)
    for tap in range(4):
        shifted = lane_shift(dconv, tap - 3)
        dpre = dpre + taps_ref[:, tap : tap + 1] * shifted
        dtaps_ref[:, tap : tap + 1] += jnp.sum(pre * shifted, axis=1, keepdims=True)
    dtaps_ref[:, 4:5] += jnp.sum(dconv, axis=1, keepdims=True)
    dpre_ref[...] = dpre.astype(BF16)


def state_forward(pre, taps, seq_count):
    rows = pre.shape[0] // seq_count
    by_seq = pl.BlockSpec((rows, LEN), lambda seq: (seq, 0))
    return pl.pallas_call(
        state_forward_kernel,
        grid=(seq_count,),
        in_specs=[by_seq, pl.BlockSpec((rows, 8), lambda seq: (0, 0))],
        out_specs=by_seq,
        out_shape=jax.ShapeDtypeStruct(pre.shape, BF16),
        name="state_forward",
    )(pre, taps)


def state_backward(back, pre, taps, seq_count):
    rows = pre.shape[0] // seq_count
    by_seq = pl.BlockSpec((rows, LEN), lambda seq: (seq, 0))
    fixed = pl.BlockSpec((rows, 8), lambda seq: (0, 0))
    return pl.pallas_call(
        state_backward_kernel,
        grid=(seq_count,),
        in_specs=[by_seq, by_seq, fixed],
        out_specs=[by_seq, fixed],
        out_shape=[
            jax.ShapeDtypeStruct(pre.shape, BF16),
            jax.ShapeDtypeStruct((rows, 8), F32),
        ],
        name="state_backward",
    )(back, pre, taps)


def adam_step(weight, first, second, grad, rate, decay):
    first = BETA_ONE * first + (1.0 - BETA_ONE) * grad
    second = BETA_TWO * second + (1.0 - BETA_TWO) * grad * grad
    update = first / (1.0 - BETA_ONE**STEP) / (jnp.sqrt(second / (1.0 - BETA_TWO**STEP)) + ADAM_EPS)
    return (weight - rate * (update + decay * weight), first, second)


def after(value, *others):
    return lax.optimization_barrier((value, *others))[0]


def after_all(values, *others):
    values = tuple(values)
    return lax.optimization_barrier(values + others)[: len(values)]


def tour_dp():
    count = lax.axis_size("dp")
    order = [*range(0, count, 2), *range(count - 1, 0, -2)]
    forth = [(order[i], order[(i + 1) % count]) for i in range(count)]
    back = [(target, source) for source, target in forth]

    def group_at(ahead):
        group = lax.axis_index("dp")
        half = group // 2
        spot = jnp.where(lax.rem(group, 2) == 0, half, count - 1 - half)
        spot = lax.rem(spot + ahead + count, count)
        return jnp.where(spot < count // 2, 2 * spot, 2 * (count - 1 - spot) + 1)

    return forth, back, group_at, count // 2


def with_all(pair, *others):
    there = list(after_all(present(pair), *others))
    return tuple(None if part is None else there.pop(0) for part in pair)


def present(pair):
    return [part for part in pair if part is not None]


def gather_step(blocks, step, far_right):
    forth, back, _, far = tour_dp()
    right, left = blocks
    return (
        lax.ppermute(right, "dp", forth) if step < far or far_right else None,
        lax.ppermute(left, "dp", back) if step < far or not far_right else None,
    )


def place_kernel(starts, widths, *refs):
    blocks, refs = refs[: len(starts)], refs[len(starts) :]
    outs, sem = refs[: len(widths)], refs[len(widths)]
    copies = []
    for index, (ref, start) in enumerate(zip(blocks, starts)):
        start = pl.multiple_of(start(), 16)
        column = 0
        for out_index, (out, width) in enumerate(zip(outs, widths)):
            copies.append(
                pltpu.make_async_copy(
                    ref.at[:, column : column + width],
                    out.at[pl.ds(start, ref.shape[0]), :],
                    sem.at[index, out_index],
                )
            )
            column += width
    for copy in copies:
        copy.start()
    for copy in copies:
        copy.wait()


def place_rows(blocks, starts, widths):
    rows = sum(block.shape[0] for block in blocks)
    return pl.pallas_call(
        functools.partial(place_kernel, starts, widths),
        in_specs=[pl.BlockSpec(memory_space=pltpu.HBM)] * len(blocks),
        out_specs=[pl.BlockSpec(memory_space=pltpu.VMEM)] * len(widths),
        out_shape=[jax.ShapeDtypeStruct((rows, width), blocks[0].dtype) for width in widths],
        scratch_shapes=[pltpu.SemaphoreType.DMA((len(blocks), len(widths)))],
        compiler_params=pltpu.CompilerParams(vmem_limit_bytes=32 * 1024 * 1024),
        name="place_rows",
    )(*blocks)


def place_blocks(own, steps, widths):
    _, _, group_at, _ = tour_dp()
    count = lax.axis_size("dp")
    rows = own.shape[0]

    def start(ahead):
        return lambda: group_at(ahead) * rows

    blocks, starts = [own], [start(0)]
    for step, (right, left) in enumerate(steps, 1):
        if right is not None:
            blocks.append(right)
            starts.append(start(count - step))
        if left is not None:
            blocks.append(left)
            starts.append(start(step))
    return place_rows(blocks, starts, widths)


def scatter_block(parts, ahead):
    _, _, group_at, _ = tour_dp()
    rows = parts[0].shape[0] // lax.axis_size("dp")
    blocks = [lax.dynamic_slice_in_dim(part, group_at(ahead) * rows, rows, 0) for part in parts]
    return blocks[0] if len(blocks) == 1 else jnp.concatenate(blocks, axis=1)


def scatter_start(parts, far_right):
    _, _, _, far = tour_dp()
    block = scatter_block(parts, far)
    return (block, None) if far_right else (None, block)


def scatter_move(sums):
    forth, back, _, _ = tour_dp()
    right, left = sums
    return (
        None if right is None else lax.ppermute(right, "dp", forth),
        None if left is None else lax.ppermute(left, "dp", back),
    )


def scatter_step(parts, sums, distance):
    count = lax.axis_size("dp")

    def add(ahead, arrived):
        block = scatter_block(parts, ahead)
        if arrived is None:
            return block
        return (block.astype(F32) + arrived.astype(F32)).astype(BF16)

    return lax.optimization_barrier((add(distance, sums[0]), add(count - distance, sums[1])))


def scatter_end(parts, sums):
    own = scatter_block(parts, 0).astype(F32)
    for arrived in sums:
        own = own + arrived.astype(F32)
    return own


def gather_tensor_blocks(values):
    count = lax.axis_size("tensor")
    blocks = {0: values}
    step = count // 2
    while step:
        swap = [(i, i ^ step) for i in range(count)]
        blocks.update(
            {bits | step: lax.ppermute(block, "tensor", swap) for bits, block in blocks.items()}
        )
        step //= 2
    return blocks


def join_tensor(blocks):
    rows, width = blocks[0].shape

    def start(bits):
        return lambda: (lax.axis_index("tensor") ^ bits) * rows

    return place_rows(list(blocks.values()), [start(bits) for bits in blocks], [width])[0]


def scatter_tensor_split(values, step):
    side = (lax.axis_index("tensor") // step) % 2
    values = values.reshape(-1, 2, *values.shape[1:])
    kept = lax.dynamic_index_in_dim(values, side, 1, keepdims=False)
    return kept, lax.dynamic_index_in_dim(values, 1 - side, 1, keepdims=False).astype(BF16)


def scatter_tensor_move(given, step):
    count = lax.axis_size("tensor")
    return lax.ppermute(given, "tensor", [(i, i ^ step) for i in range(count)])


def scatter_tensor_step(values, step):
    kept, given = scatter_tensor_split(values, step)
    return kept.astype(F32) + scatter_tensor_move(given, step).astype(F32)


def scatter_tensor(values):
    step = 1
    while step < lax.axis_size("tensor"):
        values = scatter_tensor_step(values, step)
        step *= 2
    return values[0]


def sum_over(values, axes):
    for axis in axes:
        count = lax.axis_size(axis)
        step = 1
        while step < count:
            pairs = [(place, place ^ step) for place in range(count)]
            values = values + lax.ppermute(values, axis, pairs)
            step *= 2
    return values


def deal_out(values):
    count = lax.axis_size("dp")
    own_rows, width = values.shape
    pieces = values.reshape(count, own_rows // count, width)
    return lax.all_to_all(pieces, "dp", split_axis=0, concat_axis=0, tiled=True)


def deal_in(pieces):
    arrived = lax.all_to_all(pieces, "dp", split_axis=0, concat_axis=0, tiled=True)
    return arrived.reshape(-1, arrived.shape[-1])


def shards(
    tokens,
    cotangent,
    lengths,
    order,
    in_weight,
    in_first,
    in_second,
    out_weight,
    out_first,
    out_second,
    conv_weight,
    conv_first,
    conv_second,
    gain_vector,
    gain_first,
    gain_second,
    head_params,
    head_first,
    head_second,
):
    count_dp = lax.axis_size("dp")
    count_tensor = lax.axis_size("tensor")
    group = lax.axis_index("dp")
    place = lax.axis_index("tensor")
    own_rows, width = tokens.shape
    token_rows = own_rows * count_tensor
    seq_count = token_rows // LEN
    seq_total = order.shape[0]
    head_count = head_params.shape[0]
    padded_heads = -(-head_count // 8) * 8
    inner_cols = head_count * HEAD_DIM
    conv_rows = conv_weight.shape[0]
    state_cols = conv_rows - inner_cols
    inner_total = inner_cols * count_tensor
    norm_gain = gain_vector[:width]
    gate_gain = lax.dynamic_slice_in_dim(gain_vector, width + place * inner_cols, inner_cols, 0)
    gate_gain = gate_gain.reshape(1, inner_cols)

    positions = jnp.arange(seq_total)
    inverse = jnp.sum(
        jnp.where(order[:, None] == positions[None, :], positions[:, None], 0), axis=0
    )
    own_seq = (place * own_rows) // LEN
    sources = inverse[jnp.arange(count_dp) * seq_count + own_seq] // seq_count
    seq_lengths = lax.dynamic_slice_in_dim(lengths, group * seq_count, seq_count, 0)
    live_all = (
        (jnp.arange(LEN)[None, :] < seq_lengths[:, None]).astype(F32).reshape(token_rows, 1)
    )
    live_own = lax.dynamic_slice_in_dim(live_all, place * own_rows, own_rows, 0)

    own = tokens.astype(F32)
    inv_own = lax.rsqrt(jnp.mean(own * own, axis=1, keepdims=True) + EPS_NORM)
    normed_own = (own * inv_own * norm_gain).astype(BF16)
    side_cols = 128
    far = count_dp // 2
    in_low = in_weight.astype(BF16)
    side_real = in_low.shape[1] - 2 * inner_cols
    mixed_shard = jnp.pad(in_low[:, inner_cols:], ((0, 0), (0, side_cols - side_real)))
    late_shard = jnp.concatenate([in_low[:, :inner_cols], out_weight.astype(BF16).T], axis=1)
    normed_blocks = gather_tensor_blocks(normed_own)
    first_bit = count_tensor // 2
    chan = jnp.concatenate(
        [
            conv_weight[:inner_cols].T,
            jnp.repeat(head_params[:, 2], HEAD_DIM)[None, :],
            jnp.zeros((2, inner_cols), F32),
        ],
        axis=0,
    )
    rate = -jnp.exp(head_params[:, 1])
    heads = jnp.pad(
        jnp.stack([head_params[:, 0], rate], axis=1),
        ((0, padded_heads - head_count), (0, 126)),
    )
    state_taps = jnp.pad(conv_weight[inner_cols:], ((0, 0), (0, 3)))
    prepared = (chan, heads, state_taps, gate_gain, live_own)
    mixed_steps = []
    late_steps = []
    moving = (mixed_shard, mixed_shard)
    late_moving = (late_shard, late_shard)
    for step in range(1, far + 1):
        if step == far:
            moving = after_all(moving, normed_blocks[first_bit], *prepared)
        moving = gather_step(moving, step, True)
        mixed_steps.append(moving)
        if step == 1:
            cot_first = deal_out(after(cotangent, *moving))
            cot_chosen = cot_first.at[sources].get(mode="promise_in_bounds")
        if step == far - 2:
            late_moving = gather_step(after_all(late_moving, *moving), 1, False)
            late_steps.append(late_moving)
    late_moving = gather_step(after_all(late_moving, *mixed_steps[far - 2]), 2, False)
    late_steps.append(late_moving)
    cot_own = deal_in(cot_chosen)
    back_out_own = (cot_own.astype(F32) * live_own).astype(BF16)
    back_out_blocks = gather_tensor_blocks(back_out_own)
    mixed_steps[-1] = with_all(mixed_steps[-1], cot_chosen, *late_moving)
    in_inner, in_side = place_blocks(mixed_shard, mixed_steps, [inner_cols, side_cols])
    normed = join_tensor(normed_blocks)

    side_pre = dot_general_tt(in_side, normed)
    for step in range(3, far):
        late_moving = gather_step(late_moving, step, False)
        late_steps.append(late_moving)
    inner_pre = dot_nn(after(normed, side_pre, *late_moving), in_inner)
    late_moving = gather_step(late_moving, far, False)
    late_steps.append(late_moving)
    state_pre = by_sequence(side_pre[:state_cols], seq_count)
    step_pre = by_sequence(side_pre[state_cols : state_cols + padded_heads], seq_count)
    state_own = state_forward(state_pre, state_taps, seq_count)
    states = join_tensor(gather_tensor_blocks(from_sequence(state_own, seq_count)))
    states = by_sequence(states, seq_count)

    inner_pre = after(inner_pre, back_out_own)
    scanned, conv, entry = scan_forward(inner_pre, states, step_pre, chan, heads, head_count)

    late_steps[-1] = with_all(late_moving, scanned)
    in_gate, out_low = place_blocks(late_shard, late_steps, [inner_cols, inner_cols])
    back_out = join_tensor(back_out_blocks)
    gate_pre = lax.optimization_barrier(dot_nn(normed, in_gate))
    gate_sigmoid = jax.nn.sigmoid(gate_pre)
    gate = gate_pre * gate_sigmoid
    mixed = lax.optimization_barrier(scanned * gate)
    back_normed = lax.optimization_barrier(dot_nn(back_out, out_low).astype(BF16)).astype(F32)
    row_sums = jnp.stack(
        [jnp.sum(mixed * mixed, axis=1), jnp.sum(back_normed * gate_gain * mixed, axis=1)]
    )
    row_sums = lax.psum(row_sums, "tensor")
    gate_inv = lax.rsqrt(row_sums[0] / inner_total + EPS_NORM)[:, None]
    gate_rows = row_sums[1][:, None]
    scaled = mixed * gate_inv
    normed_out = lax.optimization_barrier((scaled * gate_gain).astype(BF16))
    grad_gate_gain = jnp.sum(back_normed * scaled, axis=0)
    back_mixed = gate_inv * (back_normed * gate_gain) - mixed * (
        gate_inv**3 * (gate_rows / inner_total)
    )
    back_gate = (
        back_mixed * scanned * (gate_sigmoid * (1.0 + gate_pre * (1.0 - gate_sigmoid)))
    ).astype(BF16)
    early = lax.optimization_barrier(
        (dot_tn(normed, back_gate).astype(BF16), dot_tn(back_out, normed_out).astype(BF16))
    )
    early_sums = scatter_start(early, False)
    partial_out = lax.optimization_barrier(dot_nt(normed_out, out_low).astype(BF16))
    branch_kept, branch_given = scatter_tensor_split(
        partial_out.reshape(count_tensor, own_rows, width), 1
    )
    dy = back_mixed * gate
    dy = after(dy, branch_given)
    held = ()
    found = []
    back_parts = 2 if head_count % 4 == 0 else 1
    for part in range(back_parts):
        dy = after(dy, *present(early_sums), *held)
        result = scan_backward(
            dy, inner_pre, conv, states, step_pre, entry, chan, heads, head_count,
            part, back_parts, held,
        )
        held = (result[0], result[3])
        found.append((result[1].astype(F32), result[2], result[4]))
        early_sums = scatter_step(
            early, with_all(scatter_move(early_sums), result[1]), far - 1 - part
        )
    back_inner, dchan = held
    back_states, back_step, dhead = (sum(entries) for entries in zip(*found))
    inner_parts = [
        lax.optimization_barrier(
            dot_tn(normed, after(back_inner, *present(early_sums))).astype(BF16)
        )
    ]
    inner_sums = scatter_start(inner_parts, True)
    branch = after(scatter_tensor_move(branch_given, 1), *present(inner_sums))
    branch = branch_kept.astype(F32) + branch.astype(F32)
    step = 2
    while step < count_tensor:
        branch_kept, branch_given = scatter_tensor_split(branch, step)
        branch = branch_kept + scatter_tensor_move(branch_given, step).astype(F32)
        step *= 2
    for distance in range(far - 1, 0, -1):
        inner_sums = scatter_step(inner_parts, scatter_move(inner_sums), distance)
        if distance == far - 1:
            inner_second = inner_sums
        if distance <= far - 1 - back_parts:
            early_sums = scatter_step(early, scatter_move(early_sums), distance)
            inner_sums, early_sums = lax.optimization_barrier((inner_sums, early_sums))
    early_sums = scatter_move(early_sums)
    state_back = scatter_tensor(
        from_sequence(back_states, seq_count).reshape(count_tensor, state_cols, token_rows)
    )
    back_state_pre, dtaps_state = state_backward(
        by_sequence(after(state_back, *inner_second), seq_count), state_pre, state_taps, seq_count
    )
    back_step = from_sequence(back_step, seq_count)[:head_count].astype(BF16)
    back_side = jnp.concatenate(
        [
            from_sequence(back_state_pre, seq_count),
            back_step,
            jnp.zeros((side_cols - side_real, token_rows), BF16),
        ],
        axis=0,
    )
    grad_side = dot_general_tt(normed, back_side).astype(BF16).reshape(count_dp, -1, side_cols)
    grad_side = lax.all_to_all(grad_side, "dp", split_axis=0, concat_axis=0, tiled=True)
    grad_side = jnp.sum(grad_side.astype(F32), axis=0)[:, :side_real]
    grad_inner = scatter_end(inner_parts, scatter_move(inner_sums))
    grad_early = scatter_end(early, early_sums)
    grad_out = grad_early[:, inner_cols:].T
    grad_in = jnp.concatenate([grad_early[:, :inner_cols], grad_inner, grad_side], axis=1)
    back_input = (
        lax.optimization_barrier(
            dot_nt(after(back_gate, branch_given), in_gate)
            + dot_nt(after(back_inner, branch_given), in_inner)
        )
        + dot_general_tt(back_side, in_side)
    ).astype(BF16)
    back_part = scatter_tensor_step(back_input.reshape(count_tensor, own_rows, width), 1)
    step = 2
    while step < count_tensor:
        back_part = scatter_tensor_step(back_part, step)
        step *= 2
    back_part = back_part[0]
    row_term = jnp.sum(back_part * norm_gain * own, axis=1, keepdims=True)
    back_own = inv_own * norm_gain * back_part - own * inv_own**3 * (row_term / width)
    input_grad = (live_own * cot_own.astype(F32) + back_own).astype(BF16)
    grad_norm_gain = jnp.sum(back_part * own * inv_own, axis=0)

    branch = branch[0]
    layer_output = (live_own * (own + branch)).astype(BF16)

    grad_heads = jnp.stack(
        [
            dhead[:head_count, 0],
            dhead[:head_count, 1],
            jnp.sum(dchan[5].reshape(head_count, HEAD_DIM), axis=1),
        ],
        axis=1,
    )
    grad_taps_state = dtaps_state[:, :5]
    own_side = jnp.concatenate(
        [
            dchan[:5].reshape(-1),
            grad_taps_state.reshape(-1),
            grad_heads.reshape(-1),
            grad_gate_gain,
        ]
    )
    side_size = own_side.shape[0]
    squares = jnp.sum(grad_in * grad_in) + jnp.sum(grad_out * grad_out)
    shared = jnp.concatenate(
        [
            lax.dynamic_update_slice_in_dim(
                jnp.zeros((count_tensor * side_size,), F32), own_side, place * side_size, 0
            ),
            grad_norm_gain,
            squares[None],
        ]
    )
    shared = sum_over(shared, ("tensor", "dp"))
    sides = shared[: count_tensor * side_size]
    grad_norm_all = shared[count_tensor * side_size : -1]
    grad_norm = jnp.sqrt(
        shared[-1] + jnp.sum(sides * sides) + jnp.sum(grad_norm_all * grad_norm_all)
    )
    side_sum = lax.dynamic_slice_in_dim(sides, place * side_size, side_size, 0)
    grad_conv = jnp.concatenate(
        [
            side_sum[: 5 * inner_cols].reshape(5, inner_cols).T,
            side_sum[5 * inner_cols : 5 * conv_rows].reshape(state_cols, 5),
        ],
        axis=0,
    )
    heads_end = 5 * conv_rows + 3 * head_count
    grad_head = side_sum[5 * conv_rows : heads_end].reshape(head_count, 3)
    grad_gate_all = sides.reshape(count_tensor, side_size)[:, heads_end:].reshape(-1)
    grad_gains = jnp.concatenate([grad_norm_all, grad_gate_all])
    factor = CLIP_NORM / jnp.maximum(grad_norm, CLIP_NORM)
    new_in = adam_step(in_weight, in_first, in_second, factor * grad_in, RATE_MATRIX, DECAY)
    new_out = adam_step(out_weight, out_first, out_second, factor * grad_out, RATE_MATRIX, DECAY)
    new_conv = adam_step(conv_weight, conv_first, conv_second, factor * grad_conv, RATE_VECTOR, 0.0)
    new_gain = adam_step(
        gain_vector, gain_first, gain_second, factor * grad_gains, RATE_VECTOR, 0.0
    )
    new_head = adam_step(head_params, head_first, head_second, factor * grad_head, RATE_VECTOR, 0.0)
    return (
        layer_output,
        input_grad,
        grad_norm,
        *new_in,
        *new_out,
        *new_conv,
        *new_gain,
        *new_head,
        new_in[0].astype(BF16),
        new_out[0].astype(BF16),
    )


def solution(mesh):
    rows = P(("dp", "tensor"), None)
    in_matrix = P("dp", "tensor")
    out_matrix = P("tensor", "dp")
    by_tensor = P("tensor", None)
    same = P()
    in_specs = (
        (rows, rows, same, same)
        + (in_matrix,) * 3
        + (out_matrix,) * 3
        + (by_tensor,) * 3
        + (same,) * 3
        + (by_tensor,) * 3
    )
    out_specs = (
        (rows, rows, same)
        + (in_matrix,) * 3
        + (out_matrix,) * 3
        + (by_tensor,) * 3
        + (same,) * 3
        + (by_tensor,) * 3
        + (in_matrix, out_matrix)
    )
    return jax.shard_map(shards, mesh=mesh, in_specs=in_specs, out_specs=out_specs, check_vma=False)
```

```python
import functools

import jax
import jax.numpy as jnp
from jax import lax
from jax.experimental import pallas as pl
from jax.experimental.pallas import tpu as pltpu
from jax.sharding import PartitionSpec as P

HEAD_DIM = 64
STATE = 128
LEN = 1024
STEP = 5
CHUNK = 128
PAIR = 2 * HEAD_DIM

EPS_NORM = 1e-05
BETA_ONE = 0.5
BETA_TWO = 0.5
ADAM_EPS = 1e-08
DECAY = 0.1
RATE_MATRIX = 0.02
RATE_VECTOR = 0.8
CLIP_NORM = 1.0
HIGHEST_PRECISION = lax.Precision.HIGHEST
MASKED = -1e30
BF16 = jnp.bfloat16
F32 = jnp.float32


def sigmoid(values):
    return 1.0 / (1.0 + jnp.exp(-values))


def softplus(values):
    return jnp.maximum(values, 0.0) + jnp.log1p(jnp.exp(-jnp.abs(values)))


def vmem_limit(mebibytes):
    return pltpu.CompilerParams(vmem_limit_bytes=mebibytes * 1024 * 1024)


def in_hbm(values):
    return pltpu.with_memory_space_constraint(values, pltpu.HBM)


def weight(microseconds):
    return pl.CostEstimate(flops=microseconds * 10**9, bytes_accessed=0, transcendentals=0)


def dot_nn(left, right):
    return lax.dot_general(left, right, (((1,), (0,)), ((), ())), preferred_element_type=F32)


def dot_nt(left, right):
    return lax.dot_general(left, right, (((1,), (1,)), ((), ())), preferred_element_type=F32)


def dot_tn(left, right):
    return lax.dot_general(left, right, (((0,), (0,)), ((), ())), preferred_element_type=F32)


def dot_general_tt(left, right):
    return lax.dot_general(left, right, (((0,), (1,)), ((), ())), preferred_element_type=F32)


def by_sequence(values, seq_count):
    if seq_count == 1:
        return values
    rows = values.shape[0]
    return jnp.swapaxes(values.reshape(rows, seq_count, LEN), 0, 1).reshape(-1, LEN)


def from_sequence(values, seq_count):
    if seq_count == 1:
        return values
    rows = values.shape[0] // seq_count
    return jnp.swapaxes(values.reshape(seq_count, rows, LEN), 0, 1).reshape(rows, -1)


def dot_exact(left, right):
    high = left.astype(BF16)
    rest = left - high.astype(F32)
    middle = rest.astype(BF16)
    low = (rest - middle.astype(F32)).astype(BF16)
    rows = left.shape[0]
    product = dot_nn(jnp.concatenate([high, middle, low], axis=0), right)
    return product[:rows] + product[rows : 2 * rows] + product[2 * rows :]


def square_places():
    row = lax.broadcasted_iota(jnp.int32, (CHUNK, CHUNK), 0)
    column = lax.broadcasted_iota(jnp.int32, (CHUNK, CHUNK), 1)
    return row, column


def chunk_logs(step_ref, head_ref):
    biased = step_ref[...] + head_ref[:, 0:1]
    step = softplus(biased)
    row, column = square_places()
    upto = jnp.where(row <= column, 1.0, 0.0).astype(BF16)
    logs = dot_exact(step * head_ref[:, 1:2], upto)
    padding = jnp.zeros((CHUNK - step.shape[0], CHUNK), F32)
    step_rows = jnp.transpose(jnp.concatenate([step, padding], axis=0))
    logs_rows = jnp.transpose(jnp.concatenate([logs, padding], axis=0))
    return biased, step, logs, step_rows, logs_rows


def spread(columns, head):
    return jnp.broadcast_to(columns[:, head : head + 1], (CHUNK, CHUNK))


def scan_forward_kernel(
    head_count, x_ref, bc_ref, step_ref, chan_ref, head_ref, y_ref, xc_ref, entry_ref, rows, state, fresh
):
    @pl.when(pl.program_id(1) == 0)
    def _():
        state[...] = jnp.zeros_like(state)
        rows[0:8, :] = jnp.zeros((8, rows.shape[1]), F32)

    rows[8 : 8 + CHUNK, :] = x_ref[...].astype(F32)
    entry_ref[0, 0] = state[...].astype(BF16)
    _, _, logs, step_rows, logs_rows = chunk_logs(step_ref, head_ref)
    in_columns = bc_ref[:STATE, :]
    state_out = jnp.transpose(bc_ref[STATE:, :])
    scores = dot_nn(state_out, in_columns)
    row, column = square_places()
    first_half = column < HEAD_DIM
    later = row >= column
    for pair in range(head_count // 2):
        lanes = slice(pair * PAIR, (pair + 1) * PAIR)
        conv = chan_ref[4:5, lanes]
        for tap in range(4):
            conv = conv + chan_ref[tap : tap + 1, lanes] * rows[5 + tap : 5 + tap + CHUNK, lanes]
        xc_ref[:, lanes] = conv.astype(BF16)
        values = conv * sigmoid(conv)
        even, odd = 2 * pair, 2 * pair + 1
        step_pair = jnp.where(first_half, spread(step_rows, even), spread(step_rows, odd))
        logs_even, logs_odd = spread(logs_rows, even), spread(logs_rows, odd)
        logs_pair = jnp.where(first_half, logs_even, logs_odd)
        within_even = jnp.exp(jnp.where(later, logs_even - logs[even : even + 1, :], MASKED))
        within_odd = jnp.exp(jnp.where(later, logs_odd - logs[odd : odd + 1, :], MASKED))
        mixing = jnp.concatenate(
            [(scores * within_even).astype(BF16), (scores * within_odd).astype(BF16)], axis=1
        )
        weighted = step_pair * values
        zero = jnp.zeros_like(weighted)
        stacked = jnp.concatenate(
            [
                jnp.where(first_half, weighted, zero).astype(BF16),
                jnp.where(first_half, zero, weighted).astype(BF16),
            ],
            axis=0,
        )
        inner = dot_nn(mixing, stacked)
        outer = dot_nn(state_out, entry_ref[0, 0, :, lanes]) * jnp.exp(logs_pair)
        y_ref[:, lanes] = (inner + outer + chan_ref[5:6, lanes] * values).astype(BF16)
        last = logs_pair[CHUNK - 1 : CHUNK, :]
        fresh[:, lanes] = (jnp.exp(last - logs_pair) * weighted).astype(BF16)
        state[:, lanes] = jnp.exp(last) * state[:, lanes]
    state[...] += dot_nn(in_columns, fresh[...])
    rows[0:8, :] = rows[CHUNK : CHUNK + 8, :]


def scan_backward_kernel(
    first_head,
    head_count,
    dy_ref,
    x_ref,
    xc_ref,
    bc_ref,
    step_ref,
    entry_ref,
    chan_ref,
    head_ref,
    *outputs_and_scratch,
):
    (
    dx_ref,
    dbc_ref,
    dstep_ref,
    dchan_ref,
    dhead_ref,
    rows,
    back,
    leaving,
    arriving,
    sums_one,
    sums_two,
    sums_three,
    crossings,
    decays,
    ) = outputs_and_scratch[-14:]
    sums_before = outputs_and_scratch[2:-14]

    @pl.when(pl.program_id(1) == 0)
    def _():
        back[...] = jnp.zeros_like(back)
        rows[CHUNK : CHUNK + 8, :] = jnp.zeros((8, rows.shape[1]), F32)

    @pl.when((pl.program_id(0) == 0) & (pl.program_id(1) == 0))
    def _():
        dchan_ref[...] = jnp.zeros_like(dchan_ref)
        dhead_ref[...] = sums_before[2][...] if sums_before else jnp.zeros_like(dhead_ref)

    padded = step_ref.shape[0]
    biased, step, logs, step_rows, logs_rows = chunk_logs(step_ref, head_ref)
    in_columns = bc_ref[:STATE, :]
    out_columns = bc_ref[STATE:, :]
    state_in = jnp.transpose(in_columns)
    state_out = jnp.transpose(out_columns)
    scores = dot_nn(state_in, out_columns)
    back_low = back[...].astype(BF16)
    entry = entry_ref[0, 0]
    row, column = square_places()
    first_half = column < HEAD_DIM
    later = column >= row
    head_row = lax.broadcasted_iota(jnp.int32, (padded, CHUNK), 0)
    wide_row = lax.broadcasted_iota(jnp.int32, (head_count * CHUNK, CHUNK), 0) // CHUNK
    wide_column = lax.broadcasted_iota(jnp.int32, (head_count * CHUNK, CHUNK), 1)
    total = jnp.zeros((CHUNK, CHUNK), F32)
    over_rows = jnp.zeros((padded, CHUNK), F32)
    for pair in range(head_count // 2):
        lanes = slice(pair * PAIR, (pair + 1) * PAIR)
        even = first_head + 2 * pair
        odd = even + 1
        conv = xc_ref[:, lanes].astype(F32)
        gate = sigmoid(conv)
        values = conv * gate
        dy_low = dy_ref[:, lanes]
        dy = dy_low.astype(F32)
        step_pair = jnp.where(first_half, spread(step_rows, even), spread(step_rows, odd))
        logs_even, logs_odd = spread(logs_rows, even), spread(logs_rows, odd)
        logs_pair = jnp.where(first_half, logs_even, logs_odd)
        weighted = step_pair * values
        zero = jnp.zeros_like(weighted)
        dy_stacked = jnp.concatenate(
            [
                jnp.where(first_half, dy, zero).astype(BF16),
                jnp.where(first_half, zero, dy).astype(BF16),
            ],
            axis=0,
        )
        transfers = []
        for head, log_column, part in (
            (even, logs_even, jnp.where(first_half, weighted, zero).astype(BF16)),
            (odd, logs_odd, jnp.where(first_half, zero, weighted).astype(BF16)),
        ):
            within = jnp.exp(jnp.where(later, logs[head : head + 1, :] - log_column, MASKED))
            product = within * dot_nt(part, dy_low)
            total = total + product
            crossing = (scores * product).astype(BF16)
            local = head - first_head
            crossings[:, local * CHUNK : (local + 1) * CHUNK] = crossing
            sums = jnp.sum(crossing.astype(F32), axis=0, keepdims=True)
            over_rows = jnp.where(head_row == head, sums, over_rows)
            transfers.append((scores * within).astype(BF16))
        grown = jnp.exp(logs_pair)
        last = logs_pair[CHUNK - 1 : CHUNK, :]
        decays[0:1, lanes] = jnp.exp(last)
        to_end = jnp.exp(last - logs_pair)
        from_end = to_end * dot_nn(state_in, back_low[:, lanes])
        dweighted = dot_nn(jnp.concatenate(transfers, axis=1), dy_stacked) + from_end
        grown_dy = grown * dy
        leaving[:, lanes] = grown_dy.astype(BF16)
        arriving[:, lanes] = (to_end * weighted).astype(BF16)
        sums_one[:, lanes] = (grown_dy * dot_nn(state_out, entry[:, lanes])).astype(BF16)
        sums_two[:, lanes] = (weighted * from_end).astype(BF16)
        sums_three[:, lanes] = (values * dweighted).astype(BF16)
        dvalues = step_pair * dweighted + chan_ref[5:6, lanes] * dy
        dconv = dvalues * (gate * (1.0 + conv * (1.0 - gate)))
        rows[0:CHUNK, lanes] = dconv
        dchan_ref[5:6, lanes] += jnp.sum(dy * values, axis=0, keepdims=True)
        dchan_ref[4:5, lanes] += jnp.sum(dconv, axis=0, keepdims=True)
        raw = x_ref[:, lanes].astype(F32)
        dx = jnp.zeros((CHUNK, PAIR), F32)
        for tap in range(4):
            shifted = rows[3 - tap : 3 - tap + CHUNK, lanes]
            dx = dx + chan_ref[tap : tap + 1, lanes] * shifted
            dchan_ref[tap : tap + 1, lanes] += jnp.sum(raw * shifted, axis=0, keepdims=True)
        dx_ref[:, lanes] = dx.astype(BF16)
    rows[CHUNK : CHUNK + 8, :] = rows[0:8, :]
    total_low = total.astype(BF16)
    dstate_in = dot_nt(out_columns, total_low) + dot_nt(back_low, arriving[...])
    dstate_out = dot_nn(in_columns, total_low) + dot_nt(entry, leaving[...])
    if sums_before:
        dstate_in = dstate_in + sums_before[0][:STATE, :].astype(F32)
        dstate_out = dstate_out + sums_before[0][STATE:, :].astype(F32)
    dbc_ref[:STATE, :] = dstate_in.astype(BF16)
    dbc_ref[STATE:, :] = dstate_out.astype(BF16)
    channels = back.shape[1]
    owner = first_head + lax.broadcasted_iota(jnp.int32, (padded, channels), 1) // HEAD_DIM
    member = owner == lax.broadcasted_iota(jnp.int32, (padded, channels), 0)
    member = jnp.where(member, 1.0, 0.0).astype(BF16)
    from_entry = dot_nt(member, sums_one[...])
    to_exit = dot_nt(member, sums_two[...])
    step_direct = dot_nt(member, sums_three[...])
    decayed = decays[0:1, :] * back[...]
    carried = jnp.sum(decayed * entry.astype(F32), axis=0, keepdims=True)
    carried = jnp.broadcast_to(carried, (CHUNK, channels)).astype(BF16)
    carried = dot_nt(member, carried)
    back[...] = decayed + dot_nn(out_columns, leaving[...])
    pick = jnp.where(wide_row + first_head == wide_column, 1.0, 0.0).astype(BF16)
    over_columns = jnp.transpose(dot_nn(crossings[...], pick))[:padded]
    onward = jnp.where(row >= column, 1.0, 0.0).astype(BF16)
    before = jnp.where(row < column, 1.0, 0.0).astype(BF16)
    dlogs = dot_exact(
        jnp.concatenate([over_rows - over_columns + from_entry, to_exit], axis=1),
        jnp.concatenate([onward, before], axis=0),
    )
    dlogs = dlogs + carried
    rate = head_ref[:, 1:2]
    dstep = (rate * dlogs + step_direct) * sigmoid(biased)
    dstep_ref[...] = dstep + sums_before[1][...] if sums_before else dstep
    dhead_ref[:, 0:1] += jnp.sum(dstep, axis=1, keepdims=True)
    dhead_ref[:, 1:2] += rate * jnp.sum(step * dlogs, axis=1, keepdims=True)


def chunk_specs(seq_count, channels, padded, reverse):
    chunks = LEN // CHUNK

    def place(seq, chunk):
        return chunks - 1 - chunk if reverse else chunk

    def by_rows(width):
        return pl.BlockSpec(
            (CHUNK, width), lambda seq, chunk: (seq * chunks + place(seq, chunk), 0)
        )

    step_spec = pl.BlockSpec((padded, CHUNK), lambda seq, chunk: (seq, place(seq, chunk)))
    entry_spec = pl.BlockSpec(
        (1, 1, STATE, channels), lambda seq, chunk: (seq, place(seq, chunk), 0, 0)
    )

    def fixed(*shape):
        return pl.BlockSpec(shape, lambda seq, chunk: (0, 0))

    state_spec = pl.BlockSpec((2 * STATE, CHUNK), lambda seq, chunk: (seq, place(seq, chunk)))
    return (seq_count, chunks), by_rows, step_spec, state_spec, entry_spec, fixed


def scan_forward(x_pre, states, step_pre, chan, heads, head_count):
    token_rows, channels = x_pre.shape
    padded = heads.shape[0]
    seq_count = token_rows // LEN
    grid, by_rows, step_spec, state_spec, entry_spec, fixed = chunk_specs(seq_count, channels, padded, False)
    return pl.pallas_call(
        functools.partial(scan_forward_kernel, head_count),
        grid=grid,
        in_specs=[
            by_rows(channels),
            state_spec,
            step_spec,
            fixed(8, channels),
            fixed(padded, 128),
        ],
        out_specs=[by_rows(channels), by_rows(channels), entry_spec],
        out_shape=[
            jax.ShapeDtypeStruct((token_rows, channels), BF16),
            jax.ShapeDtypeStruct((token_rows, channels), BF16),
            jax.ShapeDtypeStruct((seq_count, LEN // CHUNK, STATE, channels), BF16),
        ],
        scratch_shapes=[
            pltpu.VMEM((CHUNK + 8, channels), F32),
            pltpu.VMEM((STATE, channels), F32),
            pltpu.VMEM((CHUNK, channels), BF16),
        ],
        compiler_params=vmem_limit(16),
        cost_estimate=weight(11),
        name="scan_forward",
    )(x_pre, states, step_pre, chan, heads)


def scan_backward(dy, x_pre, conv, states, step_pre, entry, chan, heads, head_count, part, parts, held):
    token_rows, channels = x_pre.shape
    padded = heads.shape[0]
    seq_count = token_rows // LEN
    part_heads = head_count // parts
    width = channels // parts
    chunks = LEN // CHUNK

    def by_rows(seq, chunk):
        return seq * chunks + chunks - 1 - chunk, part

    wide = pl.BlockSpec((CHUNK, width), by_rows)
    step_spec = pl.BlockSpec((padded, CHUNK), lambda seq, chunk: (seq, chunks - 1 - chunk))
    state_spec = pl.BlockSpec((2 * STATE, CHUNK), lambda seq, chunk: (seq, chunks - 1 - chunk))
    entry_spec = pl.BlockSpec(
        (1, 1, STATE, width), lambda seq, chunk: (seq, chunks - 1 - chunk, 0, part)
    )
    chan_spec = pl.BlockSpec((8, width), lambda seq, chunk: (0, part))
    head_spec = pl.BlockSpec((padded, 128), lambda seq, chunk: (0, 0))
    low_rows = pltpu.VMEM((CHUNK, width), BF16)
    in_specs = [wide, wide, wide, state_spec, step_spec, entry_spec, chan_spec, head_spec]
    in_place = {}
    if held:
        in_place = {len(in_specs): 0, len(in_specs) + 1: 3}
        dx, dbc, dstep, dchan, dhead = held
        held = (dx, dchan, dbc, dstep, dhead)
        in_specs = in_specs + [pl.BlockSpec(memory_space=pl.ANY)] * 2
        in_specs = in_specs + [state_spec, step_spec, head_spec]
    return pl.pallas_call(
        functools.partial(scan_backward_kernel, part * part_heads, part_heads),
        grid=(seq_count, chunks),
        in_specs=in_specs,
        out_specs=[wide, state_spec, step_spec, chan_spec, head_spec],
        out_shape=[
            jax.ShapeDtypeStruct((token_rows, channels), BF16),
            jax.ShapeDtypeStruct((seq_count * 2 * STATE, LEN), BF16),
            jax.ShapeDtypeStruct((seq_count * padded, LEN), F32),
            jax.ShapeDtypeStruct((8, channels), F32),
            jax.ShapeDtypeStruct((padded, 128), F32),
        ],
        scratch_shapes=[
            pltpu.VMEM((CHUNK + 8, width), F32),
            pltpu.VMEM((STATE, width), F32),
            low_rows,
            low_rows,
            low_rows,
            low_rows,
            low_rows,
            pltpu.VMEM((CHUNK, part_heads * CHUNK), BF16),
            pltpu.VMEM((8, width), F32),
        ],
        input_output_aliases=in_place,
        compiler_params=vmem_limit(16),
        cost_estimate=weight(20),
        name="scan_backward",
    )(dy, x_pre, conv, states, step_pre, entry, chan, heads, *held)


def lane_shift(values, amount):
    if amount == 0:
        return values
    lane = lax.broadcasted_iota(jnp.int32, values.shape, 1)
    if amount > 0:
        return jnp.where(lane >= amount, pltpu.roll(values, amount, 1), 0.0)
    return jnp.where(lane < LEN + amount, pltpu.roll(values, LEN + amount, 1), 0.0)


def state_conv(pre, taps_ref):
    conv = jnp.broadcast_to(taps_ref[:, 4:5], pre.shape)
    for tap in range(4):
        conv = conv + taps_ref[:, tap : tap + 1] * lane_shift(pre, 3 - tap)
    return conv


def state_forward_kernel(pre_ref, taps_ref, states_ref):
    conv = state_conv(pre_ref[...], taps_ref)
    states_ref[...] = (conv * sigmoid(conv)).astype(BF16)


def state_backward_kernel(back_ref, pre_ref, taps_ref, dpre_ref, dtaps_ref):
    @pl.when(pl.program_id(0) == 0)
    def _():
        dtaps_ref[...] = jnp.zeros_like(dtaps_ref)

    pre = pre_ref[...]
    conv = state_conv(pre, taps_ref)
    gate = sigmoid(conv)
    dconv = back_ref[...] * (gate * (1.0 + conv * (1.0 - gate)))
    dpre = jnp.zeros_like(pre)
    for tap in range(4):
        shifted = lane_shift(dconv, tap - 3)
        dpre = dpre + taps_ref[:, tap : tap + 1] * shifted
        dtaps_ref[:, tap : tap + 1] += jnp.sum(pre * shifted, axis=1, keepdims=True)
    dtaps_ref[:, 4:5] += jnp.sum(dconv, axis=1, keepdims=True)
    dpre_ref[...] = dpre.astype(BF16)


def state_forward(pre, taps, seq_count):
    rows = pre.shape[0] // seq_count
    by_seq = pl.BlockSpec((rows, LEN), lambda seq: (seq, 0))
    return pl.pallas_call(
        state_forward_kernel,
        grid=(seq_count,),
        in_specs=[by_seq, pl.BlockSpec((rows, 8), lambda seq: (0, 0))],
        out_specs=by_seq,
        out_shape=jax.ShapeDtypeStruct(pre.shape, BF16),
        compiler_params=vmem_limit(8),
        name="state_forward",
    )(pre, taps)


def state_backward(back, pre, taps, seq_count):
    rows = pre.shape[0] // seq_count
    by_seq = pl.BlockSpec((rows, LEN), lambda seq: (seq, 0))
    fixed = pl.BlockSpec((rows, 8), lambda seq: (0, 0))
    return pl.pallas_call(
        state_backward_kernel,
        grid=(seq_count,),
        in_specs=[by_seq, by_seq, fixed],
        out_specs=[by_seq, fixed],
        out_shape=[
            jax.ShapeDtypeStruct(pre.shape, BF16),
            jax.ShapeDtypeStruct((rows, 8), F32),
        ],
        compiler_params=vmem_limit(8),
        cost_estimate=weight(3),
        name="state_backward",
    )(back, pre, taps)


def adam_step(weight, first, second, grad, rate, decay):
    first = BETA_ONE * first + (1.0 - BETA_ONE) * grad
    second = BETA_TWO * second + (1.0 - BETA_TWO) * grad * grad
    update = first / (1.0 - BETA_ONE**STEP) / (jnp.sqrt(second / (1.0 - BETA_TWO**STEP)) + ADAM_EPS)
    return (weight - rate * (update + decay * weight), first, second)


def after(value, *others):
    return lax.optimization_barrier((value, *others))[0]


def after_all(values, *others):
    values = tuple(values)
    return lax.optimization_barrier(values + others)[: len(values)]


def tour_dp():
    count = lax.axis_size("dp")
    order = [*range(0, count, 2), *range(count - 1, 0, -2)]
    forth = [(order[i], order[(i + 1) % count]) for i in range(count)]
    back = [(target, source) for source, target in forth]

    def group_at(ahead):
        group = lax.axis_index("dp")
        half = group // 2
        spot = jnp.where(lax.rem(group, 2) == 0, half, count - 1 - half)
        spot = lax.rem(spot + ahead + count, count)
        return jnp.where(spot < count // 2, 2 * spot, 2 * (count - 1 - spot) + 1)

    return forth, back, group_at, count // 2


def with_all(pair, *others):
    there = list(after_all(present(pair), *others))
    return tuple(None if part is None else there.pop(0) for part in pair)


def present(pair):
    return [part for part in pair if part is not None]


def gather_step(blocks, step, far_right):
    forth, back, _, far = tour_dp()
    right, left = blocks
    return (
        lax.ppermute(right, "dp", forth) if step < far or far_right else None,
        lax.ppermute(left, "dp", back) if step < far or not far_right else None,
    )


def place_kernel(starts, widths, *refs):
    blocks, refs = refs[: len(starts)], refs[len(starts) :]
    outs, sem = refs[: len(widths)], refs[len(widths)]
    copies = []
    for index, (ref, start) in enumerate(zip(blocks, starts)):
        start = pl.multiple_of(start(), 16)
        column = 0
        for out_index, (out, width) in enumerate(zip(outs, widths)):
            copies.append(
                pltpu.make_async_copy(
                    ref.at[:, column : column + width],
                    out.at[pl.ds(start, ref.shape[0]), :],
                    sem.at[index, out_index],
                )
            )
            column += width
    for copy in copies:
        copy.start()
    for copy in copies:
        copy.wait()


def place_rows(blocks, starts, widths, cost=2):
    rows = sum(block.shape[0] for block in blocks)
    return pl.pallas_call(
        functools.partial(place_kernel, starts, widths),
        in_specs=[pl.BlockSpec(memory_space=pltpu.HBM)] * len(blocks),
        out_specs=[pl.BlockSpec(memory_space=pltpu.VMEM)] * len(widths),
        out_shape=[jax.ShapeDtypeStruct((rows, width), blocks[0].dtype) for width in widths],
        scratch_shapes=[pltpu.SemaphoreType.DMA((len(blocks), len(widths)))],
        compiler_params=vmem_limit(2),
        cost_estimate=weight(cost),
        name="place_rows",
    )(*[in_hbm(block) for block in blocks])


def place_blocks(own, steps, widths):
    _, _, group_at, _ = tour_dp()
    count = lax.axis_size("dp")
    rows = own.shape[0]

    def start(ahead):
        return lambda: group_at(ahead) * rows

    blocks, starts = [own], [start(0)]
    for step, (right, left) in enumerate(steps, 1):
        if right is not None:
            blocks.append(right)
            starts.append(start(count - step))
        if left is not None:
            blocks.append(left)
            starts.append(start(step))
    return place_rows(blocks, starts, widths)


class Gather:
    def __init__(self, shard, far_right):
        self.shard = shard
        self.far_right = far_right
        self.moving = (shard, shard)
        self.steps = []

    def step(self, *others):
        moving = with_all(self.moving, *others)
        self.moving = gather_step(moving, len(self.steps) + 1, self.far_right)
        self.steps.append(self.moving)

    def arrived(self):
        return present(self.moving)

    def wait(self, *others):
        self.steps[-1] = self.moving = with_all(self.moving, *others)

    def place(self, widths):
        return place_blocks(self.shard, self.steps, widths)


class Scatter:
    def __init__(self, parts, far_right):
        self.parts = parts
        self.sums = scatter_start(parts, far_right)
        self.distance = lax.axis_size("dp") // 2

    def going(self):
        return present(self.sums)

    def move(self):
        self.sums = scatter_move(self.sums)
        self.distance -= 1

    def wait(self, *others):
        self.sums = with_all(self.sums, *others)

    def arrive(self, sums):
        sums = list(sums)
        self.sums = tuple(None if old is None else sums.pop(0) for old in self.sums)

    def add(self):
        self.sums = scatter_step(self.parts, self.sums, self.distance)

    def end(self):
        return scatter_end(self.parts, self.sums)


def scatter_block(parts, ahead):
    _, _, group_at, _ = tour_dp()
    rows = parts[0].shape[0] // lax.axis_size("dp")
    blocks = [lax.dynamic_slice_in_dim(part, group_at(ahead) * rows, rows, 0) for part in parts]
    return blocks[0] if len(blocks) == 1 else jnp.concatenate(blocks, axis=1)


def scatter_start(parts, far_right):
    _, _, _, far = tour_dp()
    block = scatter_block(parts, far)
    return (block, None) if far_right else (None, block)


def scatter_move(sums):
    forth, back, _, _ = tour_dp()
    right, left = sums
    return (
        None if right is None else lax.ppermute(right, "dp", forth),
        None if left is None else lax.ppermute(left, "dp", back),
    )


def ring_add_kernel(distance, count, widths, present_sums, *refs):
    sums, refs = refs[: len(present_sums)], refs[len(present_sums) :]
    parts, refs = refs[: len(widths)], refs[len(widths) :]
    outs, blocks, sem = refs[:2], refs[2], refs[3]
    rows = outs[0].shape[0]
    _, _, group_at, _ = tour_dp()
    copies = []
    for way, ahead in enumerate((distance, count - distance)):
        start = pl.multiple_of(group_at(ahead) * rows, 16)
        column = 0
        for index, (part, width) in enumerate(zip(parts, widths)):
            copies.append(
                pltpu.make_async_copy(
                    part.at[pl.ds(start, rows), :],
                    blocks.at[way, :, column : column + width],
                    sem.at[way, index],
                )
            )
            column += width
    for copy in copies:
        copy.start()
    for copy in copies:
        copy.wait()
    for way, out in enumerate(outs):
        block = blocks[way]
        if way in present_sums:
            arrived = sums[present_sums.index(way)][...]
            block = (block.astype(F32) + arrived.astype(F32)).astype(BF16)
        out[...] = block


def scatter_step(parts, sums, distance):
    count = lax.axis_size("dp")
    rows = parts[0].shape[0] // count
    widths = [part.shape[1] for part in parts]
    present_sums = [way for way, arrived in enumerate(sums) if arrived is not None]
    inside = pl.BlockSpec(memory_space=pltpu.VMEM)
    out = jax.ShapeDtypeStruct((rows, sum(widths)), BF16)
    return pl.pallas_call(
        functools.partial(ring_add_kernel, distance, count, widths, present_sums),
        in_specs=[inside] * len(present_sums)
        + [pl.BlockSpec(memory_space=pltpu.HBM)] * len(parts),
        out_specs=[inside, inside],
        out_shape=[out, out],
        scratch_shapes=[
            pltpu.VMEM((2, rows, sum(widths)), BF16),
            pltpu.SemaphoreType.DMA((2, len(parts))),
        ],
        compiler_params=vmem_limit(6),
        cost_estimate=weight(1),
        name="ring_add",
    )(*present(sums), *parts)


def scatter_end(parts, sums):
    own = scatter_block(parts, 0).astype(F32)
    for arrived in sums:
        own = own + arrived.astype(F32)
    return own


def gather_tensor_blocks(values):
    count = lax.axis_size("tensor")
    blocks = {0: values}
    step = count // 2
    while step:
        swap = [(i, i ^ step) for i in range(count)]
        blocks.update(
            {bits | step: lax.ppermute(block, "tensor", swap) for bits, block in blocks.items()}
        )
        step //= 2
    return blocks


def join_tensor(blocks, cost=2):
    rows, width = blocks[0].shape

    def start(bits):
        return lambda: (lax.axis_index("tensor") ^ bits) * rows

    return place_rows(list(blocks.values()), [start(bits) for bits in blocks], [width], cost)[0]


def scatter_tensor_split(values, step):
    side = (lax.axis_index("tensor") // step) % 2
    values = values.reshape(-1, 2, *values.shape[1:])
    kept = lax.dynamic_index_in_dim(values, side, 1, keepdims=False)
    return kept, lax.dynamic_index_in_dim(values, 1 - side, 1, keepdims=False).astype(BF16)


def scatter_tensor_move(given, step):
    count = lax.axis_size("tensor")
    return lax.ppermute(given, "tensor", [(i, i ^ step) for i in range(count)])


def scatter_tensor_step(values, step):
    kept, given = scatter_tensor_split(values, step)
    return kept.astype(F32) + scatter_tensor_move(given, step).astype(F32)


def first_half_kernel(values_ref, taken_ref, kept_ref, given_ref, held, sem):
    place = lax.axis_index("tensor")
    blocks = taken_ref.shape[0]
    copies = [
        pltpu.make_async_copy(
            values_ref.at[2 * block + lax.rem(place, 2)], held.at[block], sem.at[block]
        )
        for block in range(blocks)
    ]
    for copy in copies:
        copy.start()
    for copy in copies:
        copy.wait()
    side = lax.rem(place // 2, 2)
    for block in range(blocks // 2):
        own, other = 2 * block + side, 2 * block + 1 - side
        kept_ref[block] = held[own].astype(F32) + taken_ref[own].astype(F32)
        given_ref[block] = (held[other].astype(F32) + taken_ref[other].astype(F32)).astype(BF16)


class Halving:
    def __init__(self, values):
        count = lax.axis_size("tensor")
        self.values = values.reshape(count, -1, values.shape[-1])
        self.given = scatter_tensor_split(self.values, 1)[1]
        self.step = 1

    def move(self):
        self.taken = scatter_tensor_move(self.given, self.step)

    def wait(self, *others):
        self.taken = after(self.taken, *others)

    def add(self):
        count = lax.axis_size("tensor")
        self.step *= 2
        if self.step > 2:
            self.kept = self.kept + self.taken.astype(F32)
            if self.step < count:
                self.kept, self.given = scatter_tensor_split(self.kept, self.step)
            return
        _, rows, width = self.values.shape
        inside = pl.BlockSpec(memory_space=pltpu.VMEM)
        self.kept, self.given = pl.pallas_call(
            first_half_kernel,
            in_specs=[pl.BlockSpec(memory_space=pltpu.HBM), inside],
            out_specs=[inside, inside],
            out_shape=[
                jax.ShapeDtypeStruct((count // 4, rows, width), F32),
                jax.ShapeDtypeStruct((count // 4, rows, width), BF16),
            ],
            scratch_shapes=[
                pltpu.VMEM((count // 2, rows, width), BF16),
                pltpu.SemaphoreType.DMA((count // 2,)),
            ],
            compiler_params=vmem_limit(8),
            cost_estimate=weight(2),
            name="first_half",
        )(self.values, self.taken)

    def finish(self):
        while self.step < lax.axis_size("tensor"):
            self.move()
            self.add()
        return self.kept.reshape(self.kept.shape[-2:])


def sum_over(values, axes):
    for axis in axes:
        count = lax.axis_size(axis)
        step = 1
        while step < count:
            pairs = [(place, place ^ step) for place in range(count)]
            values = values + lax.ppermute(values, axis, pairs)
            step *= 2
    return values


def deal_out(values):
    count = lax.axis_size("dp")
    own_rows, width = values.shape
    pieces = values.reshape(count, own_rows // count, width)
    return lax.all_to_all(pieces, "dp", split_axis=0, concat_axis=0, tiled=True)


def deal_in(pieces):
    arrived = lax.all_to_all(pieces, "dp", split_axis=0, concat_axis=0, tiled=True)
    return arrived.reshape(-1, arrived.shape[-1])


def shards(
    tokens,
    cotangent,
    lengths,
    order,
    in_weight,
    in_first,
    in_second,
    out_weight,
    out_first,
    out_second,
    conv_weight,
    conv_first,
    conv_second,
    gain_vector,
    gain_first,
    gain_second,
    head_params,
    head_first,
    head_second,
):
    count_dp = lax.axis_size("dp")
    count_tensor = lax.axis_size("tensor")
    group = lax.axis_index("dp")
    place = lax.axis_index("tensor")
    own_rows, width = tokens.shape
    token_rows = own_rows * count_tensor
    seq_count = token_rows // LEN
    seq_total = order.shape[0]
    head_count = head_params.shape[0]
    padded_heads = -(-head_count // 8) * 8
    inner_cols = head_count * HEAD_DIM
    conv_rows = conv_weight.shape[0]
    state_cols = conv_rows - inner_cols
    inner_total = inner_cols * count_tensor
    norm_gain = gain_vector[:width]
    gate_gain = lax.dynamic_slice_in_dim(gain_vector, width + place * inner_cols, inner_cols, 0)
    gate_gain = gate_gain.reshape(1, inner_cols)

    positions = jnp.arange(seq_total)
    inverse = jnp.sum(
        jnp.where(order[:, None] == positions[None, :], positions[:, None], 0), axis=0
    )
    own_seq = (place * own_rows) // LEN
    sources = inverse[jnp.arange(count_dp) * seq_count + own_seq] // seq_count
    seq_lengths = lax.dynamic_slice_in_dim(lengths, group * seq_count, seq_count, 0)
    live_all = (
        (jnp.arange(LEN)[None, :] < seq_lengths[:, None]).astype(F32).reshape(token_rows, 1)
    )
    live_own = lax.dynamic_slice_in_dim(live_all, place * own_rows, own_rows, 0)

    own = tokens.astype(F32)
    inv_own = lax.rsqrt(jnp.mean(own * own, axis=1, keepdims=True) + EPS_NORM)
    normed_own = (own * inv_own * norm_gain).astype(BF16)
    side_cols = 128
    far = count_dp // 2
    in_low = in_weight.astype(BF16)
    side_real = in_low.shape[1] - 2 * inner_cols
    mixed_shard = jnp.pad(in_low[:, inner_cols:], ((0, 0), (0, side_cols - side_real)))
    normed_blocks = gather_tensor_blocks(normed_own)
    first_bit = count_tensor // 2
    chan = jnp.concatenate(
        [
            conv_weight[:inner_cols].T,
            jnp.repeat(head_params[:, 2], HEAD_DIM)[None, :],
            jnp.zeros((2, inner_cols), F32),
        ],
        axis=0,
    )
    rate = -jnp.exp(head_params[:, 1])
    heads = jnp.pad(
        jnp.stack([head_params[:, 0], rate], axis=1),
        ((0, padded_heads - head_count), (0, 126)),
    )
    state_taps = jnp.pad(conv_weight[inner_cols:], ((0, 0), (0, 3)))
    prepared = (chan, heads, state_taps, gate_gain, live_own)
    late_shard = jnp.concatenate([in_low[:, :inner_cols], out_weight.astype(BF16).T], axis=1)
    mixed_ring = Gather(mixed_shard, True)
    late_ring = Gather(late_shard, False)
    mixed_ring.step()
    cot_first = deal_out(after(cotangent, *mixed_ring.arrived()))
    cot_chosen = cot_first.at[sources].get(mode="promise_in_bounds")
    for _ in range(far - 2):
        mixed_ring.step()
    late_ring.step(*mixed_ring.arrived())
    mixed_ring.step(normed_blocks[first_bit], *prepared)
    in_inner, in_side = mixed_ring.place([inner_cols, side_cols])
    normed_blocks[0] = after(normed_blocks[0], cot_chosen)
    normed = join_tensor(normed_blocks, 30)
    cot_own = after(deal_in(cot_chosen), normed)
    back_out_own = (cot_own.astype(F32) * live_own).astype(BF16)
    back_out_blocks = gather_tensor_blocks(back_out_own)
    side_pre = dot_general_tt(in_side, after(normed, *late_ring.arrived()))
    late_ring.step()
    state_pre = by_sequence(side_pre[:state_cols], seq_count)
    step_pre = by_sequence(side_pre[state_cols : state_cols + padded_heads], seq_count)
    state_own = state_forward(state_pre, state_taps, seq_count)
    states = join_tensor(gather_tensor_blocks(from_sequence(state_own, seq_count)))
    states = by_sequence(states, seq_count)
    inner_pre = dot_nn(after(normed, side_pre, *late_ring.arrived()), in_inner).astype(BF16)
    for _ in range(far - 3):
        late_ring.step()
    inner_pre = after(inner_pre, *late_ring.arrived())
    late_ring.step()
    inner_pre = after(inner_pre, back_out_own)
    scanned, conv, entry = scan_forward(inner_pre, states, step_pre, chan, heads, head_count)
    late_ring.wait(scanned)
    in_gate, out_low = late_ring.place([inner_cols, inner_cols])
    back_out = join_tensor(back_out_blocks)
    gate_pre = lax.optimization_barrier(dot_nn(normed, in_gate).astype(BF16)).astype(F32)
    scanned = scanned.astype(F32)
    gate_sigmoid = jax.nn.sigmoid(gate_pre)
    gate = gate_pre * gate_sigmoid
    mixed = scanned * gate
    back_normed = lax.optimization_barrier(dot_nn(back_out, out_low).astype(BF16)).astype(F32)
    row_sums = jnp.stack(
        [jnp.sum(mixed * mixed, axis=1), jnp.sum(back_normed * gate_gain * mixed, axis=1)]
    )
    row_sums = lax.psum(row_sums, "tensor")
    gate_inv = lax.rsqrt(row_sums[0] / inner_total + EPS_NORM)[:, None]
    gate_rows = row_sums[1][:, None]
    scaled = mixed * gate_inv
    normed_out = lax.optimization_barrier((scaled * gate_gain).astype(BF16))
    grad_gate_gain = jnp.sum(back_normed * scaled, axis=0)
    back_mixed = gate_inv * (back_normed * gate_gain) - mixed * (
        gate_inv**3 * (gate_rows / inner_total)
    )
    back_gate = (
        back_mixed * scanned * (gate_sigmoid * (1.0 + gate_pre * (1.0 - gate_sigmoid)))
    ).astype(BF16)
    grad_gate_full, grad_out_full = lax.optimization_barrier(
        (dot_tn(normed, back_gate).astype(BF16), dot_tn(back_out, normed_out).astype(BF16))
    )
    early = Scatter((grad_gate_full, grad_out_full), False)
    partial_out = lax.optimization_barrier(dot_nt(normed_out, out_low).astype(BF16))
    branch = Halving(partial_out)
    dy = after((back_mixed * gate).astype(BF16), branch.given)
    held = ()
    back_parts = 2 if head_count % 4 == 0 else 1
    for part in range(back_parts):
        dy = after(dy, *early.going(), *held)
        held = scan_backward(
            dy, inner_pre, conv, states, step_pre, entry, chan, heads, head_count,
            part, back_parts, held,
        )
        early.move()
        branch.move()
        count = len(held)
        together = lax.optimization_barrier((*held, branch.taken, *early.going()))
        held = together[:count]
        branch.taken = together[count]
        early.arrive(together[count + 1 :])
        early.add()
        branch.add()
        dy = after(dy, branch.given)
    back_inner, back_states, back_step, dchan, dhead = held
    inner = Scatter(
        [lax.optimization_barrier(dot_tn(normed, after(back_inner, *early.going())).astype(BF16))],
        True,
    )
    state_kept, state_given = scatter_tensor_split(
        from_sequence(after(back_states, *inner.going()), seq_count).reshape(
            count_tensor, state_cols, token_rows
        ),
        1,
    )
    state_back = state_kept.astype(F32) + scatter_tensor_move(state_given, 1).astype(F32)
    step = 2
    while step < count_tensor:
        state_back = scatter_tensor_step(state_back, step)
        step *= 2
    state_back = state_back[0]
    back_main = lax.optimization_barrier(
        dot_nt(after(back_gate, state_given), in_gate)
        + dot_nt(after(back_inner, state_given), in_inner)
    )
    early.move()
    inner.move()
    inner.wait(back_main, *early.going())
    inner.add()
    early.add()
    back_state_pre, dtaps_state = state_backward(
        by_sequence(after(state_back, *inner.going(), *early.going()), seq_count), state_pre, state_taps, seq_count
    )
    back_step = from_sequence(back_step, seq_count)[:head_count].astype(BF16)
    back_side = jnp.concatenate(
        [
            from_sequence(back_state_pre, seq_count),
            back_step,
            jnp.zeros((side_cols - side_real, token_rows), BF16),
        ],
        axis=0,
    )
    back_input = (back_main + dot_general_tt(back_side, in_side)).astype(BF16)
    back_sum = Halving(back_input)
    grad_side = dot_general_tt(normed, after(back_side, back_sum.given)).astype(BF16)
    grad_side = grad_side.reshape(count_dp, -1, side_cols)
    back_sum.move()
    early.move()
    inner.move()
    inner.wait(grad_side)
    inner.add()
    back_sum.wait(*inner.going())
    back_sum.add()
    grad_side = lax.all_to_all(grad_side, "dp", split_axis=0, concat_axis=0, tiled=True)
    back_part = back_sum.finish()
    layer_output = (live_own * (own + branch.finish())).astype(BF16)
    while inner.distance > 1:
        while early.distance > inner.distance - 1:
            early.add()
            early.move()
        inner.move()
        inner.wait(back_sum.given)
        inner.add()
    inner.move()
    while early.distance > 0:
        early.add()
        early.move()
    grad_early = early.end()
    inner.wait(grad_early)
    grad_side = jnp.sum(grad_side.astype(F32), axis=0)[:, :side_real]
    grad_inner = inner.end()
    grad_out = grad_early[:, inner_cols:].T
    grad_in = jnp.concatenate([grad_early[:, :inner_cols], grad_inner, grad_side], axis=1)
    row_term = jnp.sum(back_part * norm_gain * own, axis=1, keepdims=True)
    back_own = inv_own * norm_gain * back_part - own * inv_own**3 * (row_term / width)
    input_grad = (live_own * cot_own.astype(F32) + back_own).astype(BF16)
    grad_norm_gain = jnp.sum(back_part * own * inv_own, axis=0)


    def as_rows(values):
        rows, lanes = values.shape
        return jnp.pad(values, ((0, 0), (0, inner_cols - lanes)))

    squares = jnp.sum(grad_in * grad_in) + jnp.sum(grad_out * grad_out)
    gain_rows = width // inner_cols
    shared = jnp.concatenate(
        [
            dchan[:6],
            grad_gate_gain[None, :],
            grad_norm_gain.reshape(gain_rows, inner_cols),
            as_rows(dtaps_state[:, :5].T),
            as_rows(dhead[:, :2].T),
            as_rows(squares.reshape(1, 1)),
        ],
        axis=0,
    )
    shared = sum_over(jnp.pad(shared, ((0, -shared.shape[0] % 8), (0, 0))), ("dp",))
    first = 7 + gain_rows
    grad_skip = jnp.sum(shared[5].reshape(head_count, HEAD_DIM), axis=1)
    grad_conv = jnp.concatenate([shared[:5], shared[first : first + 5, :state_cols]], axis=1).T
    head_rows = shared[first + 5 : first + 7, :head_count]
    grad_head = jnp.concatenate([head_rows, grad_skip[None, :]], axis=0).T
    squares = (
        shared[first + 7, 0]
        + jnp.sum(grad_conv * grad_conv)
        + jnp.sum(grad_head * grad_head)
        + jnp.sum(shared[6] * shared[6])
    )
    across = jnp.concatenate(
        [
            shared[7:first],
            lax.dynamic_update_slice(
                jnp.zeros((count_tensor, inner_cols), F32), shared[6:7], (place, 0)
            ),
            jnp.full((1, inner_cols), squares),
        ],
        axis=0,
    )
    across = after(across, layer_output)
    across = sum_over(jnp.pad(across, ((0, -across.shape[0] % 8), (0, 0))), ("tensor",))
    grad_gains = across[: gain_rows + count_tensor].reshape(-1)
    grad_norm_all = across[:gain_rows]
    grad_norm = jnp.sqrt(
        across[gain_rows + count_tensor, 0] + jnp.sum(grad_norm_all * grad_norm_all)
    )
    factor = CLIP_NORM / jnp.maximum(grad_norm, CLIP_NORM)
    new_in = adam_step(in_weight, in_first, in_second, factor * grad_in, RATE_MATRIX, DECAY)
    new_out = adam_step(out_weight, out_first, out_second, factor * grad_out, RATE_MATRIX, DECAY)
    new_conv = adam_step(conv_weight, conv_first, conv_second, factor * grad_conv, RATE_VECTOR, 0.0)
    new_gain = adam_step(
        gain_vector, gain_first, gain_second, factor * grad_gains, RATE_VECTOR, 0.0
    )
    new_head = adam_step(head_params, head_first, head_second, factor * grad_head, RATE_VECTOR, 0.0)
    return (
        layer_output,
        input_grad,
        grad_norm,
        *new_in,
        *new_out,
        *new_conv,
        *new_gain,
        *new_head,
        new_in[0].astype(BF16),
        new_out[0].astype(BF16),
    )


def solution(mesh):
    rows = P(("dp", "tensor"), None)
    in_matrix = P("dp", "tensor")
    out_matrix = P("tensor", "dp")
    by_tensor = P("tensor", None)
    same = P()
    in_specs = (
        (rows, rows, same, same)
        + (in_matrix,) * 3
        + (out_matrix,) * 3
        + (by_tensor,) * 3
        + (same,) * 3
        + (by_tensor,) * 3
    )
    out_specs = (
        (rows, rows, same)
        + (in_matrix,) * 3
        + (out_matrix,) * 3
        + (by_tensor,) * 3
        + (same,) * 3
        + (by_tensor,) * 3
        + (in_matrix, out_matrix)
    )
    return jax.shard_map(shards, mesh=mesh, in_specs=in_specs, out_specs=out_specs, check_vma=False)
```

```python
import functools
import jax
import jax.numpy as jnp
from jax import lax
from jax.experimental import pallas as pl
from jax.experimental.pallas import tpu as pltpu
from jax.sharding import PartitionSpec as P
HEAD_DIM = 64
STATE = 128
LEN = 1024
STEP = 5
CHUNK = 128
PAIR = 2 * HEAD_DIM
EPS_NORM = 1e-05
BETA_ONE = 0.5
BETA_TWO = 0.5
ADAM_EPS = 1e-08
DECAY = 0.1
RATE_MATRIX = 0.02
RATE_VECTOR = 0.8
CLIP_NORM = 1.0
HIGHEST_PRECISION = lax.Precision.HIGHEST
MASKED = -1e+30
BF16 = jnp.bfloat16
F32 = jnp.float32


def sigmoid(values):
    return 1.0 / (1.0 + jnp.exp(-values))


def softplus(values):
    return jnp.maximum(values, 0.0) + jnp.log1p(jnp.exp(-jnp.abs(values)))


def vmem_limit(mebibytes):
    return pltpu.CompilerParams(vmem_limit_bytes=mebibytes * 1024 * 1024)


def in_hbm(values):
    return pltpu.with_memory_space_constraint(values, pltpu.HBM)


def weight(microseconds):
    return pl.CostEstimate(flops=microseconds * 10 ** 9, bytes_accessed=0, transcendentals=0)


def dot_nn(left, right):
    return lax.dot_general(left, right, (((1,), (0,)), ((), ())), preferred_element_type=F32)


def dot_nt(left, right):
    return lax.dot_general(left, right, (((1,), (1,)), ((), ())), preferred_element_type=F32)


def dot_tn(left, right):
    return lax.dot_general(left, right, (((0,), (0,)), ((), ())), preferred_element_type=F32)


def dot_general_tt(left, right):
    return lax.dot_general(left, right, (((0,), (1,)), ((), ())), preferred_element_type=F32)


def by_sequence(values, seq_count):
    if seq_count == 1:
        return values
    rows = values.shape[0]
    return jnp.swapaxes(values.reshape(rows, seq_count, LEN), 0, 1).reshape(-1, LEN)


def from_sequence(values, seq_count):
    if seq_count == 1:
        return values
    rows = values.shape[0] // seq_count
    return jnp.swapaxes(values.reshape(seq_count, rows, LEN), 0, 1).reshape(rows, -1)


def dot_exact(left, right):
    high = left.astype(BF16)
    rest = left - high.astype(F32)
    middle = rest.astype(BF16)
    low = (rest - middle.astype(F32)).astype(BF16)
    rows = left.shape[0]
    product = dot_nn(jnp.concatenate([high, middle, low], axis=0), right)
    return product[:rows] + product[rows:2 * rows] + product[2 * rows:]


def square_places():
    row = lax.broadcasted_iota(jnp.int32, (CHUNK, CHUNK), 0)
    column = lax.broadcasted_iota(jnp.int32, (CHUNK, CHUNK), 1)
    return (row, column)


def chunk_logs(step_ref, head_ref):
    biased = step_ref[...] + head_ref[:, 0:1]
    step = softplus(biased)
    row, column = square_places()
    upto = jnp.where(row <= column, 1.0, 0.0).astype(BF16)
    logs = dot_exact(step * head_ref[:, 1:2], upto)
    padding = jnp.zeros((CHUNK - step.shape[0], CHUNK), F32)
    step_rows = jnp.transpose(jnp.concatenate([step, padding], axis=0))
    logs_rows = jnp.transpose(jnp.concatenate([logs, padding], axis=0))
    return (biased, step, logs, step_rows, logs_rows)


def spread(columns, head):
    return jnp.broadcast_to(columns[:, head:head + 1], (CHUNK, CHUNK))


def scan_forward_kernel(head_count, x_ref, bc_ref, step_ref, chan_ref, head_ref, y_ref, xc_ref, entry_ref, rows, state, fresh):

    @pl.when(pl.program_id(1) == 0)
    def _():
        state[...] = jnp.zeros_like(state)
        rows[0:8, :] = jnp.zeros((8, rows.shape[1]), F32)
    rows[8:8 + CHUNK, :] = x_ref[...].astype(F32)
    entry_ref[0, 0] = state[...].astype(BF16)
    _, _, logs, step_rows, logs_rows = chunk_logs(step_ref, head_ref)
    in_columns = bc_ref[:STATE, :]
    state_out = jnp.transpose(bc_ref[STATE:, :])
    scores = dot_nn(state_out, in_columns)
    row, column = square_places()
    first_half = column < HEAD_DIM
    later = row >= column
    for pair in range(head_count // 2):
        lanes = slice(pair * PAIR, (pair + 1) * PAIR)
        conv = chan_ref[4:5, lanes]
        for tap in range(4):
            conv = conv + chan_ref[tap:tap + 1, lanes] * rows[5 + tap:5 + tap + CHUNK, lanes]
        xc_ref[:, lanes] = conv.astype(BF16)
        values = conv * sigmoid(conv)
        even, odd = (2 * pair, 2 * pair + 1)
        step_pair = jnp.where(first_half, spread(step_rows, even), spread(step_rows, odd))
        logs_even, logs_odd = (spread(logs_rows, even), spread(logs_rows, odd))
        logs_pair = jnp.where(first_half, logs_even, logs_odd)
        within_even = jnp.exp(jnp.where(later, logs_even - logs[even:even + 1, :], MASKED))
        within_odd = jnp.exp(jnp.where(later, logs_odd - logs[odd:odd + 1, :], MASKED))
        mixing = jnp.concatenate([(scores * within_even).astype(BF16), (scores * within_odd).astype(BF16)], axis=1)
        weighted = step_pair * values
        zero = jnp.zeros_like(weighted)
        stacked = jnp.concatenate([jnp.where(first_half, weighted, zero).astype(BF16), jnp.where(first_half, zero, weighted).astype(BF16)], axis=0)
        inner = dot_nn(mixing, stacked)
        outer = dot_nn(state_out, entry_ref[0, 0, :, lanes]) * jnp.exp(logs_pair)
        y_ref[:, lanes] = (inner + outer + chan_ref[5:6, lanes] * values).astype(BF16)
        last = logs_pair[CHUNK - 1:CHUNK, :]
        fresh[:, lanes] = (jnp.exp(last - logs_pair) * weighted).astype(BF16)
        state[:, lanes] = jnp.exp(last) * state[:, lanes]
    state[...] += dot_nn(in_columns, fresh[...])
    rows[0:8, :] = rows[CHUNK:CHUNK + 8, :]


def scan_backward_kernel(first_head, head_count, dy_ref, x_ref, xc_ref, bc_ref, step_ref, entry_ref, chan_ref, head_ref, *outputs_and_scratch):
    dx_ref, dbc_ref, dstep_ref, dchan_ref, dhead_ref, rows, back, leaving, arriving, sums_one, sums_two, sums_three, crossings, decays = outputs_and_scratch[-14:]
    sums_before = outputs_and_scratch[2:-14]

    @pl.when(pl.program_id(1) == 0)
    def _():
        back[...] = jnp.zeros_like(back)
        rows[CHUNK:CHUNK + 8, :] = jnp.zeros((8, rows.shape[1]), F32)

    @pl.when((pl.program_id(0) == 0) & (pl.program_id(1) == 0))
    def _():
        dchan_ref[...] = jnp.zeros_like(dchan_ref)
        dhead_ref[...] = sums_before[2][...] if sums_before else jnp.zeros_like(dhead_ref)
    padded = step_ref.shape[0]
    biased, step, logs, step_rows, logs_rows = chunk_logs(step_ref, head_ref)
    in_columns = bc_ref[:STATE, :]
    out_columns = bc_ref[STATE:, :]
    state_in = jnp.transpose(in_columns)
    state_out = jnp.transpose(out_columns)
    scores = dot_nn(state_in, out_columns)
    back_low = back[...].astype(BF16)
    entry = entry_ref[0, 0]
    row, column = square_places()
    first_half = column < HEAD_DIM
    later = column >= row
    head_row = lax.broadcasted_iota(jnp.int32, (padded, CHUNK), 0)
    wide_row = lax.broadcasted_iota(jnp.int32, (head_count * CHUNK, CHUNK), 0) // CHUNK
    wide_column = lax.broadcasted_iota(jnp.int32, (head_count * CHUNK, CHUNK), 1)
    total = jnp.zeros((CHUNK, CHUNK), F32)
    over_rows = jnp.zeros((padded, CHUNK), F32)
    for pair in range(head_count // 2):
        lanes = slice(pair * PAIR, (pair + 1) * PAIR)
        even = first_head + 2 * pair
        odd = even + 1
        conv = xc_ref[:, lanes].astype(F32)
        gate = sigmoid(conv)
        values = conv * gate
        dy_low = dy_ref[:, lanes]
        dy = dy_low.astype(F32)
        step_pair = jnp.where(first_half, spread(step_rows, even), spread(step_rows, odd))
        logs_even, logs_odd = (spread(logs_rows, even), spread(logs_rows, odd))
        logs_pair = jnp.where(first_half, logs_even, logs_odd)
        weighted = step_pair * values
        zero = jnp.zeros_like(weighted)
        dy_stacked = jnp.concatenate([jnp.where(first_half, dy, zero).astype(BF16), jnp.where(first_half, zero, dy).astype(BF16)], axis=0)
        transfers = []
        for head, log_column, part in ((even, logs_even, jnp.where(first_half, weighted, zero).astype(BF16)), (odd, logs_odd, jnp.where(first_half, zero, weighted).astype(BF16))):
            within = jnp.exp(jnp.where(later, logs[head:head + 1, :] - log_column, MASKED))
            product = within * dot_nt(part, dy_low)
            total = total + product
            crossing = (scores * product).astype(BF16)
            local = head - first_head
            crossings[:, local * CHUNK:(local + 1) * CHUNK] = crossing
            sums = jnp.sum(crossing.astype(F32), axis=0, keepdims=True)
            over_rows = jnp.where(head_row == head, sums, over_rows)
            transfers.append((scores * within).astype(BF16))
        grown = jnp.exp(logs_pair)
        last = logs_pair[CHUNK - 1:CHUNK, :]
        decays[0:1, lanes] = jnp.exp(last)
        to_end = jnp.exp(last - logs_pair)
        from_end = to_end * dot_nn(state_in, back_low[:, lanes])
        dweighted = dot_nn(jnp.concatenate(transfers, axis=1), dy_stacked) + from_end
        grown_dy = grown * dy
        leaving[:, lanes] = grown_dy.astype(BF16)
        arriving[:, lanes] = (to_end * weighted).astype(BF16)
        sums_one[:, lanes] = (grown_dy * dot_nn(state_out, entry[:, lanes])).astype(BF16)
        sums_two[:, lanes] = (weighted * from_end).astype(BF16)
        sums_three[:, lanes] = (values * dweighted).astype(BF16)
        dvalues = step_pair * dweighted + chan_ref[5:6, lanes] * dy
        dconv = dvalues * (gate * (1.0 + conv * (1.0 - gate)))
        rows[0:CHUNK, lanes] = dconv
        dchan_ref[5:6, lanes] += jnp.sum(dy * values, axis=0, keepdims=True)
        dchan_ref[4:5, lanes] += jnp.sum(dconv, axis=0, keepdims=True)
        raw = x_ref[:, lanes].astype(F32)
        dx = jnp.zeros((CHUNK, PAIR), F32)
        for tap in range(4):
            shifted = rows[3 - tap:3 - tap + CHUNK, lanes]
            dx = dx + chan_ref[tap:tap + 1, lanes] * shifted
            dchan_ref[tap:tap + 1, lanes] += jnp.sum(raw * shifted, axis=0, keepdims=True)
        dx_ref[:, lanes] = dx.astype(BF16)
    rows[CHUNK:CHUNK + 8, :] = rows[0:8, :]
    total_low = total.astype(BF16)
    dstate_in = dot_nt(out_columns, total_low) + dot_nt(back_low, arriving[...])
    dstate_out = dot_nn(in_columns, total_low) + dot_nt(entry, leaving[...])
    if sums_before:
        dstate_in = dstate_in + sums_before[0][:STATE, :].astype(F32)
        dstate_out = dstate_out + sums_before[0][STATE:, :].astype(F32)
    dbc_ref[:STATE, :] = dstate_in.astype(BF16)
    dbc_ref[STATE:, :] = dstate_out.astype(BF16)
    channels = back.shape[1]
    owner = first_head + lax.broadcasted_iota(jnp.int32, (padded, channels), 1) // HEAD_DIM
    member = owner == lax.broadcasted_iota(jnp.int32, (padded, channels), 0)
    member = jnp.where(member, 1.0, 0.0).astype(BF16)
    from_entry = dot_nt(member, sums_one[...])
    to_exit = dot_nt(member, sums_two[...])
    step_direct = dot_nt(member, sums_three[...])
    decayed = decays[0:1, :] * back[...]
    carried = jnp.sum(decayed * entry.astype(F32), axis=0, keepdims=True)
    carried = jnp.broadcast_to(carried, (CHUNK, channels)).astype(BF16)
    carried = dot_nt(member, carried)
    back[...] = decayed + dot_nn(out_columns, leaving[...])
    pick = jnp.where(wide_row + first_head == wide_column, 1.0, 0.0).astype(BF16)
    over_columns = jnp.transpose(dot_nn(crossings[...], pick))[:padded]
    onward = jnp.where(row >= column, 1.0, 0.0).astype(BF16)
    before = jnp.where(row < column, 1.0, 0.0).astype(BF16)
    dlogs = dot_exact(jnp.concatenate([over_rows - over_columns + from_entry, to_exit], axis=1), jnp.concatenate([onward, before], axis=0))
    dlogs = dlogs + carried
    rate = head_ref[:, 1:2]
    dstep = (rate * dlogs + step_direct) * sigmoid(biased)
    dstep_ref[...] = dstep + sums_before[1][...] if sums_before else dstep
    dhead_ref[:, 0:1] += jnp.sum(dstep, axis=1, keepdims=True)
    dhead_ref[:, 1:2] += rate * jnp.sum(step * dlogs, axis=1, keepdims=True)


def chunk_specs(seq_count, channels, padded, reverse):
    chunks = LEN // CHUNK

    def place(seq, chunk):
        return chunks - 1 - chunk if reverse else chunk

    def by_rows(width):
        return pl.BlockSpec((CHUNK, width), lambda seq, chunk: (seq * chunks + place(seq, chunk), 0))
    step_spec = pl.BlockSpec((padded, CHUNK), lambda seq, chunk: (seq, place(seq, chunk)))
    entry_spec = pl.BlockSpec((1, 1, STATE, channels), lambda seq, chunk: (seq, place(seq, chunk), 0, 0))

    def fixed(*shape):
        return pl.BlockSpec(shape, lambda seq, chunk: (0, 0))
    state_spec = pl.BlockSpec((2 * STATE, CHUNK), lambda seq, chunk: (seq, place(seq, chunk)))
    return ((seq_count, chunks), by_rows, step_spec, state_spec, entry_spec, fixed)


def scan_forward(x_pre, states, step_pre, chan, heads, head_count):
    token_rows, channels = x_pre.shape
    padded = heads.shape[0]
    seq_count = token_rows // LEN
    grid, by_rows, step_spec, state_spec, entry_spec, fixed = chunk_specs(seq_count, channels, padded, False)
    return pl.pallas_call(functools.partial(scan_forward_kernel, head_count), grid=grid, in_specs=[by_rows(channels), state_spec, step_spec, fixed(8, channels), fixed(padded, 128)], out_specs=[by_rows(channels), by_rows(channels), entry_spec], out_shape=[jax.ShapeDtypeStruct((token_rows, channels), BF16), jax.ShapeDtypeStruct((token_rows, channels), BF16), jax.ShapeDtypeStruct((seq_count, LEN // CHUNK, STATE, channels), BF16)], scratch_shapes=[pltpu.VMEM((CHUNK + 8, channels), F32), pltpu.VMEM((STATE, channels), F32), pltpu.VMEM((CHUNK, channels), BF16)], compiler_params=vmem_limit(16), cost_estimate=weight(11), name='scan_forward')(x_pre, states, step_pre, chan, heads)


def scan_backward(dy, x_pre, conv, states, step_pre, entry, chan, heads, head_count, part, parts, held):
    token_rows, channels = x_pre.shape
    padded = heads.shape[0]
    seq_count = token_rows // LEN
    part_heads = head_count // parts
    width = channels // parts
    chunks = LEN // CHUNK

    def by_rows(seq, chunk):
        return (seq * chunks + chunks - 1 - chunk, part)
    wide = pl.BlockSpec((CHUNK, width), by_rows)
    step_spec = pl.BlockSpec((padded, CHUNK), lambda seq, chunk: (seq, chunks - 1 - chunk))
    state_spec = pl.BlockSpec((2 * STATE, CHUNK), lambda seq, chunk: (seq, chunks - 1 - chunk))
    entry_spec = pl.BlockSpec((1, 1, STATE, width), lambda seq, chunk: (seq, chunks - 1 - chunk, 0, part))
    chan_spec = pl.BlockSpec((8, width), lambda seq, chunk: (0, part))
    head_spec = pl.BlockSpec((padded, 128), lambda seq, chunk: (0, 0))
    low_rows = pltpu.VMEM((CHUNK, width), BF16)
    in_specs = [wide, wide, wide, state_spec, step_spec, entry_spec, chan_spec, head_spec]
    in_place = {}
    if held:
        in_place = {len(in_specs): 0, len(in_specs) + 1: 3}
        dx, dbc, dstep, dchan, dhead = held
        held = (dx, dchan, dbc, dstep, dhead)
        in_specs = in_specs + [pl.BlockSpec(memory_space=pl.ANY)] * 2
        in_specs = in_specs + [state_spec, step_spec, head_spec]
    return pl.pallas_call(functools.partial(scan_backward_kernel, part * part_heads, part_heads), grid=(seq_count, chunks), in_specs=in_specs, out_specs=[wide, state_spec, step_spec, chan_spec, head_spec], out_shape=[jax.ShapeDtypeStruct((token_rows, channels), BF16), jax.ShapeDtypeStruct((seq_count * 2 * STATE, LEN), BF16), jax.ShapeDtypeStruct((seq_count * padded, LEN), F32), jax.ShapeDtypeStruct((8, channels), F32), jax.ShapeDtypeStruct((padded, 128), F32)], scratch_shapes=[pltpu.VMEM((CHUNK + 8, width), F32), pltpu.VMEM((STATE, width), F32), low_rows, low_rows, low_rows, low_rows, low_rows, pltpu.VMEM((CHUNK, part_heads * CHUNK), BF16), pltpu.VMEM((8, width), F32)], input_output_aliases=in_place, compiler_params=vmem_limit(16), cost_estimate=weight(20), name='scan_backward')(dy, x_pre, conv, states, step_pre, entry, chan, heads, *held)


def lane_shift(values, amount):
    if amount == 0:
        return values
    lane = lax.broadcasted_iota(jnp.int32, values.shape, 1)
    if amount > 0:
        return jnp.where(lane >= amount, pltpu.roll(values, amount, 1), 0.0)
    return jnp.where(lane < LEN + amount, pltpu.roll(values, LEN + amount, 1), 0.0)


def state_conv(pre, taps_ref):
    conv = jnp.broadcast_to(taps_ref[:, 4:5], pre.shape)
    for tap in range(4):
        conv = conv + taps_ref[:, tap:tap + 1] * lane_shift(pre, 3 - tap)
    return conv


def state_forward_kernel(pre_ref, taps_ref, states_ref):
    conv = state_conv(pre_ref[...], taps_ref)
    states_ref[...] = (conv * sigmoid(conv)).astype(BF16)


def state_backward_kernel(back_ref, pre_ref, taps_ref, dpre_ref, dtaps_ref):

    @pl.when(pl.program_id(0) == 0)
    def _():
        dtaps_ref[...] = jnp.zeros_like(dtaps_ref)
    pre = pre_ref[...]
    conv = state_conv(pre, taps_ref)
    gate = sigmoid(conv)
    dconv = back_ref[...] * (gate * (1.0 + conv * (1.0 - gate)))
    dpre = jnp.zeros_like(pre)
    for tap in range(4):
        shifted = lane_shift(dconv, tap - 3)
        dpre = dpre + taps_ref[:, tap:tap + 1] * shifted
        dtaps_ref[:, tap:tap + 1] += jnp.sum(pre * shifted, axis=1, keepdims=True)
    dtaps_ref[:, 4:5] += jnp.sum(dconv, axis=1, keepdims=True)
    dpre_ref[...] = dpre.astype(BF16)


def state_forward(pre, taps, seq_count):
    rows = pre.shape[0] // seq_count
    by_seq = pl.BlockSpec((rows, LEN), lambda seq: (seq, 0))
    return pl.pallas_call(state_forward_kernel, grid=(seq_count,), in_specs=[by_seq, pl.BlockSpec((rows, 8), lambda seq: (0, 0))], out_specs=by_seq, out_shape=jax.ShapeDtypeStruct(pre.shape, BF16), compiler_params=vmem_limit(8), name='state_forward')(pre, taps)


def state_backward(back, pre, taps, seq_count):
    rows = pre.shape[0] // seq_count
    by_seq = pl.BlockSpec((rows, LEN), lambda seq: (seq, 0))
    fixed = pl.BlockSpec((rows, 8), lambda seq: (0, 0))
    return pl.pallas_call(state_backward_kernel, grid=(seq_count,), in_specs=[by_seq, by_seq, fixed], out_specs=[by_seq, fixed], out_shape=[jax.ShapeDtypeStruct(pre.shape, BF16), jax.ShapeDtypeStruct((rows, 8), F32)], compiler_params=vmem_limit(8), cost_estimate=weight(3), name='state_backward')(back, pre, taps)


def adam_step(weight, first, second, grad, rate, decay):
    first = BETA_ONE * first + (1.0 - BETA_ONE) * grad
    second = BETA_TWO * second + (1.0 - BETA_TWO) * grad * grad
    update = first / (1.0 - BETA_ONE ** STEP) / (jnp.sqrt(second / (1.0 - BETA_TWO ** STEP)) + ADAM_EPS)
    return (weight - rate * (update + decay * weight), first, second)


def after(value, *others):
    return lax.optimization_barrier((value, *others))[0]


def after_all(values, *others):
    values = tuple(values)
    return lax.optimization_barrier(values + others)[:len(values)]


def tour_dp():
    count = lax.axis_size('dp')
    order = [*range(0, count, 2), *range(count - 1, 0, -2)]
    forth = [(order[i], order[(i + 1) % count]) for i in range(count)]
    back = [(target, source) for source, target in forth]

    def group_at(ahead):
        group = lax.axis_index('dp')
        half = group // 2
        spot = jnp.where(lax.rem(group, 2) == 0, half, count - 1 - half)
        spot = lax.rem(spot + ahead + count, count)
        return jnp.where(spot < count // 2, 2 * spot, 2 * (count - 1 - spot) + 1)
    return (forth, back, group_at, count // 2)


def with_all(pair, *others):
    there = list(after_all(present(pair), *others))
    return tuple((None if part is None else there.pop(0) for part in pair))


def present(pair):
    return [part for part in pair if part is not None]


def gather_step(blocks, step, far_right):
    forth, back, _, far = tour_dp()
    right, left = blocks
    return (lax.ppermute(right, 'dp', forth) if step < far or far_right else None, lax.ppermute(left, 'dp', back) if step < far or not far_right else None)


def place_kernel(starts, widths, *refs):
    blocks, refs = (refs[:len(starts)], refs[len(starts):])
    outs, sem = (refs[:len(widths)], refs[len(widths)])
    copies = []
    for index, (ref, start) in enumerate(zip(blocks, starts)):
        start = pl.multiple_of(start(), 16)
        column = 0
        for out_index, (out, width) in enumerate(zip(outs, widths)):
            copies.append(pltpu.make_async_copy(ref.at[:, column:column + width], out.at[pl.ds(start, ref.shape[0]), :], sem.at[index, out_index]))
            column += width
    for copy in copies:
        copy.start()
    for copy in copies:
        copy.wait()


def place_rows(blocks, starts, widths, cost=2):
    rows = sum((block.shape[0] for block in blocks))
    return pl.pallas_call(functools.partial(place_kernel, starts, widths), in_specs=[pl.BlockSpec(memory_space=pltpu.HBM)] * len(blocks), out_specs=[pl.BlockSpec(memory_space=pltpu.VMEM)] * len(widths), out_shape=[jax.ShapeDtypeStruct((rows, width), blocks[0].dtype) for width in widths], scratch_shapes=[pltpu.SemaphoreType.DMA((len(blocks), len(widths)))], compiler_params=vmem_limit(2), cost_estimate=weight(cost), name='place_rows')(*[in_hbm(block) for block in blocks])


def place_blocks(own, steps, widths):
    _, _, group_at, _ = tour_dp()
    count = lax.axis_size('dp')
    rows = own.shape[0]

    def start(ahead):
        return lambda: group_at(ahead) * rows
    blocks, starts = ([own], [start(0)])
    for step, (right, left) in enumerate(steps, 1):
        if right is not None:
            blocks.append(right)
            starts.append(start(count - step))
        if left is not None:
            blocks.append(left)
            starts.append(start(step))
    return place_rows(blocks, starts, widths)


def fence_kernel(token_ref, out_ref):
    out_ref[...] = token_ref[...]


def fence(*going):
    token = after(jnp.zeros((8, 128), F32), *going)
    return pl.pallas_call(fence_kernel, out_shape=jax.ShapeDtypeStruct((8, 128), F32), compiler_params=vmem_limit(1), cost_estimate=weight(100), name='fence')(token)


class Gather:
    def __init__(self, shard, far_right):
        self.shard = shard
        self.far_right = far_right
        self.moving = (shard, shard)
        self.steps = []

    def step(self, *others):
        moving = with_all(self.moving, *others)
        self.moving = gather_step(moving, len(self.steps) + 1, self.far_right)
        self.steps.append(self.moving)

    def arrived(self):
        return present(self.moving)

    def wait(self, *others):
        self.steps[-1] = self.moving = with_all(self.moving, *others)

    def place(self, widths):
        return place_blocks(self.shard, self.steps, widths)


class Scatter:
    def __init__(self, parts, far_right):
        self.parts = parts
        self.sums = scatter_start(parts, far_right)
        self.distance = lax.axis_size('dp') // 2

    def going(self):
        return present(self.sums)

    def move(self):
        self.sums = scatter_move(self.sums)
        self.distance -= 1

    def wait(self, *others):
        self.sums = with_all(self.sums, *others)

    def arrive(self, sums):
        sums = list(sums)
        self.sums = tuple((None if old is None else sums.pop(0) for old in self.sums))

    def add(self):
        self.sums = scatter_step(self.parts, self.sums, self.distance)

    def end(self):
        return scatter_end(self.parts, self.sums)


def scatter_block(parts, ahead):
    _, _, group_at, _ = tour_dp()
    rows = parts[0].shape[0] // lax.axis_size('dp')
    blocks = [lax.dynamic_slice_in_dim(part, group_at(ahead) * rows, rows, 0) for part in parts]
    return blocks[0] if len(blocks) == 1 else jnp.concatenate(blocks, axis=1)


def scatter_start(parts, far_right):
    _, _, _, far = tour_dp()
    block = scatter_block(parts, far)
    return (block, None) if far_right else (None, block)


def scatter_move(sums):
    forth, back, _, _ = tour_dp()
    right, left = sums
    return (None if right is None else lax.ppermute(right, 'dp', forth), None if left is None else lax.ppermute(left, 'dp', back))


def ring_add_kernel(distance, count, widths, present_sums, *refs):
    sums, refs = (refs[:len(present_sums)], refs[len(present_sums):])
    parts, refs = (refs[:len(widths)], refs[len(widths):])
    outs, blocks, sem = (refs[:2], refs[2], refs[3])
    rows = outs[0].shape[0]
    _, _, group_at, _ = tour_dp()
    copies = []
    for way, ahead in enumerate((distance, count - distance)):
        start = pl.multiple_of(group_at(ahead) * rows, 16)
        column = 0
        for index, (part, width) in enumerate(zip(parts, widths)):
            copies.append(pltpu.make_async_copy(part.at[pl.ds(start, rows), :], blocks.at[way, :, column:column + width], sem.at[way, index]))
            column += width
    for copy in copies:
        copy.start()
    for copy in copies:
        copy.wait()
    for way, out in enumerate(outs):
        block = blocks[way]
        if way in present_sums:
            arrived = sums[present_sums.index(way)][...]
            block = (block.astype(F32) + arrived.astype(F32)).astype(BF16)
        out[...] = block


def scatter_step(parts, sums, distance):
    count = lax.axis_size('dp')
    rows = parts[0].shape[0] // count
    widths = [part.shape[1] for part in parts]
    present_sums = [way for way, arrived in enumerate(sums) if arrived is not None]
    inside = pl.BlockSpec(memory_space=pltpu.VMEM)
    out = jax.ShapeDtypeStruct((rows, sum(widths)), BF16)
    return pl.pallas_call(functools.partial(ring_add_kernel, distance, count, widths, present_sums), in_specs=[inside] * len(present_sums) + [pl.BlockSpec(memory_space=pltpu.HBM)] * len(parts), out_specs=[inside, inside], out_shape=[out, out], scratch_shapes=[pltpu.VMEM((2, rows, sum(widths)), BF16), pltpu.SemaphoreType.DMA((2, len(parts)))], compiler_params=vmem_limit(6), cost_estimate=weight(4), name='ring_add')(*present(sums), *parts)


def scatter_end(parts, sums):
    own = scatter_block(parts, 0).astype(F32)
    for arrived in sums:
        own = own + arrived.astype(F32)
    return own


def gather_tensor_blocks(values):
    count = lax.axis_size('tensor')
    blocks = {0: values}
    step = count // 2
    while step:
        swap = [(i, i ^ step) for i in range(count)]
        blocks.update({bits | step: lax.ppermute(block, 'tensor', swap) for bits, block in blocks.items()})
        step //= 2
    return blocks


def join_tensor(blocks, cost=2):
    rows, width = blocks[0].shape

    def start(bits):
        return lambda: (lax.axis_index('tensor') ^ bits) * rows
    return place_rows(list(blocks.values()), [start(bits) for bits in blocks], [width], cost)[0]


def scatter_tensor_split(values, step):
    side = lax.axis_index('tensor') // step % 2
    values = values.reshape(-1, 2, *values.shape[1:])
    kept = lax.dynamic_index_in_dim(values, side, 1, keepdims=False)
    return (kept, lax.dynamic_index_in_dim(values, 1 - side, 1, keepdims=False).astype(BF16))


def scatter_tensor_move(given, step):
    count = lax.axis_size('tensor')
    return lax.ppermute(given, 'tensor', [(i, i ^ step) for i in range(count)])


def scatter_tensor_step(values, step):
    kept, given = scatter_tensor_split(values, step)
    return kept.astype(F32) + scatter_tensor_move(given, step).astype(F32)


def first_half_kernel(values_ref, taken_ref, kept_ref, given_ref, held, sem):
    place = lax.axis_index('tensor')
    blocks = taken_ref.shape[0]
    copies = [pltpu.make_async_copy(values_ref.at[2 * block + lax.rem(place, 2)], held.at[block], sem.at[block]) for block in range(blocks)]
    for copy in copies:
        copy.start()
    for copy in copies:
        copy.wait()
    side = lax.rem(place // 2, 2)
    for block in range(blocks // 2):
        own, other = (2 * block + side, 2 * block + 1 - side)
        kept_ref[block] = held[own].astype(F32) + taken_ref[own].astype(F32)
        given_ref[block] = (held[other].astype(F32) + taken_ref[other].astype(F32)).astype(BF16)


class Halving:
    def __init__(self, values):
        count = lax.axis_size('tensor')
        self.values = values.reshape(count, -1, values.shape[-1])
        self.given = scatter_tensor_split(self.values, 1)[1]
        self.step = 1

    def move(self):
        self.taken = scatter_tensor_move(self.given, self.step)

    def wait(self, *others):
        self.taken = after(self.taken, *others)

    def add(self):
        count = lax.axis_size('tensor')
        self.step *= 2
        if self.step > 2:
            self.kept = self.kept + self.taken.astype(F32)
            if self.step < count:
                self.kept, self.given = scatter_tensor_split(self.kept, self.step)
            return
        _, rows, width = self.values.shape
        inside = pl.BlockSpec(memory_space=pltpu.VMEM)
        self.kept, self.given = pl.pallas_call(first_half_kernel, in_specs=[pl.BlockSpec(memory_space=pltpu.HBM), inside], out_specs=[inside, inside], out_shape=[jax.ShapeDtypeStruct((count // 4, rows, width), F32), jax.ShapeDtypeStruct((count // 4, rows, width), BF16)], scratch_shapes=[pltpu.VMEM((count // 2, rows, width), BF16), pltpu.SemaphoreType.DMA((count // 2,))], compiler_params=vmem_limit(8), cost_estimate=weight(2), name='first_half')(self.values, self.taken)

    def finish(self):
        while self.step < lax.axis_size('tensor'):
            self.move()
            self.add()
        return self.kept.reshape(self.kept.shape[-2:])


def sum_parts(values, axis):
    count = lax.axis_size(axis)

    def moved(values, places):
        return lax.ppermute(values, axis, [(place, places(place)) for place in range(count)])
    if axis == 'tensor' and count == 4:
        return [values] + [moved(values, lambda place, bits=bits: place ^ bits) for bits in (1, 2, 3)]
    step = 1
    while step < count and (step == 1 or count > 8):
        values = values + moved(values, lambda place: place ^ step)
        step *= 2
    if step >= count:
        return [values]
    return [values] + [moved(values, lambda place, ahead=ahead: (place + ahead) % count) for ahead in range(2, count, 2)]


def pack_kernel(chan_ref, gate_ref, norm_ref, taps_ref, head_ref, squares_ref, out_ref):
    def turned(values):
        rows, lanes = values.shape
        values = jnp.concatenate([values, jnp.zeros((rows, 128 - lanes), F32)], axis=1) if lanes < 128 else values
        return jnp.transpose(jnp.concatenate([values, jnp.zeros((128 - rows, 128), F32)], axis=0))
    gain_rows = norm_ref.shape[0]
    first = 7 + gain_rows
    out_ref[...] = jnp.zeros_like(out_ref)
    out_ref[0:6, :] = chan_ref[0:6, :]
    out_ref[6:7, :] = gate_ref[...]
    out_ref[7:first, :] = norm_ref[...]
    out_ref[first:first + 5, 0:128] = turned(taps_ref[...])[0:5]
    out_ref[first + 5:first + 7, 0:128] = turned(head_ref[...])[0:2]
    squares = squares_ref[0] + squares_ref[1] + squares_ref[2]
    out_ref[first + 7:first + 8, :] = jnp.full((1, out_ref.shape[1]), squares)


def pack(dchan, gate, norm, taps, heads, squares):
    channels = dchan.shape[1]
    rows = -(-(15 + norm.shape[0]) // 8) * 8
    inside = pl.BlockSpec(memory_space=pltpu.VMEM)
    return pl.pallas_call(pack_kernel, in_specs=[inside] * 5 + [pl.BlockSpec(memory_space=pltpu.SMEM)], out_specs=inside, out_shape=jax.ShapeDtypeStruct((rows, channels), F32), compiler_params=vmem_limit(4), cost_estimate=weight(1), name='pack')(dchan, gate, norm, taps, heads, squares)


def small_sums_kernel(gain_rows, count_tensor, *refs):
    parts, (shared_ref, skip_ref, across_ref) = (refs[:-3], refs[-3:])
    shared = parts[0][...]
    for part in parts[1:]:
        shared = shared + part[...]
    shared_ref[...] = shared
    channels = shared.shape[1]
    first = 7 + gain_rows
    owner = lax.broadcasted_iota(jnp.int32, (channels, 128), 0) // HEAD_DIM
    member = owner == lax.broadcasted_iota(jnp.int32, (channels, 128), 1)
    member = jnp.where(member, 1.0, 0.0).astype(BF16)
    skip = dot_exact(shared[0:8], member)[5:6]
    skip_ref[...] = jnp.broadcast_to(skip, skip_ref.shape)
    squares = jnp.sum(skip * skip) + shared[first + 7, 0]
    for rows in (shared[0:5], shared[6:7], shared[first:first + 7]):
        squares = squares + jnp.sum(rows * rows)
    across_ref[...] = jnp.zeros_like(across_ref)
    across_ref[0:gain_rows, :] = shared[7:first]
    place = lax.axis_index('tensor')
    for other in range(count_tensor):
        across_ref[gain_rows + other:gain_rows + other + 1, :] = jnp.where(place == other, shared[6:7], 0.0)
    last = gain_rows + count_tensor
    across_ref[last:last + 1, :] = jnp.full((1, channels), squares)


def small_sums(parts, gain_rows, count_tensor):
    channels = parts[0].shape[1]
    rows = -(-(gain_rows + count_tensor + 1) // 8) * 8
    return pl.pallas_call(functools.partial(small_sums_kernel, gain_rows, count_tensor), out_shape=[jax.ShapeDtypeStruct(parts[0].shape, F32), jax.ShapeDtypeStruct((8, 128), F32), jax.ShapeDtypeStruct((rows, channels), F32)], compiler_params=vmem_limit(4), cost_estimate=weight(1), name='small_sums')(*parts)


def adam_values(weight_now, first, second, grad, rate, decay):
    first = BETA_ONE * first + (1.0 - BETA_ONE) * grad
    second = BETA_TWO * second + (1.0 - BETA_TWO) * grad * grad
    update = first / (1.0 - BETA_ONE ** STEP) / (jnp.sqrt(second / (1.0 - BETA_TWO ** STEP)) + ADAM_EPS)
    return (weight_now - rate * (update + decay * weight_now), first, second)


def adam_kernel(gain_rows, last, splits, count, *refs):
    across, refs = (refs[:count], refs[count:])
    early_ref, inner_ref, side_ref, refs = (*refs[:3], refs[3:])
    in_refs, out_refs, refs = (refs[:3], refs[3:6], refs[6:])
    conv_grad, conv_refs, head_grad, head_refs, refs = (refs[0], refs[1:4], refs[4], refs[5:8], refs[8:])
    across_ref, norm_ref, refs = (*refs[:2], refs[2:])
    new_in, new_out, new_conv, new_head = (refs[:4], refs[4:8], refs[8:11], refs[11:])
    total = across[0][...]
    for part in across[1:]:
        total = total + part[...]
    across_ref[...] = total
    gains = total[:gain_rows]
    norm = jnp.sqrt(jnp.full((8, 128), total[last, 0] + jnp.sum(gains * gains)))
    factor = CLIP_NORM / jnp.maximum(norm, CLIP_NORM)
    row = lax.broadcasted_iota(jnp.int32, (8, 128), 0)
    norm_ref[...] = jnp.where(row == 0, norm, factor)
    factor = factor[0:1, 0:1]
    inner_cols, columns = splits

    @pl.when(pl.program_id(0) == 0)
    def _():
        for grad, states, news in ((conv_grad, conv_refs, new_conv), (head_grad, head_refs, new_head)):
            values = adam_values(states[0][...], states[1][...], states[2][...], factor * grad[...], RATE_VECTOR, 0.0)
            for new, value in zip(news, values):
                new[...] = value

    def update(lanes, grad, states, news):
        values = adam_values(states[0][:, lanes], states[1][:, lanes], states[2][:, lanes], factor * grad, RATE_MATRIX, DECAY)
        for new, value in zip(news, (*values, values[0].astype(BF16))):
            new[:, lanes] = value
    update(slice(0, inner_cols), early_ref[:, :inner_cols], in_refs, new_in)
    update(slice(inner_cols, 2 * inner_cols), inner_ref[...], in_refs, new_in)
    side = columns - 2 * inner_cols
    update(slice(2 * inner_cols, columns), side_ref[:, :side], in_refs, new_in)
    update(slice(0, inner_cols), early_ref[:, inner_cols:], out_refs, new_out)


def adam_matrices(across, early, inner, side, in_states, out_states, conv, heads, gain_rows, last):
    rows, columns = in_states[0].shape
    inner_cols = inner.shape[1]
    steps = 3 if rows % 48 == 0 else 1

    def by_rows(width):
        return pl.BlockSpec((rows // steps, width), lambda step: (step, 0))

    def fixed(shape):
        return pl.BlockSpec(shape, lambda step: (0, 0))
    in_block, out_block = (by_rows(columns), by_rows(inner_cols))

    def like(shape, dtype=F32):
        return jax.ShapeDtypeStruct(shape, dtype)
    in_shape, out_shape = ((rows, columns), (rows, inner_cols))
    return pl.pallas_call(functools.partial(adam_kernel, gain_rows, last, (inner_cols, columns), len(across)), grid=(steps,), in_specs=[fixed(across[0].shape)] * len(across) + [by_rows(2 * inner_cols), out_block, by_rows(side.shape[1])] + [in_block] * 3 + [out_block] * 3 + [fixed(value.shape) for value in (*conv, *heads)], out_specs=[fixed(across[0].shape), fixed((8, 128))] + [in_block] * 4 + [out_block] * 4 + [fixed(conv[0].shape)] * 3 + [fixed(heads[0].shape)] * 3, out_shape=[like(across[0].shape), like((8, 128))] + [like(in_shape)] * 3 + [like(in_shape, BF16)] + [like(out_shape)] * 3 + [like(out_shape, BF16)] + [like(conv[0].shape)] * 3 + [like(heads[0].shape)] * 3, compiler_params=vmem_limit(24), name='adam_matrices')(*across, early, inner, side, *in_states, *out_states, *conv, *heads)


def deal_out(values):
    count = lax.axis_size('dp')
    own_rows, width = values.shape
    pieces = values.reshape(count, own_rows // count, width)
    return lax.all_to_all(pieces, 'dp', split_axis=0, concat_axis=0, tiled=True)


def deal_in(pieces):
    arrived = lax.all_to_all(pieces, 'dp', split_axis=0, concat_axis=0, tiled=True)
    return arrived.reshape(-1, arrived.shape[-1])


def shards(tokens, cotangent, lengths, order, in_weight, in_first, in_second, out_weight, out_first, out_second, conv_weight, conv_first, conv_second, gain_vector, gain_first, gain_second, head_params, head_first, head_second):
    count_dp = lax.axis_size('dp')
    count_tensor = lax.axis_size('tensor')
    group = lax.axis_index('dp')
    place = lax.axis_index('tensor')
    own_rows, width = tokens.shape
    token_rows = own_rows * count_tensor
    seq_count = token_rows // LEN
    seq_total = order.shape[0]
    head_count = head_params.shape[0]
    padded_heads = -(-head_count // 8) * 8
    inner_cols = head_count * HEAD_DIM
    conv_rows = conv_weight.shape[0]
    state_cols = conv_rows - inner_cols
    inner_total = inner_cols * count_tensor
    norm_gain = gain_vector[:width]
    gate_gain = lax.dynamic_slice_in_dim(gain_vector, width + place * inner_cols, inner_cols, 0)
    gate_gain = gate_gain.reshape(1, inner_cols)
    positions = jnp.arange(seq_total)
    inverse = jnp.sum(jnp.where(order[:, None] == positions[None, :], positions[:, None], 0), axis=0)
    own_seq = place * own_rows // LEN
    sources = inverse[jnp.arange(count_dp) * seq_count + own_seq] // seq_count
    seq_lengths = lax.dynamic_slice_in_dim(lengths, group * seq_count, seq_count, 0)
    live_all = (jnp.arange(LEN)[None, :] < seq_lengths[:, None]).astype(F32).reshape(token_rows, 1)
    live_own = lax.dynamic_slice_in_dim(live_all, place * own_rows, own_rows, 0)
    own = tokens.astype(F32)
    inv_own = lax.rsqrt(jnp.mean(own * own, axis=1, keepdims=True) + EPS_NORM)
    normed_own = (own * inv_own * norm_gain).astype(BF16)
    side_cols = 128
    far = count_dp // 2
    in_low = in_weight.astype(BF16)
    side_real = in_low.shape[1] - 2 * inner_cols
    mixed_shard = jnp.pad(in_low[:, inner_cols:], ((0, 0), (0, side_cols - side_real)))
    normed_blocks = gather_tensor_blocks(normed_own)
    first_bit = count_tensor // 2
    chan = jnp.concatenate([conv_weight[:inner_cols].T, jnp.repeat(head_params[:, 2], HEAD_DIM)[None, :], jnp.zeros((2, inner_cols), F32)], axis=0)
    rate = -jnp.exp(head_params[:, 1])
    heads = jnp.pad(jnp.stack([head_params[:, 0], rate], axis=1), ((0, padded_heads - head_count), (0, 126)))
    state_taps = jnp.pad(conv_weight[inner_cols:], ((0, 0), (0, 3)))
    prepared = (chan, heads, state_taps, gate_gain, live_own)
    late_shard = jnp.concatenate([in_low[:, :inner_cols], out_weight.astype(BF16).T], axis=1)
    mixed_ring = Gather(mixed_shard, True)
    late_ring = Gather(late_shard, False)
    mixed_ring.step()
    cot_first = deal_out(after(cotangent, *mixed_ring.arrived()))
    for k in range(far - 2):
        mixed_ring.step()
    late_ring.step(*mixed_ring.arrived())
    cot_chosen = cot_first.at[sources].get(mode='promise_in_bounds')
    mixed_ring.step(normed_blocks[first_bit], *prepared)
    mixed_ring.wait(cot_chosen)
    in_inner, in_side = mixed_ring.place([inner_cols, side_cols])
    normed_blocks[0] = after(normed_blocks[0], cot_chosen)
    normed = join_tensor(normed_blocks, 30)
    cot_own = deal_in(cot_chosen)
    cot_own = after(cot_own, normed)
    back_out_own = (cot_own.astype(F32) * live_own).astype(BF16)
    back_out_blocks = gather_tensor_blocks(back_out_own)
    side_pre = dot_general_tt(in_side, after(normed, *late_ring.arrived()))
    late_ring.step()
    state_pre = by_sequence(side_pre[:state_cols], seq_count)
    step_pre = by_sequence(side_pre[state_cols:state_cols + padded_heads], seq_count)
    state_own = state_forward(state_pre, state_taps, seq_count)
    states = join_tensor(gather_tensor_blocks(from_sequence(state_own, seq_count)))
    states = by_sequence(states, seq_count)
    inner_pre = dot_nn(after(normed, side_pre, *late_ring.arrived()), in_inner).astype(BF16)
    for _ in range(far - 3):
        late_ring.step()
    late_ring.wait(back_out_own)
    inner_pre = after(inner_pre, *late_ring.arrived())
    late_ring.step()
    scanned, conv, entry = scan_forward(inner_pre, states, step_pre, chan, heads, head_count)
    late_ring.wait(scanned)
    in_gate, out_low = late_ring.place([inner_cols, inner_cols])
    back_out = join_tensor(back_out_blocks)
    gate_pre = lax.optimization_barrier(dot_nn(normed, in_gate).astype(BF16)).astype(F32)
    scanned = scanned.astype(F32)
    gate_sigmoid = jax.nn.sigmoid(gate_pre)
    gate = gate_pre * gate_sigmoid
    mixed = scanned * gate
    back_normed = lax.optimization_barrier(dot_nn(back_out, out_low).astype(BF16)).astype(F32)
    row_sums = jnp.stack([jnp.sum(mixed * mixed, axis=1), jnp.sum(back_normed * gate_gain * mixed, axis=1)])
    unscaled_out = (mixed * gate_gain).astype(BF16)
    row_sums, *others = sum_parts(row_sums, 'tensor')
    partial_out = lax.optimization_barrier(dot_nt(after(unscaled_out, row_sums), out_low).astype(BF16))
    branch = Halving(partial_out)
    row_sums = sum(after_all(others, branch.given), row_sums)
    gate_inv = lax.rsqrt(row_sums[0] / inner_total + EPS_NORM)[:, None]
    gate_rows = row_sums[1][:, None]
    scaled = mixed * gate_inv
    normed_out = lax.optimization_barrier((scaled * gate_gain).astype(BF16))
    grad_gate_gain = jnp.sum(back_normed * scaled, axis=0)
    back_mixed = gate_inv * (back_normed * gate_gain) - mixed * (gate_inv ** 3 * (gate_rows / inner_total))
    back_gate = (back_mixed * scanned * (gate_sigmoid * (1.0 + gate_pre * (1.0 - gate_sigmoid)))).astype(BF16)
    grad_gate_full, grad_out_full = lax.optimization_barrier((dot_tn(normed, back_gate).astype(BF16), dot_tn(back_out, normed_out).astype(BF16)))
    early = Scatter((grad_gate_full, grad_out_full), False)
    dy = (back_mixed * gate).astype(BF16)
    held = ()
    back_parts = 2 if head_count % 4 == 0 else 1
    for part in range(back_parts):
        dy = after(dy, *early.going(), *held)
        held = scan_backward(dy, inner_pre, conv, states, step_pre, entry, chan, heads, head_count, part, back_parts, held)
        early.move()
        count = len(held)
        together = lax.optimization_barrier((*held, *early.going()))
        early.arrive(together[count:])
        held = together[:count]
        early.add()
    back_inner, back_states, back_step, dchan, dhead = held
    tok = ()
    tok = (fence(*early.going()),)
    going = early.going()
    early.move()
    if tok:
        early.wait(*tok)
    inner = Scatter([lax.optimization_barrier(dot_tn(normed, after(back_inner, *(tok or going))).astype(BF16))], True)
    tok = (fence(*inner.going()),)
    inner.move()
    inner.wait(*tok)
    state_kept, state_given = scatter_tensor_split(from_sequence(after(back_states, *tok), seq_count).reshape(count_tensor, state_cols, token_rows), 1)
    state_back = state_kept.astype(F32) + scatter_tensor_move(state_given, 1).astype(F32)
    step = 2
    while step < count_tensor:
        state_back = scatter_tensor_step(state_back, step)
        step *= 2
    state_back = state_back[0]
    tie = (state_given,)
    back_main = lax.optimization_barrier(dot_nt(after(back_gate, *tie), in_gate) + dot_nt(after(back_inner, *tie), in_inner))

    def both():
        inner.wait(back_main, *early.going())
        inner.add()
        early.add()
        early.move()
        inner.move()
    both()
    back_state_pre, dtaps_state = state_backward(by_sequence(state_back, seq_count), state_pre, state_taps, seq_count)
    back_step = from_sequence(back_step, seq_count)[:head_count].astype(BF16)
    back_side = jnp.concatenate([from_sequence(back_state_pre, seq_count), back_step, jnp.zeros((side_cols - side_real, token_rows), BF16)], axis=0)
    back_input = (back_main + dot_general_tt(back_side, in_side)).astype(BF16)
    back_sum = Halving(back_input)
    back_sum.move()
    grad_side = dot_general_tt(normed, after(back_side, back_sum.given)).astype(BF16)
    grad_side = grad_side.reshape(count_dp, -1, side_cols)

    def a2a(g):
        return lax.all_to_all(g, 'dp', split_axis=0, concat_axis=0, tiled=True)
    grad_side = a2a(grad_side)
    back_sum.wait(branch.given)
    back_sum.add()
    inner.wait(back_sum.given)
    inner.add()
    back_part = back_sum.finish()
    branch.move()
    branch.wait(*inner.going())
    branch.add()
    gate_own = lax.dynamic_slice_in_dim(gate_inv, place * own_rows, own_rows, 0)
    layer_output = (live_own * (own + gate_own * branch.finish())).astype(BF16)
    inner_last = inner.going()
    while inner.distance > 1:
        while early.distance > inner.distance - 1:
            early.add()
            early.move()
        inner.move()
        inner.wait(branch.given)
        inner.add()
    inner.move()
    early.wait(*inner_last)
    while early.distance > 0:
        early.add()
        early.move()
    grad_early = early.end()
    inner.wait(grad_early)
    grad_side = jnp.sum(grad_side.astype(F32), axis=0)
    grad_inner = inner.end()
    row_term = jnp.sum(back_part * norm_gain * own, axis=1, keepdims=True)
    back_own = inv_own * norm_gain * back_part - own * inv_own ** 3 * (row_term / width)
    input_grad = (live_own * cot_own.astype(F32) + back_own).astype(BF16)
    grad_norm_gain = jnp.sum(back_part * own * inv_own, axis=0)
    squares = jnp.stack([jnp.sum(grad_early * grad_early), jnp.sum(grad_inner * grad_inner), jnp.sum(grad_side * grad_side)])
    gain_rows = width // inner_cols
    shared = pack(dchan, grad_gate_gain[None, :], grad_norm_gain.reshape(gain_rows, inner_cols), dtaps_state, dhead, squares)
    shared = sum_parts(shared, 'dp')
    shared, skip, across = small_sums(shared, gain_rows, count_tensor)
    first = 7 + gain_rows
    grad_conv = jnp.concatenate([shared[:5], shared[first:first + 5, :state_cols]], axis=1)
    head_rows = shared[first + 5:first + 7, :head_count]
    grad_head = jnp.concatenate([head_rows, skip[:1, :head_count]], axis=0)
    across = after(across, layer_output)
    last = gain_rows + count_tensor
    across, norms, *updated = adam_matrices(sum_parts(across, 'tensor'), grad_early, grad_inner, grad_side, (in_weight, in_first, in_second), (out_weight.T, out_first.T, out_second.T), (grad_conv, conv_weight.T, conv_first.T, conv_second.T), (grad_head, head_params.T, head_first.T, head_second.T), gain_rows, last)
    grad_norm, factor = (norms[0, 0], norms[1, 0])
    grad_gains = across[:last].reshape(-1)
    new_in, in_copy = (updated[:3], updated[3])
    new_out, out_copy = ([values.T for values in updated[4:7]], updated[7].T)
    new_conv = [values.T for values in updated[8:11]]
    new_head = [values.T for values in updated[11:]]
    new_gain = adam_step(gain_vector, gain_first, gain_second, factor * grad_gains, RATE_VECTOR, 0.0)
    return (layer_output, input_grad, grad_norm, *new_in, *new_out, *new_conv, *new_gain, *new_head, in_copy, out_copy)


def solution(mesh):
    rows = P(('dp', 'tensor'), None)
    in_matrix = P('dp', 'tensor')
    out_matrix = P('tensor', 'dp')
    by_tensor = P('tensor', None)
    same = P()
    in_specs = (rows, rows, same, same) + (in_matrix,) * 3 + (out_matrix,) * 3 + (by_tensor,) * 3 + (same,) * 3 + (by_tensor,) * 3
    out_specs = (rows, rows, same) + (in_matrix,) * 3 + (out_matrix,) * 3 + (by_tensor,) * 3 + (same,) * 3 + (by_tensor,) * 3 + (in_matrix, out_matrix)
    return jax.shard_map(shards, mesh=mesh, in_specs=in_specs, out_specs=out_specs, check_vma=False)
```

```python
import functools
import jax
import jax.numpy as jnp
from jax import lax
from jax.experimental import pallas as pl
from jax.experimental.pallas import tpu as pltpu
from jax.sharding import PartitionSpec as P
HEAD_DIM = 64
STATE = 128
LEN = 1024
STEP = 5
CHUNK = 128
PAIR = 2 * HEAD_DIM
EPS_NORM = 1e-05
BETA_ONE = 0.5
BETA_TWO = 0.5
ADAM_EPS = 1e-08
DECAY = 0.1
RATE_MATRIX = 0.02
RATE_VECTOR = 0.8
CLIP_NORM = 1.0
HIGHEST_PRECISION = lax.Precision.HIGHEST
MASKED = -1e+30
BF16 = jnp.bfloat16
F32 = jnp.float32


def sigmoid(values):
    return 1.0 / (1.0 + jnp.exp(-values))


def softplus(values):
    return jnp.maximum(values, 0.0) + jnp.log1p(jnp.exp(-jnp.abs(values)))


def vmem_limit(mebibytes):
    return pltpu.CompilerParams(vmem_limit_bytes=mebibytes * 1024 * 1024)


def in_hbm(values):
    return pltpu.with_memory_space_constraint(values, pltpu.HBM)


def weight(microseconds):
    return pl.CostEstimate(flops=microseconds * 10 ** 9, bytes_accessed=0, transcendentals=0)


def dot_nn(left, right):
    return lax.dot_general(left, right, (((1,), (0,)), ((), ())), preferred_element_type=F32)


def dot_nt(left, right):
    return lax.dot_general(left, right, (((1,), (1,)), ((), ())), preferred_element_type=F32)


def dot_tn(left, right):
    return lax.dot_general(left, right, (((0,), (0,)), ((), ())), preferred_element_type=F32)


def dot_general_tt(left, right):
    return lax.dot_general(left, right, (((0,), (1,)), ((), ())), preferred_element_type=F32)


def by_sequence(values, seq_count):
    if seq_count == 1:
        return values
    rows = values.shape[0]
    return jnp.swapaxes(values.reshape(rows, seq_count, LEN), 0, 1).reshape(-1, LEN)


def from_sequence(values, seq_count):
    if seq_count == 1:
        return values
    rows = values.shape[0] // seq_count
    return jnp.swapaxes(values.reshape(seq_count, rows, LEN), 0, 1).reshape(rows, -1)


def dot_exact(left, right):
    high = left.astype(BF16)
    rest = left - high.astype(F32)
    middle = rest.astype(BF16)
    low = (rest - middle.astype(F32)).astype(BF16)
    rows = left.shape[0]
    product = dot_nn(jnp.concatenate([high, middle, low], axis=0), right)
    return product[:rows] + product[rows:2 * rows] + product[2 * rows:]


def square_places():
    row = lax.broadcasted_iota(jnp.int32, (CHUNK, CHUNK), 0)
    column = lax.broadcasted_iota(jnp.int32, (CHUNK, CHUNK), 1)
    return (row, column)


def chunk_logs(step_ref, head_ref):
    biased = step_ref[...] + head_ref[:, 0:1]
    step = softplus(biased)
    row, column = square_places()
    upto = jnp.where(row <= column, 1.0, 0.0).astype(BF16)
    logs = dot_exact(step * head_ref[:, 1:2], upto)
    padding = jnp.zeros((CHUNK - step.shape[0], CHUNK), F32)
    step_rows = jnp.transpose(jnp.concatenate([step, padding], axis=0))
    logs_rows = jnp.transpose(jnp.concatenate([logs, padding], axis=0))
    return (biased, step, logs, step_rows, logs_rows)


def spread(columns, head):
    return jnp.broadcast_to(columns[:, head:head + 1], (CHUNK, CHUNK))


def scan_forward_kernel(head_count, x_ref, bc_ref, step_ref, chan_ref, head_ref, y_ref, xc_ref, entry_ref, rows, state, fresh):

    @pl.when(pl.program_id(1) == 0)
    def _():
        state[...] = jnp.zeros_like(state)
        rows[0:8, :] = jnp.zeros((8, rows.shape[1]), F32)
    rows[8:8 + CHUNK, :] = x_ref[...].astype(F32)
    entry_ref[0, 0] = state[...].astype(BF16)
    _, _, logs, step_rows, logs_rows = chunk_logs(step_ref, head_ref)
    in_columns = bc_ref[:STATE, :]
    state_out = jnp.transpose(bc_ref[STATE:, :])
    scores = dot_nn(state_out, in_columns)
    row, column = square_places()
    first_half = column < HEAD_DIM
    later = row >= column
    for pair in range(head_count // 2):
        lanes = slice(pair * PAIR, (pair + 1) * PAIR)
        conv = chan_ref[4:5, lanes]
        for tap in range(4):
            conv = conv + chan_ref[tap:tap + 1, lanes] * rows[5 + tap:5 + tap + CHUNK, lanes]
        xc_ref[:, lanes] = conv.astype(BF16)
        values = conv * sigmoid(conv)
        even, odd = (2 * pair, 2 * pair + 1)
        step_pair = jnp.where(first_half, spread(step_rows, even), spread(step_rows, odd))
        logs_even, logs_odd = (spread(logs_rows, even), spread(logs_rows, odd))
        logs_pair = jnp.where(first_half, logs_even, logs_odd)
        within_even = jnp.exp(jnp.where(later, logs_even - logs[even:even + 1, :], MASKED))
        within_odd = jnp.exp(jnp.where(later, logs_odd - logs[odd:odd + 1, :], MASKED))
        mixing = jnp.concatenate([(scores * within_even).astype(BF16), (scores * within_odd).astype(BF16)], axis=1)
        weighted = step_pair * values
        zero = jnp.zeros_like(weighted)
        stacked = jnp.concatenate([jnp.where(first_half, weighted, zero).astype(BF16), jnp.where(first_half, zero, weighted).astype(BF16)], axis=0)
        inner = dot_nn(mixing, stacked)
        outer = dot_nn(state_out, entry_ref[0, 0, :, lanes]) * jnp.exp(logs_pair)
        y_ref[:, lanes] = (inner + outer + chan_ref[5:6, lanes] * values).astype(BF16)
        last = logs_pair[CHUNK - 1:CHUNK, :]
        fresh[:, lanes] = (jnp.exp(last - logs_pair) * weighted).astype(BF16)
        state[:, lanes] = jnp.exp(last) * state[:, lanes]
    state[...] += dot_nn(in_columns, fresh[...])
    rows[0:8, :] = rows[CHUNK:CHUNK + 8, :]


def scan_backward_kernel(first_head, head_count, dy_ref, x_ref, xc_ref, bc_ref, step_ref, entry_ref, chan_ref, head_ref, *outputs_and_scratch):
    dx_ref, dbc_ref, dstep_ref, dchan_ref, dhead_ref, rows, back, leaving, arriving, sums_one, sums_two, sums_three, crossings, decays = outputs_and_scratch[-14:]
    sums_before = outputs_and_scratch[2:-14]

    @pl.when(pl.program_id(1) == 0)
    def _():
        back[...] = jnp.zeros_like(back)
        rows[CHUNK:CHUNK + 8, :] = jnp.zeros((8, rows.shape[1]), F32)

    @pl.when((pl.program_id(0) == 0) & (pl.program_id(1) == 0))
    def _():
        dchan_ref[...] = jnp.zeros_like(dchan_ref)
        dhead_ref[...] = sums_before[2][...] if sums_before else jnp.zeros_like(dhead_ref)
    padded = step_ref.shape[0]
    biased, step, logs, step_rows, logs_rows = chunk_logs(step_ref, head_ref)
    in_columns = bc_ref[:STATE, :]
    out_columns = bc_ref[STATE:, :]
    state_in = jnp.transpose(in_columns)
    state_out = jnp.transpose(out_columns)
    scores = dot_nn(state_in, out_columns)
    back_low = back[...].astype(BF16)
    entry = entry_ref[0, 0]
    row, column = square_places()
    first_half = column < HEAD_DIM
    later = column >= row
    head_row = lax.broadcasted_iota(jnp.int32, (padded, CHUNK), 0)
    wide_row = lax.broadcasted_iota(jnp.int32, (head_count * CHUNK, CHUNK), 0) // CHUNK
    wide_column = lax.broadcasted_iota(jnp.int32, (head_count * CHUNK, CHUNK), 1)
    total = jnp.zeros((CHUNK, CHUNK), F32)
    over_rows = jnp.zeros((padded, CHUNK), F32)
    for pair in range(head_count // 2):
        lanes = slice(pair * PAIR, (pair + 1) * PAIR)
        even = first_head + 2 * pair
        odd = even + 1
        conv = xc_ref[:, lanes].astype(F32)
        gate = sigmoid(conv)
        values = conv * gate
        dy_low = dy_ref[:, lanes]
        dy = dy_low.astype(F32)
        step_pair = jnp.where(first_half, spread(step_rows, even), spread(step_rows, odd))
        logs_even, logs_odd = (spread(logs_rows, even), spread(logs_rows, odd))
        logs_pair = jnp.where(first_half, logs_even, logs_odd)
        weighted = step_pair * values
        zero = jnp.zeros_like(weighted)
        dy_stacked = jnp.concatenate([jnp.where(first_half, dy, zero).astype(BF16), jnp.where(first_half, zero, dy).astype(BF16)], axis=0)
        transfers = []
        for head, log_column, part in ((even, logs_even, jnp.where(first_half, weighted, zero).astype(BF16)), (odd, logs_odd, jnp.where(first_half, zero, weighted).astype(BF16))):
            within = jnp.exp(jnp.where(later, logs[head:head + 1, :] - log_column, MASKED))
            product = within * dot_nt(part, dy_low)
            total = total + product
            crossing = (scores * product).astype(BF16)
            local = head - first_head
            crossings[:, local * CHUNK:(local + 1) * CHUNK] = crossing
            sums = jnp.sum(crossing.astype(F32), axis=0, keepdims=True)
            over_rows = jnp.where(head_row == head, sums, over_rows)
            transfers.append((scores * within).astype(BF16))
        grown = jnp.exp(logs_pair)
        last = logs_pair[CHUNK - 1:CHUNK, :]
        decays[0:1, lanes] = jnp.exp(last)
        to_end = jnp.exp(last - logs_pair)
        from_end = to_end * dot_nn(state_in, back_low[:, lanes])
        dweighted = dot_nn(jnp.concatenate(transfers, axis=1), dy_stacked) + from_end
        grown_dy = grown * dy
        leaving[:, lanes] = grown_dy.astype(BF16)
        arriving[:, lanes] = (to_end * weighted).astype(BF16)
        sums_one[:, lanes] = (grown_dy * dot_nn(state_out, entry[:, lanes])).astype(BF16)
        sums_two[:, lanes] = (weighted * from_end).astype(BF16)
        sums_three[:, lanes] = (values * dweighted).astype(BF16)
        dvalues = step_pair * dweighted + chan_ref[5:6, lanes] * dy
        dconv = dvalues * (gate * (1.0 + conv * (1.0 - gate)))
        rows[0:CHUNK, lanes] = dconv
        dchan_ref[5:6, lanes] += jnp.sum(dy * values, axis=0, keepdims=True)
        dchan_ref[4:5, lanes] += jnp.sum(dconv, axis=0, keepdims=True)
        raw = x_ref[:, lanes].astype(F32)
        dx = jnp.zeros((CHUNK, PAIR), F32)
        for tap in range(4):
            shifted = rows[3 - tap:3 - tap + CHUNK, lanes]
            dx = dx + chan_ref[tap:tap + 1, lanes] * shifted
            dchan_ref[tap:tap + 1, lanes] += jnp.sum(raw * shifted, axis=0, keepdims=True)
        dx_ref[:, lanes] = dx.astype(BF16)
    rows[CHUNK:CHUNK + 8, :] = rows[0:8, :]
    total_low = total.astype(BF16)
    dstate_in = dot_nt(out_columns, total_low) + dot_nt(back_low, arriving[...])
    dstate_out = dot_nn(in_columns, total_low) + dot_nt(entry, leaving[...])
    if sums_before:
        dstate_in = dstate_in + sums_before[0][:STATE, :].astype(F32)
        dstate_out = dstate_out + sums_before[0][STATE:, :].astype(F32)
    dbc_ref[:STATE, :] = dstate_in.astype(BF16)
    dbc_ref[STATE:, :] = dstate_out.astype(BF16)
    channels = back.shape[1]
    owner = first_head + lax.broadcasted_iota(jnp.int32, (padded, channels), 1) // HEAD_DIM
    member = owner == lax.broadcasted_iota(jnp.int32, (padded, channels), 0)
    member = jnp.where(member, 1.0, 0.0).astype(BF16)
    from_entry = dot_nt(member, sums_one[...])
    to_exit = dot_nt(member, sums_two[...])
    step_direct = dot_nt(member, sums_three[...])
    decayed = decays[0:1, :] * back[...]
    carried = jnp.sum(decayed * entry.astype(F32), axis=0, keepdims=True)
    carried = jnp.broadcast_to(carried, (CHUNK, channels)).astype(BF16)
    carried = dot_nt(member, carried)
    back[...] = decayed + dot_nn(out_columns, leaving[...])
    pick = jnp.where(wide_row + first_head == wide_column, 1.0, 0.0).astype(BF16)
    over_columns = jnp.transpose(dot_nn(crossings[...], pick))[:padded]
    onward = jnp.where(row >= column, 1.0, 0.0).astype(BF16)
    before = jnp.where(row < column, 1.0, 0.0).astype(BF16)
    dlogs = dot_exact(jnp.concatenate([over_rows - over_columns + from_entry, to_exit], axis=1), jnp.concatenate([onward, before], axis=0))
    dlogs = dlogs + carried
    rate = head_ref[:, 1:2]
    dstep = (rate * dlogs + step_direct) * sigmoid(biased)
    dstep_ref[...] = dstep + sums_before[1][...] if sums_before else dstep
    dhead_ref[:, 0:1] += jnp.sum(dstep, axis=1, keepdims=True)
    dhead_ref[:, 1:2] += rate * jnp.sum(step * dlogs, axis=1, keepdims=True)


def chunk_specs(seq_count, channels, padded, reverse):
    chunks = LEN // CHUNK

    def place(seq, chunk):
        return chunks - 1 - chunk if reverse else chunk

    def by_rows(width):
        return pl.BlockSpec((CHUNK, width), lambda seq, chunk: (seq * chunks + place(seq, chunk), 0))
    step_spec = pl.BlockSpec((padded, CHUNK), lambda seq, chunk: (seq, place(seq, chunk)))
    entry_spec = pl.BlockSpec((1, 1, STATE, channels), lambda seq, chunk: (seq, place(seq, chunk), 0, 0))

    def fixed(*shape):
        return pl.BlockSpec(shape, lambda seq, chunk: (0, 0))
    state_spec = pl.BlockSpec((2 * STATE, CHUNK), lambda seq, chunk: (seq, place(seq, chunk)))
    return ((seq_count, chunks), by_rows, step_spec, state_spec, entry_spec, fixed)


def scan_forward(x_pre, states, step_pre, chan, heads, head_count):
    token_rows, channels = x_pre.shape
    padded = heads.shape[0]
    seq_count = token_rows // LEN
    grid, by_rows, step_spec, state_spec, entry_spec, fixed = chunk_specs(seq_count, channels, padded, False)
    return pl.pallas_call(functools.partial(scan_forward_kernel, head_count), grid=grid, in_specs=[by_rows(channels), state_spec, step_spec, fixed(8, channels), fixed(padded, 128)], out_specs=[by_rows(channels), by_rows(channels), entry_spec], out_shape=[jax.ShapeDtypeStruct((token_rows, channels), BF16), jax.ShapeDtypeStruct((token_rows, channels), BF16), jax.ShapeDtypeStruct((seq_count, LEN // CHUNK, STATE, channels), BF16)], scratch_shapes=[pltpu.VMEM((CHUNK + 8, channels), F32), pltpu.VMEM((STATE, channels), F32), pltpu.VMEM((CHUNK, channels), BF16)], compiler_params=vmem_limit(16), cost_estimate=weight(11), name='scan_forward')(x_pre, states, step_pre, chan, heads)


def scan_backward(dy, x_pre, conv, states, step_pre, entry, chan, heads, head_count, part, parts, held):
    token_rows, channels = x_pre.shape
    padded = heads.shape[0]
    seq_count = token_rows // LEN
    part_heads = head_count // parts
    width = channels // parts
    chunks = LEN // CHUNK

    def by_rows(seq, chunk):
        return (seq * chunks + chunks - 1 - chunk, part)
    wide = pl.BlockSpec((CHUNK, width), by_rows)
    step_spec = pl.BlockSpec((padded, CHUNK), lambda seq, chunk: (seq, chunks - 1 - chunk))
    state_spec = pl.BlockSpec((2 * STATE, CHUNK), lambda seq, chunk: (seq, chunks - 1 - chunk))
    entry_spec = pl.BlockSpec((1, 1, STATE, width), lambda seq, chunk: (seq, chunks - 1 - chunk, 0, part))
    chan_spec = pl.BlockSpec((8, width), lambda seq, chunk: (0, part))
    head_spec = pl.BlockSpec((padded, 128), lambda seq, chunk: (0, 0))
    low_rows = pltpu.VMEM((CHUNK, width), BF16)
    in_specs = [wide, wide, wide, state_spec, step_spec, entry_spec, chan_spec, head_spec]
    in_place = {}
    if held:
        in_place = {len(in_specs): 0, len(in_specs) + 1: 3}
        dx, dbc, dstep, dchan, dhead = held
        held = (dx, dchan, dbc, dstep, dhead)
        in_specs = in_specs + [pl.BlockSpec(memory_space=pl.ANY)] * 2
        in_specs = in_specs + [state_spec, step_spec, head_spec]
    return pl.pallas_call(functools.partial(scan_backward_kernel, part * part_heads, part_heads), grid=(seq_count, chunks), in_specs=in_specs, out_specs=[wide, state_spec, step_spec, chan_spec, head_spec], out_shape=[jax.ShapeDtypeStruct((token_rows, channels), BF16), jax.ShapeDtypeStruct((seq_count * 2 * STATE, LEN), BF16), jax.ShapeDtypeStruct((seq_count * padded, LEN), F32), jax.ShapeDtypeStruct((8, channels), F32), jax.ShapeDtypeStruct((padded, 128), F32)], scratch_shapes=[pltpu.VMEM((CHUNK + 8, width), F32), pltpu.VMEM((STATE, width), F32), low_rows, low_rows, low_rows, low_rows, low_rows, pltpu.VMEM((CHUNK, part_heads * CHUNK), BF16), pltpu.VMEM((8, width), F32)], input_output_aliases=in_place, compiler_params=vmem_limit(16), cost_estimate=weight(20), name='scan_backward')(dy, x_pre, conv, states, step_pre, entry, chan, heads, *held)


def lane_shift(values, amount):
    if amount == 0:
        return values
    lane = lax.broadcasted_iota(jnp.int32, values.shape, 1)
    if amount > 0:
        return jnp.where(lane >= amount, pltpu.roll(values, amount, 1), 0.0)
    return jnp.where(lane < LEN + amount, pltpu.roll(values, LEN + amount, 1), 0.0)


def state_conv(pre, taps_ref):
    conv = jnp.broadcast_to(taps_ref[:, 4:5], pre.shape)
    for tap in range(4):
        conv = conv + taps_ref[:, tap:tap + 1] * lane_shift(pre, 3 - tap)
    return conv


def state_forward_kernel(pre_ref, taps_ref, states_ref):
    conv = state_conv(pre_ref[...], taps_ref)
    states_ref[...] = (conv * sigmoid(conv)).astype(BF16)


def state_backward_kernel(back_ref, pre_ref, taps_ref, dpre_ref, dtaps_ref):

    @pl.when(pl.program_id(0) == 0)
    def _():
        dtaps_ref[...] = jnp.zeros_like(dtaps_ref)
    pre = pre_ref[...]
    conv = state_conv(pre, taps_ref)
    gate = sigmoid(conv)
    dconv = back_ref[...] * (gate * (1.0 + conv * (1.0 - gate)))
    dpre = jnp.zeros_like(pre)
    for tap in range(4):
        shifted = lane_shift(dconv, tap - 3)
        dpre = dpre + taps_ref[:, tap:tap + 1] * shifted
        dtaps_ref[:, tap:tap + 1] += jnp.sum(pre * shifted, axis=1, keepdims=True)
    dtaps_ref[:, 4:5] += jnp.sum(dconv, axis=1, keepdims=True)
    dpre_ref[...] = dpre.astype(BF16)


def state_forward(pre, taps, seq_count):
    rows = pre.shape[0] // seq_count
    by_seq = pl.BlockSpec((rows, LEN), lambda seq: (seq, 0))
    return pl.pallas_call(state_forward_kernel, grid=(seq_count,), in_specs=[by_seq, pl.BlockSpec((rows, 8), lambda seq: (0, 0))], out_specs=by_seq, out_shape=jax.ShapeDtypeStruct(pre.shape, BF16), compiler_params=vmem_limit(8), name='state_forward')(pre, taps)


def state_backward(back, pre, taps, seq_count):
    rows = pre.shape[0] // seq_count
    by_seq = pl.BlockSpec((rows, LEN), lambda seq: (seq, 0))
    fixed = pl.BlockSpec((rows, 8), lambda seq: (0, 0))
    return pl.pallas_call(state_backward_kernel, grid=(seq_count,), in_specs=[by_seq, by_seq, fixed], out_specs=[by_seq, fixed], out_shape=[jax.ShapeDtypeStruct(pre.shape, BF16), jax.ShapeDtypeStruct((rows, 8), F32)], compiler_params=vmem_limit(8), cost_estimate=weight(3), name='state_backward')(back, pre, taps)


def adam_step(weight, first, second, grad, rate, decay):
    first = BETA_ONE * first + (1.0 - BETA_ONE) * grad
    second = BETA_TWO * second + (1.0 - BETA_TWO) * grad * grad
    update = first / (1.0 - BETA_ONE ** STEP) / (jnp.sqrt(second / (1.0 - BETA_TWO ** STEP)) + ADAM_EPS)
    return (weight - rate * (update + decay * weight), first, second)


def after(value, *others):
    return lax.optimization_barrier((value, *others))[0]


def after_all(values, *others):
    values = tuple(values)
    return lax.optimization_barrier(values + others)[:len(values)]


def tour_dp():
    count = lax.axis_size('dp')
    order = [*range(0, count, 2), *range(count - 1, 0, -2)]
    forth = [(order[i], order[(i + 1) % count]) for i in range(count)]
    back = [(target, source) for source, target in forth]

    def group_at(ahead):
        group = lax.axis_index('dp')
        half = group // 2
        spot = jnp.where(lax.rem(group, 2) == 0, half, count - 1 - half)
        spot = lax.rem(spot + ahead + count, count)
        return jnp.where(spot < count // 2, 2 * spot, 2 * (count - 1 - spot) + 1)
    return (forth, back, group_at, count // 2)


def with_all(pair, *others):
    there = list(after_all(present(pair), *others))
    return tuple((None if part is None else there.pop(0) for part in pair))


def present(pair):
    return [part for part in pair if part is not None]


def gather_step(blocks, step, far_right):
    forth, back, _, far = tour_dp()
    right, left = blocks
    return (lax.ppermute(right, 'dp', forth) if step < far or far_right else None, lax.ppermute(left, 'dp', back) if step < far or not far_right else None)


def place_kernel(starts, widths, *refs):
    blocks, refs = (refs[:len(starts)], refs[len(starts):])
    outs, sem = (refs[:len(widths)], refs[len(widths)])
    copies = []
    for index, (ref, start) in enumerate(zip(blocks, starts)):
        start = pl.multiple_of(start(), 16)
        column = 0
        for out_index, (out, width) in enumerate(zip(outs, widths)):
            copies.append(pltpu.make_async_copy(ref.at[:, column:column + width], out.at[pl.ds(start, ref.shape[0]), :], sem.at[index, out_index]))
            column += width
    for copy in copies:
        copy.start()
    for copy in copies:
        copy.wait()


def place_rows(blocks, starts, widths, cost=2):
    rows = sum((block.shape[0] for block in blocks))
    return pl.pallas_call(functools.partial(place_kernel, starts, widths), in_specs=[pl.BlockSpec(memory_space=pltpu.HBM)] * len(blocks), out_specs=[pl.BlockSpec(memory_space=pltpu.VMEM)] * len(widths), out_shape=[jax.ShapeDtypeStruct((rows, width), blocks[0].dtype) for width in widths], scratch_shapes=[pltpu.SemaphoreType.DMA((len(blocks), len(widths)))], compiler_params=vmem_limit(2), cost_estimate=weight(cost), name='place_rows')(*[in_hbm(block) for block in blocks])


def place_blocks(own, steps, widths):
    _, _, group_at, _ = tour_dp()
    count = lax.axis_size('dp')
    rows = own.shape[0]

    def start(ahead):
        return lambda: group_at(ahead) * rows
    blocks, starts = ([own], [start(0)])
    for step, (right, left) in enumerate(steps, 1):
        if right is not None:
            blocks.append(right)
            starts.append(start(count - step))
        if left is not None:
            blocks.append(left)
            starts.append(start(step))
    return place_rows(blocks, starts, widths)


def fence_kernel(token_ref, out_ref):
    out_ref[...] = token_ref[...]


def fence(*going):
    token = after(jnp.zeros((8, 128), F32), *going)
    return pl.pallas_call(fence_kernel, out_shape=jax.ShapeDtypeStruct((8, 128), F32), compiler_params=vmem_limit(1), cost_estimate=weight(100), name='fence')(token)


class Gather:
    def __init__(self, shard, far_right):
        self.shard = shard
        self.far_right = far_right
        self.moving = (shard, shard)
        self.steps = []

    def step(self, *others):
        moving = with_all(self.moving, *others)
        self.moving = gather_step(moving, len(self.steps) + 1, self.far_right)
        self.steps.append(self.moving)

    def arrived(self):
        return present(self.moving)

    def wait(self, *others):
        self.steps[-1] = self.moving = with_all(self.moving, *others)

    def place(self, widths):
        return place_blocks(self.shard, self.steps, widths)


class Scatter:
    def __init__(self, parts, far_right):
        self.parts = parts
        self.sums = scatter_start(parts, far_right)
        self.distance = lax.axis_size('dp') // 2

    def going(self):
        return present(self.sums)

    def move(self):
        self.sums = scatter_move(self.sums)
        self.distance -= 1

    def wait(self, *others):
        self.sums = with_all(self.sums, *others)

    def arrive(self, sums):
        sums = list(sums)
        self.sums = tuple((None if old is None else sums.pop(0) for old in self.sums))

    def add(self):
        self.sums = scatter_step(self.parts, self.sums, self.distance)

    def end(self):
        return scatter_end(self.parts, self.sums)


def scatter_block(parts, ahead):
    _, _, group_at, _ = tour_dp()
    rows = parts[0].shape[0] // lax.axis_size('dp')
    blocks = [lax.dynamic_slice_in_dim(part, group_at(ahead) * rows, rows, 0) for part in parts]
    return blocks[0] if len(blocks) == 1 else jnp.concatenate(blocks, axis=1)


def scatter_start(parts, far_right):
    _, _, _, far = tour_dp()
    block = scatter_block(parts, far)
    return (block, None) if far_right else (None, block)


def scatter_move(sums):
    forth, back, _, _ = tour_dp()
    right, left = sums
    return (None if right is None else lax.ppermute(right, 'dp', forth), None if left is None else lax.ppermute(left, 'dp', back))


def ring_add_kernel(distance, count, widths, present_sums, *refs):
    sums, refs = (refs[:len(present_sums)], refs[len(present_sums):])
    parts, refs = (refs[:len(widths)], refs[len(widths):])
    outs, blocks, sem = (refs[:2], refs[2], refs[3])
    rows = outs[0].shape[0]
    _, _, group_at, _ = tour_dp()
    copies = []
    for way, ahead in enumerate((distance, count - distance)):
        start = pl.multiple_of(group_at(ahead) * rows, 16)
        column = 0
        for index, (part, width) in enumerate(zip(parts, widths)):
            copies.append(pltpu.make_async_copy(part.at[pl.ds(start, rows), :], blocks.at[way, :, column:column + width], sem.at[way, index]))
            column += width
    for copy in copies:
        copy.start()
    for copy in copies:
        copy.wait()
    for way, out in enumerate(outs):
        block = blocks[way]
        if way in present_sums:
            arrived = sums[present_sums.index(way)][...]
            block = (block.astype(F32) + arrived.astype(F32)).astype(BF16)
        out[...] = block


def scatter_step(parts, sums, distance):
    count = lax.axis_size('dp')
    rows = parts[0].shape[0] // count
    widths = [part.shape[1] for part in parts]
    present_sums = [way for way, arrived in enumerate(sums) if arrived is not None]
    inside = pl.BlockSpec(memory_space=pltpu.VMEM)
    out = jax.ShapeDtypeStruct((rows, sum(widths)), BF16)
    return pl.pallas_call(functools.partial(ring_add_kernel, distance, count, widths, present_sums), in_specs=[inside] * len(present_sums) + [pl.BlockSpec(memory_space=pltpu.HBM)] * len(parts), out_specs=[inside, inside], out_shape=[out, out], scratch_shapes=[pltpu.VMEM((2, rows, sum(widths)), BF16), pltpu.SemaphoreType.DMA((2, len(parts)))], compiler_params=vmem_limit(6), cost_estimate=weight(4), name='ring_add')(*present(sums), *parts)


def scatter_end(parts, sums):
    own = scatter_block(parts, 0).astype(F32)
    for arrived in sums:
        own = own + arrived.astype(F32)
    return own


def gather_tensor_blocks(values):
    count = lax.axis_size('tensor')
    blocks = {0: values}
    step = count // 2
    while step:
        swap = [(i, i ^ step) for i in range(count)]
        blocks.update({bits | step: lax.ppermute(block, 'tensor', swap) for bits, block in blocks.items()})
        step //= 2
    return blocks


def join_tensor(blocks, cost=2):
    rows, width = blocks[0].shape

    def start(bits):
        return lambda: (lax.axis_index('tensor') ^ bits) * rows
    return place_rows(list(blocks.values()), [start(bits) for bits in blocks], [width], cost)[0]


def scatter_tensor_split(values, step):
    side = lax.axis_index('tensor') // step % 2
    values = values.reshape(-1, 2, *values.shape[1:])
    kept = lax.dynamic_index_in_dim(values, side, 1, keepdims=False)
    return (kept, lax.dynamic_index_in_dim(values, 1 - side, 1, keepdims=False).astype(BF16))


def scatter_tensor_move(given, step):
    count = lax.axis_size('tensor')
    return lax.ppermute(given, 'tensor', [(i, i ^ step) for i in range(count)])


def scatter_tensor_step(values, step):
    kept, given = scatter_tensor_split(values, step)
    return kept.astype(F32) + scatter_tensor_move(given, step).astype(F32)


def first_half_kernel(values_ref, taken_ref, kept_ref, given_ref, held, sem):
    place = lax.axis_index('tensor')
    blocks = taken_ref.shape[0]
    copies = [pltpu.make_async_copy(values_ref.at[2 * block + lax.rem(place, 2)], held.at[block], sem.at[block]) for block in range(blocks)]
    for copy in copies:
        copy.start()
    for copy in copies:
        copy.wait()
    side = lax.rem(place // 2, 2)
    for block in range(blocks // 2):
        own, other = (2 * block + side, 2 * block + 1 - side)
        kept_ref[block] = held[own].astype(F32) + taken_ref[own].astype(F32)
        given_ref[block] = (held[other].astype(F32) + taken_ref[other].astype(F32)).astype(BF16)


class Halving:
    def __init__(self, values):
        count = lax.axis_size('tensor')
        self.values = values.reshape(count, -1, values.shape[-1])
        self.given = scatter_tensor_split(self.values, 1)[1]
        self.step = 1

    def move(self):
        self.taken = scatter_tensor_move(self.given, self.step)

    def wait(self, *others):
        self.taken = after(self.taken, *others)

    def add(self):
        count = lax.axis_size('tensor')
        self.step *= 2
        if self.step > 2:
            self.kept = self.kept + self.taken.astype(F32)
            if self.step < count:
                self.kept, self.given = scatter_tensor_split(self.kept, self.step)
            return
        _, rows, width = self.values.shape
        inside = pl.BlockSpec(memory_space=pltpu.VMEM)
        self.kept, self.given = pl.pallas_call(first_half_kernel, in_specs=[pl.BlockSpec(memory_space=pltpu.HBM), inside], out_specs=[inside, inside], out_shape=[jax.ShapeDtypeStruct((count // 4, rows, width), F32), jax.ShapeDtypeStruct((count // 4, rows, width), BF16)], scratch_shapes=[pltpu.VMEM((count // 2, rows, width), BF16), pltpu.SemaphoreType.DMA((count // 2,))], compiler_params=vmem_limit(8), cost_estimate=weight(2), name='first_half')(self.values, self.taken)

    def finish(self):
        while self.step < lax.axis_size('tensor'):
            self.move()
            self.add()
        return self.kept.reshape(self.kept.shape[-2:])


def sum_parts(values, axis):
    count = lax.axis_size(axis)

    def moved(values, places):
        return lax.ppermute(values, axis, [(place, places(place)) for place in range(count)])
    if axis == 'tensor' and count == 4:
        return [values] + [moved(values, lambda place, bits=bits: place ^ bits) for bits in (1, 2, 3)]
    step = 1
    while step < count and (step == 1 or count > 8):
        values = values + moved(values, lambda place: place ^ step)
        step *= 2
    if step >= count:
        return [values]
    return [values] + [moved(values, lambda place, ahead=ahead: (place + ahead) % count) for ahead in range(2, count, 2)]


def pack_kernel(chan_ref, gate_ref, norm_ref, taps_ref, head_ref, squares_ref, out_ref):
    def turned(values):
        rows, lanes = values.shape
        values = jnp.concatenate([values, jnp.zeros((rows, 128 - lanes), F32)], axis=1) if lanes < 128 else values
        return jnp.transpose(jnp.concatenate([values, jnp.zeros((128 - rows, 128), F32)], axis=0))
    gain_rows = norm_ref.shape[0]
    first = 7 + gain_rows
    out_ref[...] = jnp.zeros_like(out_ref)
    out_ref[0:6, :] = chan_ref[0:6, :]
    out_ref[6:7, :] = gate_ref[...]
    out_ref[7:first, :] = norm_ref[...]
    out_ref[first:first + 5, 0:128] = turned(taps_ref[...])[0:5]
    out_ref[first + 5:first + 7, 0:128] = turned(head_ref[...])[0:2]
    squares = squares_ref[0] + squares_ref[1] + squares_ref[2]
    out_ref[first + 7:first + 8, :] = jnp.full((1, out_ref.shape[1]), squares)


def pack(dchan, gate, norm, taps, heads, squares):
    channels = dchan.shape[1]
    rows = -(-(15 + norm.shape[0]) // 8) * 8
    inside = pl.BlockSpec(memory_space=pltpu.VMEM)
    return pl.pallas_call(pack_kernel, in_specs=[inside] * 5 + [pl.BlockSpec(memory_space=pltpu.SMEM)], out_specs=inside, out_shape=jax.ShapeDtypeStruct((rows, channels), F32), compiler_params=vmem_limit(4), cost_estimate=weight(1), name='pack')(dchan, gate, norm, taps, heads, squares)


def small_sums_kernel(gain_rows, count_tensor, *refs):
    parts, (shared_ref, skip_ref, across_ref) = (refs[:-3], refs[-3:])
    shared = parts[0][...]
    for part in parts[1:]:
        shared = shared + part[...]
    shared_ref[...] = shared
    channels = shared.shape[1]
    first = 7 + gain_rows
    owner = lax.broadcasted_iota(jnp.int32, (channels, 128), 0) // HEAD_DIM
    member = owner == lax.broadcasted_iota(jnp.int32, (channels, 128), 1)
    member = jnp.where(member, 1.0, 0.0).astype(BF16)
    skip = dot_exact(shared[0:8], member)[5:6]
    skip_ref[...] = jnp.broadcast_to(skip, skip_ref.shape)
    squares = jnp.sum(skip * skip) + shared[first + 7, 0]
    for rows in (shared[0:5], shared[6:7], shared[first:first + 7]):
        squares = squares + jnp.sum(rows * rows)
    across_ref[...] = jnp.zeros_like(across_ref)
    across_ref[0:gain_rows, :] = shared[7:first]
    place = lax.axis_index('tensor')
    for other in range(count_tensor):
        across_ref[gain_rows + other:gain_rows + other + 1, :] = jnp.where(place == other, shared[6:7], 0.0)
    last = gain_rows + count_tensor
    across_ref[last:last + 1, :] = jnp.full((1, channels), squares)


def small_sums(parts, gain_rows, count_tensor):
    channels = parts[0].shape[1]
    rows = -(-(gain_rows + count_tensor + 1) // 8) * 8
    return pl.pallas_call(functools.partial(small_sums_kernel, gain_rows, count_tensor), out_shape=[jax.ShapeDtypeStruct(parts[0].shape, F32), jax.ShapeDtypeStruct((8, 128), F32), jax.ShapeDtypeStruct((rows, channels), F32)], compiler_params=vmem_limit(4), cost_estimate=weight(1), name='small_sums')(*parts)


def adam_values(weight_now, first, second, grad, rate, decay):
    first = BETA_ONE * first + (1.0 - BETA_ONE) * grad
    second = BETA_TWO * second + (1.0 - BETA_TWO) * grad * grad
    update = first / (1.0 - BETA_ONE ** STEP) / (jnp.sqrt(second / (1.0 - BETA_TWO ** STEP)) + ADAM_EPS)
    return (weight_now - rate * (update + decay * weight_now), first, second)


def adam_kernel(gain_rows, last, splits, count, *refs):
    across, refs = (refs[:count], refs[count:])
    early_ref, inner_ref, side_ref, refs = (*refs[:3], refs[3:])
    in_refs, out_refs, refs = (refs[:3], refs[3:6], refs[6:])
    conv_grad, conv_refs, head_grad, head_refs, refs = (refs[0], refs[1:4], refs[4], refs[5:8], refs[8:])
    across_ref, norm_ref, refs = (*refs[:2], refs[2:])
    new_in, new_out, new_conv, new_head = (refs[:4], refs[4:8], refs[8:11], refs[11:])
    total = across[0][...]
    for part in across[1:]:
        total = total + part[...]
    across_ref[...] = total
    gains = total[:gain_rows]
    norm = jnp.sqrt(jnp.full((8, 128), total[last, 0] + jnp.sum(gains * gains)))
    factor = CLIP_NORM / jnp.maximum(norm, CLIP_NORM)
    row = lax.broadcasted_iota(jnp.int32, (8, 128), 0)
    norm_ref[...] = jnp.where(row == 0, norm, factor)
    factor = factor[0:1, 0:1]
    inner_cols, columns = splits

    @pl.when(pl.program_id(0) == 0)
    def _():
        for grad, states, news in ((conv_grad, conv_refs, new_conv), (head_grad, head_refs, new_head)):
            values = adam_values(states[0][...], states[1][...], states[2][...], factor * grad[...], RATE_VECTOR, 0.0)
            for new, value in zip(news, values):
                new[...] = value

    def update(lanes, grad, states, news):
        values = adam_values(states[0][:, lanes], states[1][:, lanes], states[2][:, lanes], factor * grad, RATE_MATRIX, DECAY)
        for new, value in zip(news, (*values, values[0].astype(BF16))):
            new[:, lanes] = value
    update(slice(0, inner_cols), early_ref[:, :inner_cols], in_refs, new_in)
    update(slice(inner_cols, 2 * inner_cols), inner_ref[...], in_refs, new_in)
    side = columns - 2 * inner_cols
    update(slice(2 * inner_cols, columns), side_ref[:, :side], in_refs, new_in)
    update(slice(0, inner_cols), early_ref[:, inner_cols:], out_refs, new_out)


def adam_matrices(across, early, inner, side, in_states, out_states, conv, heads, gain_rows, last):
    rows, columns = in_states[0].shape
    inner_cols = inner.shape[1]
    steps = 3 if rows % 48 == 0 else 1

    def by_rows(width):
        return pl.BlockSpec((rows // steps, width), lambda step: (step, 0))

    def fixed(shape):
        return pl.BlockSpec(shape, lambda step: (0, 0))
    in_block, out_block = (by_rows(columns), by_rows(inner_cols))

    def like(shape, dtype=F32):
        return jax.ShapeDtypeStruct(shape, dtype)
    in_shape, out_shape = ((rows, columns), (rows, inner_cols))
    return pl.pallas_call(functools.partial(adam_kernel, gain_rows, last, (inner_cols, columns), len(across)), grid=(steps,), in_specs=[fixed(across[0].shape)] * len(across) + [by_rows(2 * inner_cols), out_block, by_rows(side.shape[1])] + [in_block] * 3 + [out_block] * 3 + [fixed(value.shape) for value in (*conv, *heads)], out_specs=[fixed(across[0].shape), fixed((8, 128))] + [in_block] * 4 + [out_block] * 4 + [fixed(conv[0].shape)] * 3 + [fixed(heads[0].shape)] * 3, out_shape=[like(across[0].shape), like((8, 128))] + [like(in_shape)] * 3 + [like(in_shape, BF16)] + [like(out_shape)] * 3 + [like(out_shape, BF16)] + [like(conv[0].shape)] * 3 + [like(heads[0].shape)] * 3, compiler_params=vmem_limit(24), name='adam_matrices')(*across, early, inner, side, *in_states, *out_states, *conv, *heads)


def deal_out(values):
    count = lax.axis_size('dp')
    own_rows, width = values.shape
    pieces = values.reshape(count, own_rows // count, width)
    return lax.all_to_all(pieces, 'dp', split_axis=0, concat_axis=0, tiled=True)


def deal_in(pieces):
    arrived = lax.all_to_all(pieces, 'dp', split_axis=0, concat_axis=0, tiled=True)
    return arrived.reshape(-1, arrived.shape[-1])


def shards(tokens, cotangent, lengths, order, in_weight, in_first, in_second, out_weight, out_first, out_second, conv_weight, conv_first, conv_second, gain_vector, gain_first, gain_second, head_params, head_first, head_second):
    count_dp = lax.axis_size('dp')
    count_tensor = lax.axis_size('tensor')
    group = lax.axis_index('dp')
    place = lax.axis_index('tensor')
    own_rows, width = tokens.shape
    token_rows = own_rows * count_tensor
    seq_count = token_rows // LEN
    seq_total = order.shape[0]
    head_count = head_params.shape[0]
    padded_heads = -(-head_count // 8) * 8
    inner_cols = head_count * HEAD_DIM
    conv_rows = conv_weight.shape[0]
    state_cols = conv_rows - inner_cols
    inner_total = inner_cols * count_tensor
    norm_gain = gain_vector[:width]
    gate_gain = lax.dynamic_slice_in_dim(gain_vector, width + place * inner_cols, inner_cols, 0)
    gate_gain = gate_gain.reshape(1, inner_cols)
    positions = jnp.arange(seq_total)
    inverse = jnp.sum(jnp.where(order[:, None] == positions[None, :], positions[:, None], 0), axis=0)
    own_seq = place * own_rows // LEN
    sources = inverse[jnp.arange(count_dp) * seq_count + own_seq] // seq_count
    seq_lengths = lax.dynamic_slice_in_dim(lengths, group * seq_count, seq_count, 0)
    live_all = (jnp.arange(LEN)[None, :] < seq_lengths[:, None]).astype(F32).reshape(token_rows, 1)
    live_own = lax.dynamic_slice_in_dim(live_all, place * own_rows, own_rows, 0)
    own = tokens.astype(F32)
    inv_own = lax.rsqrt(jnp.mean(own * own, axis=1, keepdims=True) + EPS_NORM)
    normed_own = (own * inv_own * norm_gain).astype(BF16)
    side_cols = 128
    far = count_dp // 2
    in_low = in_weight.astype(BF16)
    side_real = in_low.shape[1] - 2 * inner_cols
    mixed_shard = jnp.pad(in_low[:, inner_cols:], ((0, 0), (0, side_cols - side_real)))
    normed_blocks = gather_tensor_blocks(normed_own)
    first_bit = count_tensor // 2
    chan = jnp.concatenate([conv_weight[:inner_cols].T, jnp.repeat(head_params[:, 2], HEAD_DIM)[None, :], jnp.zeros((2, inner_cols), F32)], axis=0)
    rate = -jnp.exp(head_params[:, 1])
    heads = jnp.pad(jnp.stack([head_params[:, 0], rate], axis=1), ((0, padded_heads - head_count), (0, 126)))
    state_taps = jnp.pad(conv_weight[inner_cols:], ((0, 0), (0, 3)))
    prepared = (chan, heads, state_taps, gate_gain, live_own)
    late_shard = jnp.concatenate([in_low[:, :inner_cols], out_weight.astype(BF16).T], axis=1)
    mixed_ring = Gather(mixed_shard, True)
    late_ring = Gather(late_shard, False)
    mixed_ring.step()
    cot_first = deal_out(after(cotangent, *mixed_ring.arrived()))
    for k in range(far - 2):
        mixed_ring.step()
    late_ring.step(*mixed_ring.arrived())
    cot_chosen = cot_first.at[sources].get(mode='promise_in_bounds')
    mixed_ring.step(normed_blocks[first_bit], *prepared)
    mixed_ring.wait(cot_chosen)
    in_inner, in_side = mixed_ring.place([inner_cols, side_cols])
    normed_blocks[0] = after(normed_blocks[0], cot_chosen)
    normed = join_tensor(normed_blocks, 30)
    cot_own = deal_in(cot_chosen)
    cot_own = after(cot_own, normed)
    back_out_own = (cot_own.astype(F32) * live_own).astype(BF16)
    back_out_blocks = gather_tensor_blocks(back_out_own)
    side_pre = dot_general_tt(in_side, after(normed, *late_ring.arrived()))
    late_ring.step()
    state_pre = by_sequence(side_pre[:state_cols], seq_count)
    step_pre = by_sequence(side_pre[state_cols:state_cols + padded_heads], seq_count)
    state_own = state_forward(state_pre, state_taps, seq_count)
    states = join_tensor(gather_tensor_blocks(from_sequence(state_own, seq_count)))
    states = by_sequence(states, seq_count)
    inner_pre = dot_nn(after(normed, side_pre, *late_ring.arrived()), in_inner).astype(BF16)
    for _ in range(far - 3):
        late_ring.step()
    late_ring.wait(back_out_own)
    inner_pre = after(inner_pre, *late_ring.arrived())
    late_ring.step()
    scanned, conv, entry = scan_forward(inner_pre, states, step_pre, chan, heads, head_count)
    late_ring.wait(scanned)
    in_gate, out_low = late_ring.place([inner_cols, inner_cols])
    back_out = join_tensor(back_out_blocks)
    gate_pre = lax.optimization_barrier(dot_nn(normed, in_gate).astype(BF16)).astype(F32)
    scanned = scanned.astype(F32)
    gate_sigmoid = jax.nn.sigmoid(gate_pre)
    gate = gate_pre * gate_sigmoid
    mixed = scanned * gate
    back_normed = lax.optimization_barrier(dot_nn(back_out, out_low).astype(BF16)).astype(F32)
    row_sums = jnp.stack([jnp.sum(mixed * mixed, axis=1), jnp.sum(back_normed * gate_gain * mixed, axis=1)])
    unscaled_out = (mixed * gate_gain).astype(BF16)
    row_sums, *others = sum_parts(row_sums, 'tensor')
    partial_out = lax.optimization_barrier(dot_nt(after(unscaled_out, row_sums), out_low).astype(BF16))
    branch = Halving(partial_out)
    row_sums = sum(after_all(others, branch.given), row_sums)
    gate_inv = lax.rsqrt(row_sums[0] / inner_total + EPS_NORM)[:, None]
    gate_rows = row_sums[1][:, None]
    scaled = mixed * gate_inv
    normed_out = lax.optimization_barrier((scaled * gate_gain).astype(BF16))
    grad_gate_gain = jnp.sum(back_normed * scaled, axis=0)
    back_mixed = gate_inv * (back_normed * gate_gain) - mixed * (gate_inv ** 3 * (gate_rows / inner_total))
    back_gate = (back_mixed * scanned * (gate_sigmoid * (1.0 + gate_pre * (1.0 - gate_sigmoid)))).astype(BF16)
    grad_gate_full, grad_out_full = lax.optimization_barrier((dot_tn(normed, back_gate).astype(BF16), dot_tn(back_out, normed_out).astype(BF16)))
    early = Scatter((grad_gate_full, grad_out_full), False)
    dy = (back_mixed * gate).astype(BF16)
    held = ()
    back_parts = 2 if head_count % 4 == 0 else 1
    for part in range(back_parts):
        dy = after(dy, *early.going(), *held)
        held = scan_backward(dy, inner_pre, conv, states, step_pre, entry, chan, heads, head_count, part, back_parts, held)
        early.move()
        count = len(held)
        together = lax.optimization_barrier((*held, *early.going()))
        early.arrive(together[count:])
        held = together[:count]
        early.add()
    back_inner, back_states, back_step, dchan, dhead = held
    tok = ()
    tok = (fence(*early.going()),)
    going = early.going()
    early.move()
    if tok:
        early.wait(*tok)
    inner = Scatter([lax.optimization_barrier(dot_tn(normed, after(back_inner, *(tok or going))).astype(BF16))], True)
    tok = (fence(*inner.going()),)
    inner.move()
    inner.wait(*tok)
    state_kept, state_given = scatter_tensor_split(from_sequence(after(back_states, *tok), seq_count).reshape(count_tensor, state_cols, token_rows), 1)
    state_back = state_kept.astype(F32) + scatter_tensor_move(state_given, 1).astype(F32)
    step = 2
    while step < count_tensor:
        state_back = scatter_tensor_step(state_back, step)
        step *= 2
    state_back = state_back[0]
    tie = (state_given,)
    back_main = lax.optimization_barrier(dot_nt(after(back_gate, *tie), in_gate) + dot_nt(after(back_inner, *tie), in_inner))
    third = early.going()
    inner.wait(back_main, *third)
    inner.add()
    early.add()
    early.move()
    inner.move()
    back_state_pre, dtaps_state = state_backward(by_sequence(state_back, seq_count), state_pre, state_taps, seq_count)
    back_step = from_sequence(back_step, seq_count)[:head_count].astype(BF16)
    back_side = jnp.concatenate([from_sequence(back_state_pre, seq_count), back_step, jnp.zeros((side_cols - side_real, token_rows), BF16)], axis=0)
    back_main = after(back_main, *third)
    back_input = (back_main + dot_general_tt(back_side, in_side)).astype(BF16)
    back_sum = Halving(back_input)
    back_sum.move()
    grad_side = dot_general_tt(normed, after(back_side, back_sum.given)).astype(BF16)
    grad_side = grad_side.reshape(count_dp, -1, side_cols)

    def a2a(g):
        return lax.all_to_all(g, 'dp', split_axis=0, concat_axis=0, tiled=True)
    grad_side = a2a(grad_side)
    back_sum.wait(branch.given)
    back_sum.add()
    inner.wait(back_sum.given)
    inner.add()
    back_part = back_sum.finish()
    branch.move()
    branch.wait(*inner.going())
    branch.add()
    gate_own = lax.dynamic_slice_in_dim(gate_inv, place * own_rows, own_rows, 0)
    layer_output = (live_own * (own + gate_own * branch.finish())).astype(BF16)
    inner_last = inner.going()
    while inner.distance > 1:
        while early.distance > inner.distance - 1:
            early.add()
            early.move()
        inner.move()
        inner.wait(branch.given)
        inner.add()
    inner.move()
    early.wait(*inner_last)
    while early.distance > 0:
        early.add()
        early.move()
    grad_early = early.end()
    inner.wait(grad_early)
    grad_side = jnp.sum(grad_side.astype(F32), axis=0)
    grad_inner = inner.end()
    row_term = jnp.sum(back_part * norm_gain * own, axis=1, keepdims=True)
    back_own = inv_own * norm_gain * back_part - own * inv_own ** 3 * (row_term / width)
    input_grad = (live_own * cot_own.astype(F32) + back_own).astype(BF16)
    grad_norm_gain = jnp.sum(back_part * own * inv_own, axis=0)
    squares = jnp.stack([jnp.sum(grad_early * grad_early), jnp.sum(grad_inner * grad_inner), jnp.sum(grad_side * grad_side)])
    gain_rows = width // inner_cols
    shared = pack(dchan, grad_gate_gain[None, :], grad_norm_gain.reshape(gain_rows, inner_cols), dtaps_state, dhead, squares)
    shared = sum_parts(shared, 'dp')
    shared, skip, across = small_sums(shared, gain_rows, count_tensor)
    first = 7 + gain_rows
    grad_conv = jnp.concatenate([shared[:5], shared[first:first + 5, :state_cols]], axis=1)
    head_rows = shared[first + 5:first + 7, :head_count]
    grad_head = jnp.concatenate([head_rows, skip[:1, :head_count]], axis=0)
    across = after(across, layer_output)
    last = gain_rows + count_tensor
    across, norms, *updated = adam_matrices(sum_parts(across, 'tensor'), grad_early, grad_inner, grad_side, (in_weight, in_first, in_second), (out_weight.T, out_first.T, out_second.T), (grad_conv, conv_weight.T, conv_first.T, conv_second.T), (grad_head, head_params.T, head_first.T, head_second.T), gain_rows, last)
    grad_norm, factor = (norms[0, 0], norms[1, 0])
    grad_gains = across[:last].reshape(-1)
    new_in, in_copy = (updated[:3], updated[3])
    new_out, out_copy = ([values.T for values in updated[4:7]], updated[7].T)
    new_conv = [values.T for values in updated[8:11]]
    new_head = [values.T for values in updated[11:]]
    new_gain = adam_step(gain_vector, gain_first, gain_second, factor * grad_gains, RATE_VECTOR, 0.0)
    return (layer_output, input_grad, grad_norm, *new_in, *new_out, *new_conv, *new_gain, *new_head, in_copy, out_copy)


def solution(mesh):
    rows = P(('dp', 'tensor'), None)
    in_matrix = P('dp', 'tensor')
    out_matrix = P('tensor', 'dp')
    by_tensor = P('tensor', None)
    same = P()
    in_specs = (rows, rows, same, same) + (in_matrix,) * 3 + (out_matrix,) * 3 + (by_tensor,) * 3 + (same,) * 3 + (by_tensor,) * 3
    out_specs = (rows, rows, same) + (in_matrix,) * 3 + (out_matrix,) * 3 + (by_tensor,) * 3 + (same,) * 3 + (by_tensor,) * 3 + (in_matrix, out_matrix)
    return jax.shard_map(shards, mesh=mesh, in_specs=in_specs, out_specs=out_specs, check_vma=False)
```

```python
import functools
import jax
import jax.numpy as jnp
from jax import lax
from jax.experimental import pallas as pl
from jax.experimental.pallas import tpu as pltpu
from jax.sharding import PartitionSpec as P
HEAD_DIM = 64
STATE = 128
LEN = 1024
STEP = 5
CHUNK = 128
PAIR = 2 * HEAD_DIM
EPS_NORM = 1e-05
BETA_ONE = 0.5
BETA_TWO = 0.5
ADAM_EPS = 1e-08
DECAY = 0.1
RATE_MATRIX = 0.02
RATE_VECTOR = 0.8
CLIP_NORM = 1.0
HIGHEST_PRECISION = lax.Precision.HIGHEST
MASKED = -1e+30
BF16 = jnp.bfloat16
F32 = jnp.float32


def sigmoid(values):
    return 1.0 / (1.0 + jnp.exp(-values))


def softplus(values):
    return jnp.maximum(values, 0.0) + jnp.log1p(jnp.exp(-jnp.abs(values)))


def vmem_limit(mebibytes):
    return pltpu.CompilerParams(vmem_limit_bytes=mebibytes * 1024 * 1024)


def in_hbm(values):
    return pltpu.with_memory_space_constraint(values, pltpu.HBM)


def weight(microseconds):
    return pl.CostEstimate(flops=microseconds * 10 ** 9, bytes_accessed=0, transcendentals=0)


def dot_nn(left, right):
    return lax.dot_general(left, right, (((1,), (0,)), ((), ())), preferred_element_type=F32)


def dot_nt(left, right):
    return lax.dot_general(left, right, (((1,), (1,)), ((), ())), preferred_element_type=F32)


def dot_tn(left, right):
    return lax.dot_general(left, right, (((0,), (0,)), ((), ())), preferred_element_type=F32)


def dot_general_tt(left, right):
    return lax.dot_general(left, right, (((0,), (1,)), ((), ())), preferred_element_type=F32)


def by_sequence(values, seq_count):
    if seq_count == 1:
        return values
    rows = values.shape[0]
    return jnp.swapaxes(values.reshape(rows, seq_count, LEN), 0, 1).reshape(-1, LEN)


def from_sequence(values, seq_count):
    if seq_count == 1:
        return values
    rows = values.shape[0] // seq_count
    return jnp.swapaxes(values.reshape(seq_count, rows, LEN), 0, 1).reshape(rows, -1)


def dot_exact(left, right):
    high = left.astype(BF16)
    rest = left - high.astype(F32)
    middle = rest.astype(BF16)
    low = (rest - middle.astype(F32)).astype(BF16)
    rows = left.shape[0]
    product = dot_nn(jnp.concatenate([high, middle, low], axis=0), right)
    return product[:rows] + product[rows:2 * rows] + product[2 * rows:]


def square_places():
    row = lax.broadcasted_iota(jnp.int32, (CHUNK, CHUNK), 0)
    column = lax.broadcasted_iota(jnp.int32, (CHUNK, CHUNK), 1)
    return (row, column)


def chunk_logs(step_ref, head_ref):
    biased = step_ref[...] + head_ref[:, 0:1]
    step = softplus(biased)
    row, column = square_places()
    upto = jnp.where(row <= column, 1.0, 0.0).astype(BF16)
    logs = dot_exact(step * head_ref[:, 1:2], upto)
    padding = jnp.zeros((CHUNK - step.shape[0], CHUNK), F32)
    step_rows = jnp.transpose(jnp.concatenate([step, padding], axis=0))
    logs_rows = jnp.transpose(jnp.concatenate([logs, padding], axis=0))
    return (biased, step, logs, step_rows, logs_rows)


def spread(columns, head):
    return jnp.broadcast_to(columns[:, head:head + 1], (CHUNK, CHUNK))


def scan_forward_kernel(head_count, x_ref, bc_ref, step_ref, chan_ref, head_ref, y_ref, xc_ref, entry_ref, rows, state, fresh):

    @pl.when(pl.program_id(1) == 0)
    def _():
        state[...] = jnp.zeros_like(state)
        rows[0:8, :] = jnp.zeros((8, rows.shape[1]), F32)
    rows[8:8 + CHUNK, :] = x_ref[...].astype(F32)
    entry_ref[0, 0] = state[...].astype(BF16)
    _, _, logs, step_rows, logs_rows = chunk_logs(step_ref, head_ref)
    in_columns = bc_ref[:STATE, :]
    state_out = jnp.transpose(bc_ref[STATE:, :])
    scores = dot_nn(state_out, in_columns)
    row, column = square_places()
    first_half = column < HEAD_DIM
    later = row >= column
    for pair in range(head_count // 2):
        lanes = slice(pair * PAIR, (pair + 1) * PAIR)
        conv = chan_ref[4:5, lanes]
        for tap in range(4):
            conv = conv + chan_ref[tap:tap + 1, lanes] * rows[5 + tap:5 + tap + CHUNK, lanes]
        xc_ref[:, lanes] = conv.astype(BF16)
        values = conv * sigmoid(conv)
        even, odd = (2 * pair, 2 * pair + 1)
        step_pair = jnp.where(first_half, spread(step_rows, even), spread(step_rows, odd))
        logs_even, logs_odd = (spread(logs_rows, even), spread(logs_rows, odd))
        logs_pair = jnp.where(first_half, logs_even, logs_odd)
        within_even = jnp.exp(jnp.where(later, logs_even - logs[even:even + 1, :], MASKED))
        within_odd = jnp.exp(jnp.where(later, logs_odd - logs[odd:odd + 1, :], MASKED))
        mixing = jnp.concatenate([(scores * within_even).astype(BF16), (scores * within_odd).astype(BF16)], axis=1)
        weighted = step_pair * values
        zero = jnp.zeros_like(weighted)
        stacked = jnp.concatenate([jnp.where(first_half, weighted, zero).astype(BF16), jnp.where(first_half, zero, weighted).astype(BF16)], axis=0)
        inner = dot_nn(mixing, stacked)
        outer = dot_nn(state_out, entry_ref[0, 0, :, lanes]) * jnp.exp(logs_pair)
        y_ref[:, lanes] = (inner + outer + chan_ref[5:6, lanes] * values).astype(BF16)
        last = logs_pair[CHUNK - 1:CHUNK, :]
        fresh[:, lanes] = (jnp.exp(last - logs_pair) * weighted).astype(BF16)
        state[:, lanes] = jnp.exp(last) * state[:, lanes]
    state[...] += dot_nn(in_columns, fresh[...])
    rows[0:8, :] = rows[CHUNK:CHUNK + 8, :]


def scan_backward_kernel(first_head, head_count, dy_ref, x_ref, xc_ref, bc_ref, step_ref, entry_ref, chan_ref, head_ref, *outputs_and_scratch):
    dx_ref, dbc_ref, dstep_ref, dchan_ref, dhead_ref, rows, back, leaving, arriving, sums_one, sums_two, sums_three, crossings, decays = outputs_and_scratch[-14:]
    sums_before = outputs_and_scratch[2:-14]

    @pl.when(pl.program_id(1) == 0)
    def _():
        back[...] = jnp.zeros_like(back)
        rows[CHUNK:CHUNK + 8, :] = jnp.zeros((8, rows.shape[1]), F32)

    @pl.when((pl.program_id(0) == 0) & (pl.program_id(1) == 0))
    def _():
        dchan_ref[...] = jnp.zeros_like(dchan_ref)
        dhead_ref[...] = sums_before[2][...] if sums_before else jnp.zeros_like(dhead_ref)
    padded = step_ref.shape[0]
    biased, step, logs, step_rows, logs_rows = chunk_logs(step_ref, head_ref)
    in_columns = bc_ref[:STATE, :]
    out_columns = bc_ref[STATE:, :]
    state_in = jnp.transpose(in_columns)
    state_out = jnp.transpose(out_columns)
    scores = dot_nn(state_in, out_columns)
    back_low = back[...].astype(BF16)
    entry = entry_ref[0, 0]
    row, column = square_places()
    first_half = column < HEAD_DIM
    later = column >= row
    head_row = lax.broadcasted_iota(jnp.int32, (padded, CHUNK), 0)
    wide_row = lax.broadcasted_iota(jnp.int32, (head_count * CHUNK, CHUNK), 0) // CHUNK
    wide_column = lax.broadcasted_iota(jnp.int32, (head_count * CHUNK, CHUNK), 1)
    total = jnp.zeros((CHUNK, CHUNK), F32)
    over_rows = jnp.zeros((padded, CHUNK), F32)
    for pair in range(head_count // 2):
        lanes = slice(pair * PAIR, (pair + 1) * PAIR)
        even = first_head + 2 * pair
        odd = even + 1
        conv = xc_ref[:, lanes].astype(F32)
        gate = sigmoid(conv)
        values = conv * gate
        dy_low = dy_ref[:, lanes]
        dy = dy_low.astype(F32)
        step_pair = jnp.where(first_half, spread(step_rows, even), spread(step_rows, odd))
        logs_even, logs_odd = (spread(logs_rows, even), spread(logs_rows, odd))
        logs_pair = jnp.where(first_half, logs_even, logs_odd)
        weighted = step_pair * values
        zero = jnp.zeros_like(weighted)
        dy_stacked = jnp.concatenate([jnp.where(first_half, dy, zero).astype(BF16), jnp.where(first_half, zero, dy).astype(BF16)], axis=0)
        transfers = []
        for head, log_column, part in ((even, logs_even, jnp.where(first_half, weighted, zero).astype(BF16)), (odd, logs_odd, jnp.where(first_half, zero, weighted).astype(BF16))):
            within = jnp.exp(jnp.where(later, logs[head:head + 1, :] - log_column, MASKED))
            product = within * dot_nt(part, dy_low)
            total = total + product
            crossing = (scores * product).astype(BF16)
            local = head - first_head
            crossings[:, local * CHUNK:(local + 1) * CHUNK] = crossing
            sums = jnp.sum(crossing.astype(F32), axis=0, keepdims=True)
            over_rows = jnp.where(head_row == head, sums, over_rows)
            transfers.append((scores * within).astype(BF16))
        grown = jnp.exp(logs_pair)
        last = logs_pair[CHUNK - 1:CHUNK, :]
        decays[0:1, lanes] = jnp.exp(last)
        to_end = jnp.exp(last - logs_pair)
        from_end = to_end * dot_nn(state_in, back_low[:, lanes])
        dweighted = dot_nn(jnp.concatenate(transfers, axis=1), dy_stacked) + from_end
        grown_dy = grown * dy
        leaving[:, lanes] = grown_dy.astype(BF16)
        arriving[:, lanes] = (to_end * weighted).astype(BF16)
        sums_one[:, lanes] = (grown_dy * dot_nn(state_out, entry[:, lanes])).astype(BF16)
        sums_two[:, lanes] = (weighted * from_end).astype(BF16)
        sums_three[:, lanes] = (values * dweighted).astype(BF16)
        dvalues = step_pair * dweighted + chan_ref[5:6, lanes] * dy
        dconv = dvalues * (gate * (1.0 + conv * (1.0 - gate)))
        rows[0:CHUNK, lanes] = dconv
        dchan_ref[5:6, lanes] += jnp.sum(dy * values, axis=0, keepdims=True)
        dchan_ref[4:5, lanes] += jnp.sum(dconv, axis=0, keepdims=True)
        raw = x_ref[:, lanes].astype(F32)
        dx = jnp.zeros((CHUNK, PAIR), F32)
        for tap in range(4):
            shifted = rows[3 - tap:3 - tap + CHUNK, lanes]
            dx = dx + chan_ref[tap:tap + 1, lanes] * shifted
            dchan_ref[tap:tap + 1, lanes] += jnp.sum(raw * shifted, axis=0, keepdims=True)
        dx_ref[:, lanes] = dx.astype(BF16)
    rows[CHUNK:CHUNK + 8, :] = rows[0:8, :]
    total_low = total.astype(BF16)
    dstate_in = dot_nt(out_columns, total_low) + dot_nt(back_low, arriving[...])
    dstate_out = dot_nn(in_columns, total_low) + dot_nt(entry, leaving[...])
    if sums_before:
        dstate_in = dstate_in + sums_before[0][:STATE, :].astype(F32)
        dstate_out = dstate_out + sums_before[0][STATE:, :].astype(F32)
    dbc_ref[:STATE, :] = dstate_in.astype(BF16)
    dbc_ref[STATE:, :] = dstate_out.astype(BF16)
    channels = back.shape[1]
    owner = first_head + lax.broadcasted_iota(jnp.int32, (padded, channels), 1) // HEAD_DIM
    member = owner == lax.broadcasted_iota(jnp.int32, (padded, channels), 0)
    member = jnp.where(member, 1.0, 0.0).astype(BF16)
    from_entry = dot_nt(member, sums_one[...])
    to_exit = dot_nt(member, sums_two[...])
    step_direct = dot_nt(member, sums_three[...])
    decayed = decays[0:1, :] * back[...]
    carried = jnp.sum(decayed * entry.astype(F32), axis=0, keepdims=True)
    carried = jnp.broadcast_to(carried, (CHUNK, channels)).astype(BF16)
    carried = dot_nt(member, carried)
    back[...] = decayed + dot_nn(out_columns, leaving[...])
    pick = jnp.where(wide_row + first_head == wide_column, 1.0, 0.0).astype(BF16)
    over_columns = jnp.transpose(dot_nn(crossings[...], pick))[:padded]
    onward = jnp.where(row >= column, 1.0, 0.0).astype(BF16)
    before = jnp.where(row < column, 1.0, 0.0).astype(BF16)
    dlogs = dot_exact(jnp.concatenate([over_rows - over_columns + from_entry, to_exit], axis=1), jnp.concatenate([onward, before], axis=0))
    dlogs = dlogs + carried
    rate = head_ref[:, 1:2]
    dstep = (rate * dlogs + step_direct) * sigmoid(biased)
    dstep_ref[...] = dstep + sums_before[1][...] if sums_before else dstep
    dhead_ref[:, 0:1] += jnp.sum(dstep, axis=1, keepdims=True)
    dhead_ref[:, 1:2] += rate * jnp.sum(step * dlogs, axis=1, keepdims=True)


def chunk_specs(seq_count, channels, padded, reverse):
    chunks = LEN // CHUNK

    def place(seq, chunk):
        return chunks - 1 - chunk if reverse else chunk

    def by_rows(width):
        return pl.BlockSpec((CHUNK, width), lambda seq, chunk: (seq * chunks + place(seq, chunk), 0))
    step_spec = pl.BlockSpec((padded, CHUNK), lambda seq, chunk: (seq, place(seq, chunk)))
    entry_spec = pl.BlockSpec((1, 1, STATE, channels), lambda seq, chunk: (seq, place(seq, chunk), 0, 0))

    def fixed(*shape):
        return pl.BlockSpec(shape, lambda seq, chunk: (0, 0))
    state_spec = pl.BlockSpec((2 * STATE, CHUNK), lambda seq, chunk: (seq, place(seq, chunk)))
    return ((seq_count, chunks), by_rows, step_spec, state_spec, entry_spec, fixed)


def scan_forward(x_pre, states, step_pre, chan, heads, head_count):
    token_rows, channels = x_pre.shape
    padded = heads.shape[0]
    seq_count = token_rows // LEN
    grid, by_rows, step_spec, state_spec, entry_spec, fixed = chunk_specs(seq_count, channels, padded, False)
    return pl.pallas_call(functools.partial(scan_forward_kernel, head_count), grid=grid, in_specs=[by_rows(channels), state_spec, step_spec, fixed(8, channels), fixed(padded, 128)], out_specs=[by_rows(channels), by_rows(channels), entry_spec], out_shape=[jax.ShapeDtypeStruct((token_rows, channels), BF16), jax.ShapeDtypeStruct((token_rows, channels), BF16), jax.ShapeDtypeStruct((seq_count, LEN // CHUNK, STATE, channels), BF16)], scratch_shapes=[pltpu.VMEM((CHUNK + 8, channels), F32), pltpu.VMEM((STATE, channels), F32), pltpu.VMEM((CHUNK, channels), BF16)], compiler_params=vmem_limit(16), cost_estimate=weight(11), name='scan_forward')(x_pre, states, step_pre, chan, heads)


def scan_backward(dy, x_pre, conv, states, step_pre, entry, chan, heads, head_count, part, parts, held):
    token_rows, channels = x_pre.shape
    padded = heads.shape[0]
    seq_count = token_rows // LEN
    part_heads = head_count // parts
    width = channels // parts
    chunks = LEN // CHUNK

    def by_rows(seq, chunk):
        return (seq * chunks + chunks - 1 - chunk, part)
    wide = pl.BlockSpec((CHUNK, width), by_rows)
    step_spec = pl.BlockSpec((padded, CHUNK), lambda seq, chunk: (seq, chunks - 1 - chunk))
    state_spec = pl.BlockSpec((2 * STATE, CHUNK), lambda seq, chunk: (seq, chunks - 1 - chunk))
    entry_spec = pl.BlockSpec((1, 1, STATE, width), lambda seq, chunk: (seq, chunks - 1 - chunk, 0, part))
    chan_spec = pl.BlockSpec((8, width), lambda seq, chunk: (0, part))
    head_spec = pl.BlockSpec((padded, 128), lambda seq, chunk: (0, 0))
    low_rows = pltpu.VMEM((CHUNK, width), BF16)
    in_specs = [wide, wide, wide, state_spec, step_spec, entry_spec, chan_spec, head_spec]
    in_place = {}
    if held:
        in_place = {len(in_specs): 0, len(in_specs) + 1: 3}
        dx, dbc, dstep, dchan, dhead = held
        held = (dx, dchan, dbc, dstep, dhead)
        in_specs = in_specs + [pl.BlockSpec(memory_space=pl.ANY)] * 2
        in_specs = in_specs + [state_spec, step_spec, head_spec]
    return pl.pallas_call(functools.partial(scan_backward_kernel, part * part_heads, part_heads), grid=(seq_count, chunks), in_specs=in_specs, out_specs=[wide, state_spec, step_spec, chan_spec, head_spec], out_shape=[jax.ShapeDtypeStruct((token_rows, channels), BF16), jax.ShapeDtypeStruct((seq_count * 2 * STATE, LEN), BF16), jax.ShapeDtypeStruct((seq_count * padded, LEN), F32), jax.ShapeDtypeStruct((8, channels), F32), jax.ShapeDtypeStruct((padded, 128), F32)], scratch_shapes=[pltpu.VMEM((CHUNK + 8, width), F32), pltpu.VMEM((STATE, width), F32), low_rows, low_rows, low_rows, low_rows, low_rows, pltpu.VMEM((CHUNK, part_heads * CHUNK), BF16), pltpu.VMEM((8, width), F32)], input_output_aliases=in_place, compiler_params=vmem_limit(16), cost_estimate=weight(20), name='scan_backward')(dy, x_pre, conv, states, step_pre, entry, chan, heads, *held)


def lane_shift(values, amount):
    if amount == 0:
        return values
    lane = lax.broadcasted_iota(jnp.int32, values.shape, 1)
    if amount > 0:
        return jnp.where(lane >= amount, pltpu.roll(values, amount, 1), 0.0)
    return jnp.where(lane < LEN + amount, pltpu.roll(values, LEN + amount, 1), 0.0)


def state_conv(pre, taps_ref):
    conv = jnp.broadcast_to(taps_ref[:, 4:5], pre.shape)
    for tap in range(4):
        conv = conv + taps_ref[:, tap:tap + 1] * lane_shift(pre, 3 - tap)
    return conv


def state_forward_kernel(pre_ref, taps_ref, states_ref):
    conv = state_conv(pre_ref[...], taps_ref)
    states_ref[...] = (conv * sigmoid(conv)).astype(BF16)


def state_backward_kernel(back_ref, pre_ref, taps_ref, dpre_ref, dtaps_ref):

    @pl.when(pl.program_id(0) == 0)
    def _():
        dtaps_ref[...] = jnp.zeros_like(dtaps_ref)
    pre = pre_ref[...]
    conv = state_conv(pre, taps_ref)
    gate = sigmoid(conv)
    dconv = back_ref[...] * (gate * (1.0 + conv * (1.0 - gate)))
    dpre = jnp.zeros_like(pre)
    for tap in range(4):
        shifted = lane_shift(dconv, tap - 3)
        dpre = dpre + taps_ref[:, tap:tap + 1] * shifted
        dtaps_ref[:, tap:tap + 1] += jnp.sum(pre * shifted, axis=1, keepdims=True)
    dtaps_ref[:, 4:5] += jnp.sum(dconv, axis=1, keepdims=True)
    dpre_ref[...] = dpre.astype(BF16)


def state_forward(pre, taps, seq_count):
    rows = pre.shape[0] // seq_count
    by_seq = pl.BlockSpec((rows, LEN), lambda seq: (seq, 0))
    return pl.pallas_call(state_forward_kernel, grid=(seq_count,), in_specs=[by_seq, pl.BlockSpec((rows, 8), lambda seq: (0, 0))], out_specs=by_seq, out_shape=jax.ShapeDtypeStruct(pre.shape, BF16), compiler_params=vmem_limit(8), name='state_forward')(pre, taps)


def state_backward(back, pre, taps, seq_count):
    rows = pre.shape[0] // seq_count
    by_seq = pl.BlockSpec((rows, LEN), lambda seq: (seq, 0))
    fixed = pl.BlockSpec((rows, 8), lambda seq: (0, 0))
    return pl.pallas_call(state_backward_kernel, grid=(seq_count,), in_specs=[by_seq, by_seq, fixed], out_specs=[by_seq, fixed], out_shape=[jax.ShapeDtypeStruct(pre.shape, BF16), jax.ShapeDtypeStruct((rows, 8), F32)], compiler_params=vmem_limit(8), cost_estimate=weight(3), name='state_backward')(back, pre, taps)


def adam_step(weight, first, second, grad, rate, decay):
    first = BETA_ONE * first + (1.0 - BETA_ONE) * grad
    second = BETA_TWO * second + (1.0 - BETA_TWO) * grad * grad
    update = first / (1.0 - BETA_ONE ** STEP) / (jnp.sqrt(second / (1.0 - BETA_TWO ** STEP)) + ADAM_EPS)
    return (weight - rate * (update + decay * weight), first, second)


def after(value, *others):
    return lax.optimization_barrier((value, *others))[0]


def after_all(values, *others):
    values = tuple(values)
    return lax.optimization_barrier(values + others)[:len(values)]


def tour_dp():
    count = lax.axis_size('dp')
    order = [*range(0, count, 2), *range(count - 1, 0, -2)]
    forth = [(order[i], order[(i + 1) % count]) for i in range(count)]
    back = [(target, source) for source, target in forth]

    def group_at(ahead):
        group = lax.axis_index('dp')
        half = group // 2
        spot = jnp.where(lax.rem(group, 2) == 0, half, count - 1 - half)
        spot = lax.rem(spot + ahead + count, count)
        return jnp.where(spot < count // 2, 2 * spot, 2 * (count - 1 - spot) + 1)
    return (forth, back, group_at, count // 2)


def with_all(pair, *others):
    there = list(after_all(present(pair), *others))
    return tuple((None if part is None else there.pop(0) for part in pair))


def present(pair):
    return [part for part in pair if part is not None]


def gather_step(blocks, step, far_right):
    forth, back, _, far = tour_dp()
    right, left = blocks
    return (lax.ppermute(right, 'dp', forth) if step < far or far_right else None, lax.ppermute(left, 'dp', back) if step < far or not far_right else None)


def place_kernel(starts, widths, *refs):
    blocks, refs = (refs[:len(starts)], refs[len(starts):])
    outs, sem = (refs[:len(widths)], refs[len(widths)])
    copies = []
    for index, (ref, start) in enumerate(zip(blocks, starts)):
        start = pl.multiple_of(start(), 16)
        column = 0
        for out_index, (out, width) in enumerate(zip(outs, widths)):
            copies.append(pltpu.make_async_copy(ref.at[:, column:column + width], out.at[pl.ds(start, ref.shape[0]), :], sem.at[index, out_index]))
            column += width
    for copy in copies:
        copy.start()
    for copy in copies:
        copy.wait()


def place_rows(blocks, starts, widths, cost=2):
    rows = sum((block.shape[0] for block in blocks))
    return pl.pallas_call(functools.partial(place_kernel, starts, widths), in_specs=[pl.BlockSpec(memory_space=pltpu.HBM)] * len(blocks), out_specs=[pl.BlockSpec(memory_space=pltpu.VMEM)] * len(widths), out_shape=[jax.ShapeDtypeStruct((rows, width), blocks[0].dtype) for width in widths], scratch_shapes=[pltpu.SemaphoreType.DMA((len(blocks), len(widths)))], compiler_params=vmem_limit(2), cost_estimate=weight(cost), name='place_rows')(*[in_hbm(block) for block in blocks])


def place_blocks(own, steps, widths):
    _, _, group_at, _ = tour_dp()
    count = lax.axis_size('dp')
    rows = own.shape[0]

    def start(ahead):
        return lambda: group_at(ahead) * rows
    blocks, starts = ([own], [start(0)])
    for step, (right, left) in enumerate(steps, 1):
        if right is not None:
            blocks.append(right)
            starts.append(start(count - step))
        if left is not None:
            blocks.append(left)
            starts.append(start(step))
    return place_rows(blocks, starts, widths)


def fence_kernel(token_ref, out_ref):
    out_ref[...] = token_ref[...]


def fence(*going):
    token = after(jnp.zeros((8, 128), F32), *going)
    return pl.pallas_call(fence_kernel, out_shape=jax.ShapeDtypeStruct((8, 128), F32), compiler_params=vmem_limit(1), cost_estimate=weight(100), name='fence')(token)


class Gather:
    def __init__(self, shard, far_right):
        self.shard = shard
        self.far_right = far_right
        self.moving = (shard, shard)
        self.steps = []

    def step(self, *others):
        moving = with_all(self.moving, *others)
        self.moving = gather_step(moving, len(self.steps) + 1, self.far_right)
        self.steps.append(self.moving)

    def arrived(self):
        return present(self.moving)

    def wait(self, *others):
        self.steps[-1] = self.moving = with_all(self.moving, *others)

    def place(self, widths):
        return place_blocks(self.shard, self.steps, widths)


class Scatter:
    def __init__(self, parts, far_right):
        self.parts = parts
        self.sums = scatter_start(parts, far_right)
        self.distance = lax.axis_size('dp') // 2

    def going(self):
        return present(self.sums)

    def move(self):
        self.sums = scatter_move(self.sums)
        self.distance -= 1

    def wait(self, *others):
        self.sums = with_all(self.sums, *others)

    def arrive(self, sums):
        sums = list(sums)
        self.sums = tuple((None if old is None else sums.pop(0) for old in self.sums))

    def add(self):
        self.sums = scatter_step(self.parts, self.sums, self.distance)

    def end(self):
        return scatter_end(self.parts, self.sums)


def scatter_block(parts, ahead):
    _, _, group_at, _ = tour_dp()
    rows = parts[0].shape[0] // lax.axis_size('dp')
    blocks = [lax.dynamic_slice_in_dim(part, group_at(ahead) * rows, rows, 0) for part in parts]
    return blocks[0] if len(blocks) == 1 else jnp.concatenate(blocks, axis=1)


def scatter_start(parts, far_right):
    _, _, _, far = tour_dp()
    block = scatter_block(parts, far)
    return (block, None) if far_right else (None, block)


def scatter_move(sums):
    forth, back, _, _ = tour_dp()
    right, left = sums
    return (None if right is None else lax.ppermute(right, 'dp', forth), None if left is None else lax.ppermute(left, 'dp', back))


def ring_add_kernel(distance, count, widths, present_sums, *refs):
    sums, refs = (refs[:len(present_sums)], refs[len(present_sums):])
    parts, refs = (refs[:len(widths)], refs[len(widths):])
    outs, blocks, sem = (refs[:2], refs[2], refs[3])
    rows = outs[0].shape[0]
    _, _, group_at, _ = tour_dp()
    copies = []
    for way, ahead in enumerate((distance, count - distance)):
        start = pl.multiple_of(group_at(ahead) * rows, 16)
        column = 0
        for index, (part, width) in enumerate(zip(parts, widths)):
            copies.append(pltpu.make_async_copy(part.at[pl.ds(start, rows), :], blocks.at[way, :, column:column + width], sem.at[way, index]))
            column += width
    for copy in copies:
        copy.start()
    for copy in copies:
        copy.wait()
    for way, out in enumerate(outs):
        block = blocks[way]
        if way in present_sums:
            arrived = sums[present_sums.index(way)][...]
            block = (block.astype(F32) + arrived.astype(F32)).astype(BF16)
        out[...] = block


def scatter_step(parts, sums, distance):
    count = lax.axis_size('dp')
    rows = parts[0].shape[0] // count
    widths = [part.shape[1] for part in parts]
    present_sums = [way for way, arrived in enumerate(sums) if arrived is not None]
    inside = pl.BlockSpec(memory_space=pltpu.VMEM)
    out = jax.ShapeDtypeStruct((rows, sum(widths)), BF16)
    return pl.pallas_call(functools.partial(ring_add_kernel, distance, count, widths, present_sums), in_specs=[inside] * len(present_sums) + [pl.BlockSpec(memory_space=pltpu.HBM)] * len(parts), out_specs=[inside, inside], out_shape=[out, out], scratch_shapes=[pltpu.VMEM((2, rows, sum(widths)), BF16), pltpu.SemaphoreType.DMA((2, len(parts)))], compiler_params=vmem_limit(6), cost_estimate=weight(4), name='ring_add')(*present(sums), *parts)


def scatter_end(parts, sums):
    own = scatter_block(parts, 0).astype(F32)
    for arrived in sums:
        own = own + arrived.astype(F32)
    return own


def gather_tensor_blocks(values):
    count = lax.axis_size('tensor')
    blocks = {0: values}
    step = count // 2
    while step:
        swap = [(i, i ^ step) for i in range(count)]
        blocks.update({bits | step: lax.ppermute(block, 'tensor', swap) for bits, block in blocks.items()})
        step //= 2
    return blocks


def join_tensor(blocks, cost=2):
    rows, width = blocks[0].shape

    def start(bits):
        return lambda: (lax.axis_index('tensor') ^ bits) * rows
    return place_rows(list(blocks.values()), [start(bits) for bits in blocks], [width], cost)[0]


def scatter_tensor_split(values, step):
    side = lax.axis_index('tensor') // step % 2
    values = values.reshape(-1, 2, *values.shape[1:])
    kept = lax.dynamic_index_in_dim(values, side, 1, keepdims=False)
    return (kept, lax.dynamic_index_in_dim(values, 1 - side, 1, keepdims=False).astype(BF16))


def scatter_tensor_move(given, step):
    count = lax.axis_size('tensor')
    return lax.ppermute(given, 'tensor', [(i, i ^ step) for i in range(count)])


def scatter_tensor_step(values, step):
    kept, given = scatter_tensor_split(values, step)
    return kept.astype(F32) + scatter_tensor_move(given, step).astype(F32)


def first_half_kernel(values_ref, taken_ref, kept_ref, given_ref, held, sem):
    place = lax.axis_index('tensor')
    blocks = taken_ref.shape[0]
    copies = [pltpu.make_async_copy(values_ref.at[2 * block + lax.rem(place, 2)], held.at[block], sem.at[block]) for block in range(blocks)]
    for copy in copies:
        copy.start()
    for copy in copies:
        copy.wait()
    side = lax.rem(place // 2, 2)
    for block in range(blocks // 2):
        own, other = (2 * block + side, 2 * block + 1 - side)
        kept_ref[block] = held[own].astype(F32) + taken_ref[own].astype(F32)
        given_ref[block] = (held[other].astype(F32) + taken_ref[other].astype(F32)).astype(BF16)


class Halving:
    def __init__(self, values):
        count = lax.axis_size('tensor')
        self.values = values.reshape(count, -1, values.shape[-1])
        self.given = scatter_tensor_split(self.values, 1)[1]
        self.step = 1

    def move(self):
        self.taken = scatter_tensor_move(self.given, self.step)

    def wait(self, *others):
        self.taken = after(self.taken, *others)

    def add(self):
        count = lax.axis_size('tensor')
        self.step *= 2
        if self.step > 2:
            self.kept = self.kept + self.taken.astype(F32)
            if self.step < count:
                self.kept, self.given = scatter_tensor_split(self.kept, self.step)
            return
        _, rows, width = self.values.shape
        inside = pl.BlockSpec(memory_space=pltpu.VMEM)
        self.kept, self.given = pl.pallas_call(first_half_kernel, in_specs=[pl.BlockSpec(memory_space=pltpu.HBM), inside], out_specs=[inside, inside], out_shape=[jax.ShapeDtypeStruct((count // 4, rows, width), F32), jax.ShapeDtypeStruct((count // 4, rows, width), BF16)], scratch_shapes=[pltpu.VMEM((count // 2, rows, width), BF16), pltpu.SemaphoreType.DMA((count // 2,))], compiler_params=vmem_limit(8), cost_estimate=weight(2), name='first_half')(self.values, self.taken)

    def finish(self):
        while self.step < lax.axis_size('tensor'):
            self.move()
            self.add()
        return self.kept.reshape(self.kept.shape[-2:])


def sum_parts(values, axis):
    count = lax.axis_size(axis)

    def moved(values, places):
        return lax.ppermute(values, axis, [(place, places(place)) for place in range(count)])
    if axis == 'tensor' and count == 4:
        return [values] + [moved(values, lambda place, bits=bits: place ^ bits) for bits in (1, 2, 3)]
    step = 1
    while step < count and (step == 1 or count > 8):
        values = values + moved(values, lambda place: place ^ step)
        step *= 2
    if step >= count:
        return [values]
    return [values] + [moved(values, lambda place, ahead=ahead: (place + ahead) % count) for ahead in range(2, count, 2)]


def pack_kernel(chan_ref, gate_ref, norm_ref, taps_ref, head_ref, squares_ref, out_ref):
    def turned(values):
        rows, lanes = values.shape
        values = jnp.concatenate([values, jnp.zeros((rows, 128 - lanes), F32)], axis=1) if lanes < 128 else values
        return jnp.transpose(jnp.concatenate([values, jnp.zeros((128 - rows, 128), F32)], axis=0))
    gain_rows = norm_ref.shape[0]
    first = 7 + gain_rows
    out_ref[...] = jnp.zeros_like(out_ref)
    out_ref[0:6, :] = chan_ref[0:6, :]
    out_ref[6:7, :] = gate_ref[...]
    out_ref[7:first, :] = norm_ref[...]
    out_ref[first:first + 5, 0:128] = turned(taps_ref[...])[0:5]
    out_ref[first + 5:first + 7, 0:128] = turned(head_ref[...])[0:2]
    squares = squares_ref[0] + squares_ref[1] + squares_ref[2]
    out_ref[first + 7:first + 8, :] = jnp.full((1, out_ref.shape[1]), squares)


def pack(dchan, gate, norm, taps, heads, squares):
    channels = dchan.shape[1]
    rows = -(-(15 + norm.shape[0]) // 8) * 8
    inside = pl.BlockSpec(memory_space=pltpu.VMEM)
    return pl.pallas_call(pack_kernel, in_specs=[inside] * 5 + [pl.BlockSpec(memory_space=pltpu.SMEM)], out_specs=inside, out_shape=jax.ShapeDtypeStruct((rows, channels), F32), compiler_params=vmem_limit(4), cost_estimate=weight(1), name='pack')(dchan, gate, norm, taps, heads, squares)


def small_sums_kernel(gain_rows, count_tensor, *refs):
    parts, (shared_ref, skip_ref, across_ref) = (refs[:-3], refs[-3:])
    shared = parts[0][...]
    for part in parts[1:]:
        shared = shared + part[...]
    shared_ref[...] = shared
    channels = shared.shape[1]
    first = 7 + gain_rows
    owner = lax.broadcasted_iota(jnp.int32, (channels, 128), 0) // HEAD_DIM
    member = owner == lax.broadcasted_iota(jnp.int32, (channels, 128), 1)
    member = jnp.where(member, 1.0, 0.0).astype(BF16)
    skip = dot_exact(shared[0:8], member)[5:6]
    skip_ref[...] = jnp.broadcast_to(skip, skip_ref.shape)
    squares = jnp.sum(skip * skip) + shared[first + 7, 0]
    for rows in (shared[0:5], shared[6:7], shared[first:first + 7]):
        squares = squares + jnp.sum(rows * rows)
    across_ref[...] = jnp.zeros_like(across_ref)
    across_ref[0:gain_rows, :] = shared[7:first]
    place = lax.axis_index('tensor')
    for other in range(count_tensor):
        across_ref[gain_rows + other:gain_rows + other + 1, :] = jnp.where(place == other, shared[6:7], 0.0)
    last = gain_rows + count_tensor
    across_ref[last:last + 1, :] = jnp.full((1, channels), squares)


def small_sums(parts, gain_rows, count_tensor):
    channels = parts[0].shape[1]
    rows = -(-(gain_rows + count_tensor + 1) // 8) * 8
    return pl.pallas_call(functools.partial(small_sums_kernel, gain_rows, count_tensor), out_shape=[jax.ShapeDtypeStruct(parts[0].shape, F32), jax.ShapeDtypeStruct((8, 128), F32), jax.ShapeDtypeStruct((rows, channels), F32)], compiler_params=vmem_limit(4), cost_estimate=weight(1), name='small_sums')(*parts)


def adam_values(weight_now, first, second, grad, rate, decay):
    first = BETA_ONE * first + (1.0 - BETA_ONE) * grad
    second = BETA_TWO * second + (1.0 - BETA_TWO) * grad * grad
    update = first / (1.0 - BETA_ONE ** STEP) / (jnp.sqrt(second / (1.0 - BETA_TWO ** STEP)) + ADAM_EPS)
    return (weight_now - rate * (update + decay * weight_now), first, second)


def adam_kernel(gain_rows, last, splits, count, *refs):
    across, refs = (refs[:count], refs[count:])
    early_ref, inner_ref, side_ref, refs = (*refs[:3], refs[3:])
    in_refs, out_refs, refs = (refs[:3], refs[3:6], refs[6:])
    conv_grad, conv_refs, head_grad, head_refs, refs = (refs[0], refs[1:4], refs[4], refs[5:8], refs[8:])
    across_ref, norm_ref, refs = (*refs[:2], refs[2:])
    new_in, new_out, new_conv, new_head = (refs[:4], refs[4:8], refs[8:11], refs[11:])
    total = across[0][...]
    for part in across[1:]:
        total = total + part[...]
    across_ref[...] = total
    gains = total[:gain_rows]
    norm = jnp.sqrt(jnp.full((8, 128), total[last, 0] + jnp.sum(gains * gains)))
    factor = CLIP_NORM / jnp.maximum(norm, CLIP_NORM)
    row = lax.broadcasted_iota(jnp.int32, (8, 128), 0)
    norm_ref[...] = jnp.where(row == 0, norm, factor)
    factor = factor[0:1, 0:1]
    inner_cols, columns = splits

    @pl.when(pl.program_id(0) == 0)
    def _():
        for grad, states, news in ((conv_grad, conv_refs, new_conv), (head_grad, head_refs, new_head)):
            values = adam_values(states[0][...], states[1][...], states[2][...], factor * grad[...], RATE_VECTOR, 0.0)
            for new, value in zip(news, values):
                new[...] = value

    def update(lanes, grad, states, news):
        values = adam_values(states[0][:, lanes], states[1][:, lanes], states[2][:, lanes], factor * grad, RATE_MATRIX, DECAY)
        for new, value in zip(news, (*values, values[0].astype(BF16))):
            new[:, lanes] = value
    update(slice(0, inner_cols), early_ref[:, :inner_cols], in_refs, new_in)
    update(slice(inner_cols, 2 * inner_cols), inner_ref[...], in_refs, new_in)
    side = columns - 2 * inner_cols
    update(slice(2 * inner_cols, columns), side_ref[:, :side], in_refs, new_in)
    update(slice(0, inner_cols), early_ref[:, inner_cols:], out_refs, new_out)


def adam_matrices(across, early, inner, side, in_states, out_states, conv, heads, gain_rows, last):
    rows, columns = in_states[0].shape
    inner_cols = inner.shape[1]
    steps = 3 if rows % 48 == 0 else 1

    def by_rows(width):
        return pl.BlockSpec((rows // steps, width), lambda step: (step, 0))

    def fixed(shape):
        return pl.BlockSpec(shape, lambda step: (0, 0))
    in_block, out_block = (by_rows(columns), by_rows(inner_cols))

    def like(shape, dtype=F32):
        return jax.ShapeDtypeStruct(shape, dtype)
    in_shape, out_shape = ((rows, columns), (rows, inner_cols))
    return pl.pallas_call(functools.partial(adam_kernel, gain_rows, last, (inner_cols, columns), len(across)), grid=(steps,), in_specs=[fixed(across[0].shape)] * len(across) + [by_rows(2 * inner_cols), out_block, by_rows(side.shape[1])] + [in_block] * 3 + [out_block] * 3 + [fixed(value.shape) for value in (*conv, *heads)], out_specs=[fixed(across[0].shape), fixed((8, 128))] + [in_block] * 4 + [out_block] * 4 + [fixed(conv[0].shape)] * 3 + [fixed(heads[0].shape)] * 3, out_shape=[like(across[0].shape), like((8, 128))] + [like(in_shape)] * 3 + [like(in_shape, BF16)] + [like(out_shape)] * 3 + [like(out_shape, BF16)] + [like(conv[0].shape)] * 3 + [like(heads[0].shape)] * 3, compiler_params=vmem_limit(24), name='adam_matrices')(*across, early, inner, side, *in_states, *out_states, *conv, *heads)


def deal_out(values):
    count = lax.axis_size('dp')
    own_rows, width = values.shape
    pieces = values.reshape(count, own_rows // count, width)
    return lax.all_to_all(pieces, 'dp', split_axis=0, concat_axis=0, tiled=True)


def deal_in(pieces):
    arrived = lax.all_to_all(pieces, 'dp', split_axis=0, concat_axis=0, tiled=True)
    return arrived.reshape(-1, arrived.shape[-1])


def shards(tokens, cotangent, lengths, order, in_weight, in_first, in_second, out_weight, out_first, out_second, conv_weight, conv_first, conv_second, gain_vector, gain_first, gain_second, head_params, head_first, head_second):
    count_dp = lax.axis_size('dp')
    count_tensor = lax.axis_size('tensor')
    group = lax.axis_index('dp')
    place = lax.axis_index('tensor')
    own_rows, width = tokens.shape
    token_rows = own_rows * count_tensor
    seq_count = token_rows // LEN
    seq_total = order.shape[0]
    head_count = head_params.shape[0]
    padded_heads = -(-head_count // 8) * 8
    inner_cols = head_count * HEAD_DIM
    conv_rows = conv_weight.shape[0]
    state_cols = conv_rows - inner_cols
    inner_total = inner_cols * count_tensor
    norm_gain = gain_vector[:width]
    gate_gain = lax.dynamic_slice_in_dim(gain_vector, width + place * inner_cols, inner_cols, 0)
    gate_gain = gate_gain.reshape(1, inner_cols)
    positions = jnp.arange(seq_total)
    inverse = jnp.sum(jnp.where(order[:, None] == positions[None, :], positions[:, None], 0), axis=0)
    own_seq = place * own_rows // LEN
    sources = inverse[jnp.arange(count_dp) * seq_count + own_seq] // seq_count
    seq_lengths = lax.dynamic_slice_in_dim(lengths, group * seq_count, seq_count, 0)
    live_all = (jnp.arange(LEN)[None, :] < seq_lengths[:, None]).astype(F32).reshape(token_rows, 1)
    live_own = lax.dynamic_slice_in_dim(live_all, place * own_rows, own_rows, 0)
    own = tokens.astype(F32)
    inv_own = lax.rsqrt(jnp.mean(own * own, axis=1, keepdims=True) + EPS_NORM)
    normed_own = (own * inv_own * norm_gain).astype(BF16)
    side_cols = 128
    far = count_dp // 2
    in_low = in_weight.astype(BF16)
    side_real = in_low.shape[1] - 2 * inner_cols
    mixed_shard = jnp.pad(in_low[:, inner_cols:], ((0, 0), (0, side_cols - side_real)))
    normed_blocks = gather_tensor_blocks(normed_own)
    first_bit = count_tensor // 2
    chan = jnp.concatenate([conv_weight[:inner_cols].T, jnp.repeat(head_params[:, 2], HEAD_DIM)[None, :], jnp.zeros((2, inner_cols), F32)], axis=0)
    rate = -jnp.exp(head_params[:, 1])
    heads = jnp.pad(jnp.stack([head_params[:, 0], rate], axis=1), ((0, padded_heads - head_count), (0, 126)))
    state_taps = jnp.pad(conv_weight[inner_cols:], ((0, 0), (0, 3)))
    prepared = (chan, heads, state_taps, gate_gain, live_own)
    late_shard = jnp.concatenate([in_low[:, :inner_cols], out_weight.astype(BF16).T], axis=1)
    mixed_ring = Gather(mixed_shard, True)
    late_ring = Gather(late_shard, False)
    mixed_ring.step()
    cot_first = deal_out(after(cotangent, *mixed_ring.arrived()))
    for k in range(far - 2):
        mixed_ring.step()
        if k == 0:
            late_ring.step(*mixed_ring.arrived())
    cot_chosen = cot_first.at[sources].get(mode='promise_in_bounds')
    mixed_ring.step(normed_blocks[first_bit], *prepared)
    mixed_ring.wait(cot_chosen)
    in_inner, in_side = mixed_ring.place([inner_cols, side_cols])
    normed_blocks[0] = after(normed_blocks[0], cot_chosen)
    normed = join_tensor(normed_blocks, 30)
    cot_own = deal_in(cot_chosen)
    cot_own = after(cot_own, normed)
    back_out_own = (cot_own.astype(F32) * live_own).astype(BF16)
    back_out_blocks = gather_tensor_blocks(back_out_own)
    side_pre = dot_general_tt(in_side, after(normed, *late_ring.arrived()))
    late_ring.step()
    state_pre = by_sequence(side_pre[:state_cols], seq_count)
    step_pre = by_sequence(side_pre[state_cols:state_cols + padded_heads], seq_count)
    state_own = state_forward(state_pre, state_taps, seq_count)
    states = join_tensor(gather_tensor_blocks(from_sequence(state_own, seq_count)))
    states = by_sequence(states, seq_count)
    inner_pre = dot_nn(after(normed, side_pre, *late_ring.arrived()), in_inner).astype(BF16)
    for _ in range(far - 3):
        late_ring.step()
    late_ring.wait(back_out_own)
    inner_pre = after(inner_pre, *late_ring.arrived())
    late_ring.step()
    scanned, conv, entry = scan_forward(inner_pre, states, step_pre, chan, heads, head_count)
    late_ring.wait(scanned)
    in_gate, out_low = late_ring.place([inner_cols, inner_cols])
    back_out = join_tensor(back_out_blocks)
    gate_pre = lax.optimization_barrier(dot_nn(normed, in_gate).astype(BF16)).astype(F32)
    scanned = scanned.astype(F32)
    gate_sigmoid = jax.nn.sigmoid(gate_pre)
    gate = gate_pre * gate_sigmoid
    mixed = scanned * gate
    back_normed = lax.optimization_barrier(dot_nn(back_out, out_low).astype(BF16)).astype(F32)
    row_sums = jnp.stack([jnp.sum(mixed * mixed, axis=1), jnp.sum(back_normed * gate_gain * mixed, axis=1)])
    unscaled_out = (mixed * gate_gain).astype(BF16)
    row_sums, *others = sum_parts(row_sums, 'tensor')
    partial_out = lax.optimization_barrier(dot_nt(after(unscaled_out, row_sums), out_low).astype(BF16))
    branch = Halving(partial_out)
    row_sums = sum(after_all(others, branch.given), row_sums)
    gate_inv = lax.rsqrt(row_sums[0] / inner_total + EPS_NORM)[:, None]
    gate_rows = row_sums[1][:, None]
    scaled = mixed * gate_inv
    normed_out = lax.optimization_barrier((scaled * gate_gain).astype(BF16))
    grad_gate_gain = jnp.sum(back_normed * scaled, axis=0)
    back_mixed = gate_inv * (back_normed * gate_gain) - mixed * (gate_inv ** 3 * (gate_rows / inner_total))
    back_gate = (back_mixed * scanned * (gate_sigmoid * (1.0 + gate_pre * (1.0 - gate_sigmoid)))).astype(BF16)
    grad_gate_full, grad_out_full = lax.optimization_barrier((dot_tn(normed, back_gate).astype(BF16), dot_tn(back_out, normed_out).astype(BF16)))
    early = Scatter((grad_gate_full, grad_out_full), False)
    dy = (back_mixed * gate).astype(BF16)
    held = ()
    back_parts = 2 if head_count % 4 == 0 else 1
    for part in range(back_parts):
        dy = after(dy, *early.going(), *held)
        held = scan_backward(dy, inner_pre, conv, states, step_pre, entry, chan, heads, head_count, part, back_parts, held)
        early.move()
        count = len(held)
        together = lax.optimization_barrier((*held, *early.going()))
        early.arrive(together[count:])
        held = together[:count]
        early.add()
    back_inner, back_states, back_step, dchan, dhead = held
    tok = ()
    tok = (fence(*early.going()),)
    going = early.going()
    early.move()
    if tok:
        early.wait(*tok)
    inner = Scatter([lax.optimization_barrier(dot_tn(normed, after(back_inner, *(tok or going))).astype(BF16))], True)
    tok = (fence(*inner.going()),)
    inner.move()
    inner.wait(*tok)
    state_kept, state_given = scatter_tensor_split(from_sequence(after(back_states, *tok), seq_count).reshape(count_tensor, state_cols, token_rows), 1)
    state_back = state_kept.astype(F32) + scatter_tensor_move(state_given, 1).astype(F32)
    step = 2
    while step < count_tensor:
        state_back = scatter_tensor_step(state_back, step)
        step *= 2
    state_back = state_back[0]
    tie = (state_given,)
    back_main = lax.optimization_barrier(dot_nt(after(back_gate, *tie), in_gate) + dot_nt(after(back_inner, *tie), in_inner))
    third = early.going()
    inner.wait(back_main, *third)
    inner.add()
    early.add()
    early.move()
    inner.move()
    back_state_pre, dtaps_state = state_backward(by_sequence(state_back, seq_count), state_pre, state_taps, seq_count)
    back_step = from_sequence(back_step, seq_count)[:head_count].astype(BF16)
    back_side = jnp.concatenate([from_sequence(back_state_pre, seq_count), back_step, jnp.zeros((side_cols - side_real, token_rows), BF16)], axis=0)
    back_main = after(back_main, *third)
    back_input = (back_main + dot_general_tt(back_side, in_side)).astype(BF16)
    back_sum = Halving(back_input)
    back_sum.move()
    grad_side = dot_general_tt(normed, after(back_side, back_sum.given)).astype(BF16)
    grad_side = grad_side.reshape(count_dp, -1, side_cols)

    def a2a(g):
        return lax.all_to_all(g, 'dp', split_axis=0, concat_axis=0, tiled=True)
    grad_side = a2a(grad_side)
    back_sum.wait(branch.given)
    back_sum.add()
    inner.wait(back_sum.given)
    inner.add()
    back_part = back_sum.finish()
    branch.move()
    branch.wait(*inner.going())
    branch.add()
    gate_own = lax.dynamic_slice_in_dim(gate_inv, place * own_rows, own_rows, 0)
    layer_output = (live_own * (own + gate_own * branch.finish())).astype(BF16)
    inner_last = inner.going()
    while inner.distance > 1:
        while early.distance > inner.distance - 1:
            early.add()
            early.move()
        inner.move()
        inner.wait(branch.given)
        inner.add()
    inner.move()
    early.wait(*inner_last)
    while early.distance > 0:
        early.add()
        early.move()
    grad_early = early.end()
    inner.wait(grad_early)
    grad_side = jnp.sum(grad_side.astype(F32), axis=0)
    grad_inner = inner.end()
    row_term = jnp.sum(back_part * norm_gain * own, axis=1, keepdims=True)
    back_own = inv_own * norm_gain * back_part - own * inv_own ** 3 * (row_term / width)
    input_grad = (live_own * cot_own.astype(F32) + back_own).astype(BF16)
    grad_norm_gain = jnp.sum(back_part * own * inv_own, axis=0)
    squares = jnp.stack([jnp.sum(grad_early * grad_early), jnp.sum(grad_inner * grad_inner), jnp.sum(grad_side * grad_side)])
    gain_rows = width // inner_cols
    shared = pack(dchan, grad_gate_gain[None, :], grad_norm_gain.reshape(gain_rows, inner_cols), dtaps_state, dhead, squares)
    shared = sum_parts(shared, 'dp')
    shared, skip, across = small_sums(shared, gain_rows, count_tensor)
    first = 7 + gain_rows
    grad_conv = jnp.concatenate([shared[:5], shared[first:first + 5, :state_cols]], axis=1)
    head_rows = shared[first + 5:first + 7, :head_count]
    grad_head = jnp.concatenate([head_rows, skip[:1, :head_count]], axis=0)
    across = after(across, layer_output)
    last = gain_rows + count_tensor
    across, norms, *updated = adam_matrices(sum_parts(across, 'tensor'), grad_early, grad_inner, grad_side, (in_weight, in_first, in_second), (out_weight.T, out_first.T, out_second.T), (grad_conv, conv_weight.T, conv_first.T, conv_second.T), (grad_head, head_params.T, head_first.T, head_second.T), gain_rows, last)
    grad_norm, factor = (norms[0, 0], norms[1, 0])
    grad_gains = across[:last].reshape(-1)
    new_in, in_copy = (updated[:3], updated[3])
    new_out, out_copy = ([values.T for values in updated[4:7]], updated[7].T)
    new_conv = [values.T for values in updated[8:11]]
    new_head = [values.T for values in updated[11:]]
    new_gain = adam_step(gain_vector, gain_first, gain_second, factor * grad_gains, RATE_VECTOR, 0.0)
    return (layer_output, input_grad, grad_norm, *new_in, *new_out, *new_conv, *new_gain, *new_head, in_copy, out_copy)


def solution(mesh):
    rows = P(('dp', 'tensor'), None)
    in_matrix = P('dp', 'tensor')
    out_matrix = P('tensor', 'dp')
    by_tensor = P('tensor', None)
    same = P()
    in_specs = (rows, rows, same, same) + (in_matrix,) * 3 + (out_matrix,) * 3 + (by_tensor,) * 3 + (same,) * 3 + (by_tensor,) * 3
    out_specs = (rows, rows, same) + (in_matrix,) * 3 + (out_matrix,) * 3 + (by_tensor,) * 3 + (same,) * 3 + (by_tensor,) * 3 + (in_matrix, out_matrix)
    return jax.shard_map(shards, mesh=mesh, in_specs=in_specs, out_specs=out_specs, check_vma=False)
```
